32 devices in a mesh: batch: 8 (over z, x), heads: 4 (over y, core).
Axes of the slice: x: 2, y: 2, z: 4, core: 2. Of those that a mesh axis runs over, the one named last changes fastest.
Arguments:
- tokens: bfloat16 [16384, 768], P('batch'), may hold values from -6 to 6
- w_query: bfloat16 [768, 768], P(None, 'heads'), may hold values from -0.21875 to 0.21875
- w_key: bfloat16 [768, 768], P(None, 'heads'), may hold values from -0.21875 to 0.21875
- w_value: bfloat16 [768, 768], P(None, 'heads'), may hold values from -0.375 to 0.375
- w_output: bfloat16 [768, 768], P('heads'), may hold values from -0.375 to 0.375
- gain_attn: bfloat16 [768], replicated, may hold values from 0.099609375 to 1.8984375
- gain_inner: bfloat16 [768], P('heads'), may hold values from 0.099609375 to 1.8984375
- gain_ffn: bfloat16 [768], replicated, may hold values from 0.099609375 to 1.8984375
- w_expand: bfloat16 [3072, 768], P(('batch', 'heads')), may hold values from -0.375 to 0.375
- w_reduce: bfloat16 [3072, 768], P(('batch', 'heads')), may hold values from -0.1875 to 0.1875
- gain_hidden: bfloat16 [3072], P(('batch', 'heads')), may hold values from 0.099609375 to 1.8984375
- cotangent: bfloat16 [16384, 768], P(('batch', 'heads')), may hold values from -6 to 6
- seq_length: int32 [29], replicated, may hold values from 512 to 2048, as said below
- seq_group: int32 [29], replicated, may hold values from 0 to 7, as said below
Outputs:
- output: bfloat16 [16384, 768], P(('batch', 'heads'))
- grad_tokens: bfloat16 [16384, 768], P(('batch', 'heads'))
- grad_query: float32 [768, 768], P(None, 'heads')
- grad_key: float32 [768, 768], P(None, 'heads')
- grad_value: float32 [768, 768], P(None, 'heads')
- grad_output: float32 [768, 768], P('heads')
- grad_attn: float32 [768], replicated
- grad_inner: float32 [768], P('heads')
- grad_ffn: float32 [768], replicated
- grad_expand: float32 [3072, 768], P(('batch', 'heads'))
- grad_reduce: float32 [3072, 768], P(('batch', 'heads'))
- grad_hidden: float32 [3072], P(('batch', 'heads'))
The draws below stay inside these ranges and needn't reach their ends.
Inputs may be any that keep to these rules, and one draw needn't show every extreme that they name: `seq_length`: each sequence has 512 or 2048 tokens; exactly 1 have 2048. `seq_group`: the sequences of each group have 2048 tokens together; 1 group hold one sequence of 2048 each.
All inputs are finite; a program needn't handle non-finite values.
Results may differ from the reference program's by a relative error of at most 0.018.
Values may be sent and summed in bfloat16 or wider, within the bound.
No kernel may reach another device: no remote copies, remote signals or barrier semaphores. Data moves between devices by JAX's collectives and lax.ppermute only.
A program may use at most 256 MiB of HBM per device.

```python
import jax
import jax.numpy as jnp
from jax import lax

D = 768
HEADS = 12
HD = 64
FF = 3072
SHORT = 512
UNITS = 4
LONG = 2048
CAP = 2048
GROUPS = 8
NLONG = 1
NSEQ = 29
TOKENS = 16384


def sequence_table(key):
    group_order = jax.random.permutation(jax.random.fold_in(key, 11), GROUPS)
    long_mark = jnp.zeros((GROUPS,), jnp.int32).at[group_order[:NLONG]].set(1)
    unit_index = jnp.arange(GROUPS * UNITS, dtype=jnp.int32)
    unit_group = unit_index // UNITS
    unit_place = unit_index % UNITS
    is_taken = (unit_place < 4 * long_mark[unit_group]).astype(jnp.int32)
    short_units = jnp.argsort(is_taken, stable=True)[:GROUPS * UNITS - 4 * NLONG]
    canon_group = jnp.concatenate([group_order[:NLONG].astype(jnp.int32), unit_group[short_units]])
    canon_length = jnp.concatenate([jnp.full((NLONG,), LONG, jnp.int32), jnp.full((GROUPS * UNITS - 4 * NLONG,), SHORT, jnp.int32)])
    shuffle = jax.random.permutation(jax.random.fold_in(key, 13), NSEQ)
    return (canon_length[shuffle], canon_group[shuffle])


def draw_seq_length(key, part):
    return sequence_table(key)[0]


def draw_seq_group(key, part):
    return sequence_table(key)[1]


def level_of(key, shape, split, least, high):
    def one(dim, parts):
        heights = jax.random.uniform(jax.random.fold_in(jax.random.fold_in(key, 6), dim), (parts,), jnp.float32, least / len(split), high / len(split))
        return jnp.repeat(jnp.exp(heights), shape[dim] // parts).reshape((-1,) + (1,) * (len(shape) - dim - 1))

    factor_of = one(*split[0])
    for cut in split[1:]:
        factor_of = factor_of * one(*cut)
    return factor_of


def normal_values(stream_key, dims, deviation, most, cuts=(), kind=jnp.bfloat16):
    factor_of = level_of(stream_key, dims, cuts, -0.22, 0.18) if cuts else 1.0
    drawn = jax.random.normal(stream_key, dims, jnp.float32) * deviation * factor_of
    return jnp.minimum(jnp.maximum(drawn, -most), most).astype(kind)


def setup_inputs(seed: int = 0) -> dict:
    key_of = jax.random.split(jax.random.key(seed), 15)
    tokens = normal_values(key_of[0], (TOKENS, D), 1.0, 6.0, ((0, 8),))
    w_query = normal_values(key_of[1], (D, D), D ** -0.5, 0.21875, ((1, 4),))
    w_key = normal_values(key_of[2], (D, D), D ** -0.5, 0.21875, ((1, 4),))
    w_value = normal_values(key_of[3], (D, D), (D * 10 // 32) ** -0.5, 0.375, ((1, 4),))
    w_output = normal_values(key_of[4], (D, D), (D * 10 // 32) ** -0.5, 0.375, ((0, 4),))
    gain_attn = jnp.clip(1.0 + 0.18 * jax.random.normal(key_of[5], (D,), jnp.float32), 0.099609375, 1.8984375).astype(jnp.bfloat16)
    gain_inner = jnp.clip(1.0 + 0.18 * jax.random.normal(key_of[6], (D,), jnp.float32), 0.099609375, 1.8984375).astype(jnp.bfloat16)
    gain_ffn = jnp.clip(1.0 + 0.18 * jax.random.normal(key_of[7], (D,), jnp.float32), 0.099609375, 1.8984375).astype(jnp.bfloat16)
    w_expand = normal_values(key_of[8], (FF, D), (D * 10 // 32) ** -0.5, 0.375, ((0, 32),))
    w_reduce = normal_values(key_of[9], (FF, D), (FF * 10 // 32) ** -0.5, 0.1875, ((0, 32),))
    gain_hidden = jnp.clip(1.0 + 0.18 * jax.random.normal(key_of[10], (FF,), jnp.float32), 0.099609375, 1.8984375).astype(jnp.bfloat16)
    cotangent = normal_values(key_of[11], (TOKENS, D), 1.0, 6.0, ((0, 32),))
    seq_length = draw_seq_length(jax.random.fold_in(key_of[14], 71), 0)
    seq_group = draw_seq_group(jax.random.fold_in(key_of[14], 71), 0)
    return {"tokens": tokens, "w_query": w_query, "w_key": w_key, "w_value": w_value, "w_output": w_output, "gain_attn": gain_attn, "gain_inner": gain_inner, "gain_ffn": gain_ffn, "w_expand": w_expand, "w_reduce": w_reduce, "gain_hidden": gain_hidden, "cotangent": cotangent, "seq_length": seq_length, "seq_group": seq_group}


@jax.custom_vjp
def low(v):
    return lax.optimization_barrier(v.astype(jnp.bfloat16)).astype(jnp.float32)

@jax.custom_vjp
def low_back(v):
    return v

def low_keep(v):
    return (low(v), None)

def low_pass(kept, grad):
    return (grad,)

def back_keep(v):
    return (v, None)

def back_low(kept, grad):
    return (low(grad),)
low.defvjp(low_keep, low_pass)
low_back.defvjp(back_keep, back_low)
EPSILON = 1e-05
HIGH = lax.Precision.HIGHEST

def normalize(values):
    average = lax.optimization_barrier(jnp.mean(values, axis=-1, keepdims=True))
    spread = lax.optimization_barrier(jnp.mean((values - average) ** 2, axis=-1, keepdims=True))
    return (values - average) * lax.rsqrt(spread + EPSILON)

def matmul(left, right):
    return jnp.dot(left, right, precision=HIGH, preferred_element_type=jnp.float32)

def segments(seq_length, seq_group):
    places = jnp.arange(CAP, dtype=jnp.int32)

    def one_group(group_id):
        mine_lengths = jnp.where(seq_group == group_id, seq_length, 0)
        finish = jnp.cumsum(mine_lengths).astype(jnp.int32)
        return lax.optimization_barrier(jnp.sum((finish[None, :] <= places[:, None]).astype(jnp.int32), axis=1)).astype(jnp.int32)
    return jax.vmap(one_group)(jnp.arange(GROUPS, dtype=jnp.int32))

def block_forward(params, group_rows, segment):
    w_query, w_key, w_value, w_output, gain_attn, gain_inner, gain_ffn, w_expand, w_reduce, gain_hidden = params
    pre = low(normalize(group_rows) * gain_attn)
    queries = low_back(low(matmul(pre, w_query))).reshape(CAP, HEADS, HD)
    keys_all = low_back(low(matmul(pre, w_key))).reshape(CAP, HEADS, HD)
    values_all = low_back(low(matmul(pre, w_value))).reshape(CAP, HEADS, HD)
    scores = low_back(jnp.einsum('qhd,khd->hqk', queries, keys_all, precision=HIGH) * HD ** (-0.5))
    places = jnp.arange(CAP, dtype=jnp.int32)
    allowed = (segment[:, None] == segment[None, :]) & (places[None, :] <= places[:, None])
    scores = jnp.where(allowed[None], scores, -1e+30)
    largest = lax.optimization_barrier(jnp.max(scores, axis=-1, keepdims=True))
    shifted_exp = jnp.exp(scores - largest)
    probs = low(shifted_exp / lax.optimization_barrier(jnp.sum(shifted_exp, axis=-1, keepdims=True)))
    attended = jnp.einsum('hqk,khd->qhd', probs, values_all, precision=HIGH).reshape(CAP, D)
    attended = low_back(attended)
    inner = low(normalize(attended) * gain_inner)
    middle = group_rows + low_back(matmul(inner, w_output))
    mid_low = low(normalize(middle) * gain_ffn)
    hidden = low_back(jnp.dot(mid_low, w_expand.T, precision=HIGH, preferred_element_type=jnp.float32))
    post = low(normalize(jax.nn.gelu(hidden, approximate=False)) * gain_hidden)
    return middle + matmul(post, w_reduce)

def reference(tokens, w_query, w_key, w_value, w_output, gain_attn, gain_inner, gain_ffn, w_expand, w_reduce, gain_hidden, cotangent, seq_length, seq_group):
    segment = segments(seq_length, seq_group)
    params = tuple((weight.astype(jnp.float32) for weight in (w_query, w_key, w_value, w_output, gain_attn, gain_inner, gain_ffn, w_expand, w_reduce, gain_hidden)))

    def forward(all_rows, weights):

        def visit(carried, group_pair):
            return (carried, jax.checkpoint(block_forward)(weights, group_pair[0], group_pair[1]))
        unused, mixed = lax.scan(visit, jnp.zeros((), jnp.float32), (all_rows.reshape(GROUPS, CAP, D), segment))
        return mixed.reshape(GROUPS * CAP, D)
    result, pullback = jax.vjp(forward, tokens.astype(jnp.float32), params)
    grad_rows, grads = pullback(cotangent.astype(jnp.float32))
    return (result.astype(jnp.bfloat16), grad_rows.astype(jnp.bfloat16), grads[0], grads[1], grads[2], grads[3], grads[4], grads[5], grads[6], grads[7], grads[8], grads[9])
```

```python
from functools import partial

import jax
import jax.numpy as jnp
from jax import lax
from jax.experimental import pallas as pl
from jax.experimental.pallas import tpu as pltpu
from jax.sharding import PartitionSpec as P

HD = 64
SHORT = 512
EPSILON = 1e-05
MASKED = -1e30
AXES = ("batch", "heads")
BF = jnp.bfloat16
F32 = jnp.float32
VMEM_LIMIT = 60 * 1024 * 1024


def dot(left, right, left_dim, right_dim):
    return lax.dot_general(
        left, right, (((left_dim,), (right_dim,)), ((), ())), preferred_element_type=F32
    )


def params(limit=VMEM_LIMIT):
    return pltpu.CompilerParams(vmem_limit_bytes=limit)


def vmem():
    return pl.BlockSpec(memory_space=pltpu.VMEM)


def smem():
    return pl.BlockSpec(memory_space=pltpu.SMEM)


def cost(flops, moved, special=0):
    return pl.CostEstimate(flops=flops, bytes_accessed=moved, transcendentals=special)


def attention_forward_kernel(
    flags, tokens, w_query, w_key, w_value, gain, pre, qkv, lse, *rest, n_own
):
    pieces, (w_t, s_buf, att_buf, acc) = rest[:n_own], rest[n_own:]
    rows, width = tokens.shape
    local = w_query.shape[1]
    heads = local // HD
    blocks = rows // SHORT
    tile = 64
    is_long, mine = flags[0], flags[1]
    gain_row = gain[...].astype(F32)

    for place, weight in enumerate((w_query, w_key, w_value)):
        w_t[place * local : (place + 1) * local, :] = weight[...].astype(F32).T.astype(BF)

    def norm_rows(step, unused):
        at = pl.ds(step * tile, tile)
        x = tokens[at, :].astype(F32)
        centred = x - jnp.mean(x, axis=1, keepdims=True)
        factor = lax.rsqrt(jnp.mean(centred * centred, axis=1, keepdims=True) + EPSILON)
        pre[at, :] = (centred * factor * gain_row).astype(BF)
        return unused

    lax.fori_loop(0, rows // tile, norm_rows, 0)

    for block in range(blocks):
        cols = slice(block * SHORT, (block + 1) * SHORT)
        product = dot(w_t[...], pre[cols, :], 1, 1)
        qkv[0:local, cols] = (product[0:local] * HD ** (-0.5)).astype(BF)
        qkv[local:, cols] = product[local:].astype(BF)

    def column_max(values):
        return jnp.max(values.reshape(values.shape[0] // 8, 8, SHORT), axis=0)

    def column_sum(values):
        return jnp.sum(values.reshape(values.shape[0] // 8, 8, SHORT), axis=0)

    key_place = lax.broadcasted_iota(jnp.int32, (SHORT, SHORT), 0)
    query_place = lax.broadcasted_iota(jnp.int32, (SHORT, SHORT), 1)

    def one_block(step, unused):
        head, block = step // blocks, step % blocks
        low = jnp.where(is_long > 0, 0, block)
        q_rows = pl.ds(pl.multiple_of(head * HD, HD), HD)
        k_rows = pl.ds(pl.multiple_of(local + head * HD, HD), HD)
        v_rows = pl.ds(pl.multiple_of(2 * local + head * HD, HD), HD)
        q_cols = pl.ds(pl.multiple_of(block * SHORT, SHORT), SHORT)
        q_t = qkv[q_rows, q_cols]

        def scores(index):
            cols = pl.ds(pl.multiple_of(index * SHORT, SHORT), SHORT)
            return dot(qkv[k_rows, cols], q_t, 0, 0)

        def visit(index, largest):
            s = scores(index)
            s_buf[pl.ds(pl.multiple_of(index * SHORT, SHORT), SHORT), :] = s
            return jnp.maximum(largest, column_max(s))

        largest = lax.fori_loop(low, block, visit, jnp.full((8, SHORT), MASKED, F32))
        s = jnp.where(key_place <= query_place, scores(block), MASKED)
        s_buf[pl.ds(pl.multiple_of(block * SHORT, SHORT), SHORT), :] = s
        largest = jnp.maximum(largest, column_max(s))
        top = jnp.max(largest, axis=0, keepdims=True)
        acc[...] = jnp.zeros_like(acc)

        def gather(index, total):
            cols = pl.ds(pl.multiple_of(index * SHORT, SHORT), SHORT)
            p = jnp.exp(s_buf[cols, :] - top)
            acc[...] += dot(qkv[v_rows, cols], p.astype(BF), 1, 0)
            return total + column_sum(p)

        total = lax.fori_loop(low, block + 1, gather, jnp.zeros((8, SHORT), F32))
        total = jnp.sum(total, axis=0, keepdims=True)
        att_buf[block, q_rows, :] = (acc[...] / total).astype(BF)
        lse[head, block] = jnp.broadcast_to(top + jnp.log(total), (8, SHORT))
        return unused

    lax.fori_loop(0, heads * blocks, one_block, 0)
    for place in range(n_own):
        pieces[place][...] = att_buf[mine ^ place]


def attention_forward(flags, tokens, w_query, w_key, w_value, gain, n_own):
    rows, width = tokens.shape
    local = w_query.shape[1]
    blocks = rows // SHORT
    heads = local // HD
    return pl.pallas_call(
        partial(attention_forward_kernel, n_own=n_own),
        out_shape=(
            jax.ShapeDtypeStruct((rows, width), BF),
            jax.ShapeDtypeStruct((3 * local, rows), BF),
            jax.ShapeDtypeStruct((heads, blocks, 8, SHORT), F32),
        )
        + (jax.ShapeDtypeStruct((local, SHORT), BF),) * n_own,
        in_specs=[smem()] + [vmem()] * 5,
        out_specs=[vmem()] * (3 + n_own),
        scratch_shapes=[
            pltpu.VMEM((3 * local, width), BF),
            pltpu.VMEM((rows, SHORT), F32),
            pltpu.VMEM((blocks, local, SHORT), BF),
            pltpu.VMEM((HD, SHORT), F32),
        ],
        compiler_params=params(),
        cost_estimate=cost(12_000_000_000, 10_000_000, 6_000_000),
        name="attention_forward",
    )(flags, tokens, w_query, w_key, w_value, gain)


def attention_backward_kernel(
    flags, qkv, lse, pre, w_query, w_key, w_value, *rest, n_own
):
    att, grads = rest[:n_own], rest[n_own : 2 * n_own]
    d_weight, attn_sum, sent, kept, ag, delta, d_qkv, dq, dk, dv = rest[2 * n_own :]
    rows, width = pre.shape
    local = w_query.shape[1]
    heads = local // HD
    blocks = rows // SHORT
    is_long, mine = flags[0], flags[1]

    for place in range(n_own):
        grad = grads[place][...]
        ag[mine ^ place] = grad
        product = grad.astype(F32) * att[place][...].astype(F32)
        for head in range(heads):
            summed = jnp.sum(product[head * HD : (head + 1) * HD], axis=0, keepdims=True)
            delta[head, mine ^ place] = jnp.broadcast_to(summed, (8, SHORT))

    key_place = lax.broadcasted_iota(jnp.int32, (SHORT, SHORT), 0)
    query_place = lax.broadcasted_iota(jnp.int32, (SHORT, SHORT), 1)

    def one_head(head, unused):
        q_rows = pl.ds(pl.multiple_of(head * HD, HD), HD)
        k_rows = pl.ds(pl.multiple_of(local + head * HD, HD), HD)
        v_rows = pl.ds(pl.multiple_of(2 * local + head * HD, HD), HD)
        dq[...] = jnp.zeros_like(dq)

        def one_key(block, unused):
            k_cols = pl.ds(pl.multiple_of(block * SHORT, SHORT), SHORT)
            k_t = qkv[k_rows, k_cols]
            v_t = qkv[v_rows, k_cols]

            def pair(index, masked):
                q_cols = pl.ds(pl.multiple_of(index * SHORT, SHORT), SHORT)
                q_t = qkv[q_rows, q_cols]
                grad = ag[index, q_rows, :]
                s = dot(k_t, q_t, 0, 0)
                p = jnp.exp(s - lse[head, index][0:1])
                if masked:
                    p = jnp.where(key_place <= query_place, p, 0.0)
                d_p = dot(v_t, grad, 0, 0)
                d_s = (p * (d_p - delta[head, index][0:1])).astype(BF)
                p = p.astype(BF)
                return (
                    dot(k_t, d_s, 1, 0),
                    dot(q_t, d_s, 1, 1),
                    dot(grad, p, 1, 1),
                )

            add_q, add_k, add_v = pair(block, True)
            dq[block] += add_q
            dk[...] = add_k
            dv[...] = add_v

            def visit(index, unused):
                add_q, add_k, add_v = pair(index, False)
                dq[index] += add_q
                dk[...] += add_k
                dv[...] += add_v
                return unused

            high = jnp.where(is_long > 0, blocks, block + 1)
            lax.fori_loop(block + 1, high, visit, 0)
            d_qkv[k_rows, k_cols] = dk[...].astype(BF)
            d_qkv[v_rows, k_cols] = dv[...].astype(BF)
            return unused

        lax.fori_loop(0, blocks, one_key, 0)
        for block in range(blocks):
            d_qkv[q_rows, block * SHORT : (block + 1) * SHORT] = (
                dq[block] * HD ** (-0.5)
            ).astype(BF)
        return unused

    lax.fori_loop(0, heads, one_head, 0)

    total = jnp.zeros((8, width), F32)
    for place, weight in enumerate((w_query, w_key, w_value)):
        at = slice(place * local, (place + 1) * local)
        product = dot(d_qkv[at, :], pre[...], 1, 0)
        d_weight[at, :] = product.astype(BF)
        cross = product * weight[...].astype(F32).T
        total = total + jnp.sum(cross.reshape(local // 8, 8, width), axis=0)
    attn_sum[...] = jnp.broadcast_to(jnp.sum(total, axis=0, keepdims=True), (8, width))

    half = n_own // 2
    for place in range(n_own):
        cols = pl.ds(pl.multiple_of((mine ^ place) * SHORT, SHORT), SHORT)
        grad = dot(w_query[...], d_qkv[0:local, cols], 1, 0)
        grad += dot(w_key[...], d_qkv[local : 2 * local, cols], 1, 0)
        grad += dot(w_value[...], d_qkv[2 * local :, cols], 1, 0)
        target = sent if place % 2 else kept
        target[place // 2] = grad.astype(BF)


def attention_backward(flags, qkv, lse, pre, w_query, w_key, w_value, att, grads):
    rows, width = pre.shape
    local = w_query.shape[1]
    blocks = rows // SHORT
    heads = local // HD
    n_own = len(att)
    half = max(n_own // 2, 1)
    return pl.pallas_call(
        partial(attention_backward_kernel, n_own=n_own),
        out_shape=(
            jax.ShapeDtypeStruct((3 * local, width), BF),
            jax.ShapeDtypeStruct((8, width), F32),
            jax.ShapeDtypeStruct((half, width, SHORT), BF),
            jax.ShapeDtypeStruct((half, width, SHORT), BF),
        ),
        in_specs=[smem()] + [vmem()] * (6 + 2 * n_own),
        out_specs=[vmem()] * 4,
        scratch_shapes=[
            pltpu.VMEM((blocks, local, SHORT), BF),
            pltpu.VMEM((heads, blocks, 8, SHORT), F32),
            pltpu.VMEM((3 * local, rows), BF),
            pltpu.VMEM((blocks, HD, SHORT), F32),
            pltpu.VMEM((HD, SHORT), F32),
            pltpu.VMEM((HD, SHORT), F32),
        ],
        compiler_params=params(),
        cost_estimate=cost(30_000_000_000, 16_000_000, 6_000_000),
        name="attention_backward",
    )(flags, qkv, lse, pre, w_query, w_key, w_value, *att, *grads)


def gelu_parts(h):
    phi = jnp.exp(h * h * (-0.5)) * 0.3989422804014327
    big = 0.5 * lax.erf(h * 0.7071067811865476) + 0.5
    return h * big, big + h * phi


def feed_forward_kernel(*refs, n_own):
    att, w_out, rest = refs[:n_own], refs[n_own : 2 * n_own], refs[2 * n_own :]
    (
        tokens,
        cotangent,
        gain_ffn,
        expand_a,
        expand_b,
        reduce_a,
        reduce_b,
        output,
        middle_grad,
        post,
        hidden_grad,
        mid_low,
        inner_t,
        branch_grad,
        ffn_sum,
    ) = rest[:15]
    grads = rest[15 : 15 + n_own]
    middle, act, slope, d_post, mid_acc = rest[15 + n_own :]
    rows, width = tokens.shape
    local = att[0].shape[0]
    chunk = SHORT
    tile = 16
    half = expand_a.shape[0]
    steps = half // chunk
    gain_row = gain_ffn[...].astype(F32)

    total = jnp.zeros((1, rows), F32)
    for piece in att:
        total = total + jnp.sum(piece[...].astype(F32), axis=0, keepdims=True)
    average = total / width
    square = jnp.zeros((1, rows), F32)
    for piece in att:
        centred = piece[...].astype(F32) - average
        square = square + jnp.sum(centred * centred, axis=0, keepdims=True)
    inner_factor = lax.rsqrt(square / width + EPSILON)
    for place, piece in enumerate(att):
        hat = (piece[...].astype(F32) - average) * inner_factor
        inner_t[place * local : (place + 1) * local, :] = hat.astype(BF)

    branch = dot(inner_t[0:local, :], w_out[0][...], 0, 0)
    for place in range(1, n_own):
        branch += dot(inner_t[place * local : (place + 1) * local, :], w_out[place][...], 0, 0)
    middle[...] = tokens[...].astype(F32) + branch

    def norm_tile(at):
        x = middle[at, :]
        centred = x - jnp.mean(x, axis=1, keepdims=True)
        factor = lax.rsqrt(jnp.mean(centred * centred, axis=1, keepdims=True) + EPSILON)
        return centred * factor, factor

    def norm_rows(step, unused):
        at = pl.ds(pl.multiple_of(step * tile, tile), tile)
        mid_low[at, :] = (norm_tile(at)[0] * gain_row).astype(BF)
        return unused

    lax.fori_loop(0, rows // tile, norm_rows, 0)

    for part, weight in enumerate((expand_a, expand_b)):
        def expand(step, unused, weight=weight, part=part):
            at = pl.ds(pl.multiple_of(step * chunk, chunk), chunk)
            to = pl.ds(pl.multiple_of(part * half + step * chunk, chunk), chunk)
            d_post[:, pl.ds(0, chunk)] = dot(mid_low[...], weight[at, :], 1, 1)

            def apply(row, unused):
                over = pl.ds(pl.multiple_of(row * tile, tile), tile)
                a, s = gelu_parts(d_post[over, pl.ds(0, chunk)])
                act[over, to] = a
                slope[over, to] = s.astype(BF)
                return unused

            lax.fori_loop(0, rows // tile, apply, 0)
            return unused

        lax.fori_loop(0, steps, expand, 0)

    hidden = 2 * half

    def act_tile(at):
        a = act[at, :]
        centred = a - jnp.sum(a, axis=1, keepdims=True) / hidden
        factor = lax.rsqrt(jnp.sum(centred * centred, axis=1, keepdims=True) / hidden + EPSILON)
        return centred * factor, factor

    def post_rows(step, unused):
        at = pl.ds(pl.multiple_of(step * tile, tile), tile)
        n, factor = act_tile(at)
        post[at, :] = n.astype(BF)
        mid_acc[at, 0:128] = jnp.broadcast_to(factor, (tile, 128))
        return unused

    lax.fori_loop(0, rows // tile, post_rows, 0)
    act_factor = mid_acc

    for part, weight in enumerate((reduce_a, reduce_b)):
        def up(step, unused, weight=weight, part=part):
            at = pl.ds(pl.multiple_of(step * chunk, chunk), chunk)
            to = pl.ds(pl.multiple_of(part * half + step * chunk, chunk), chunk)
            d_post[:, to] = dot(cotangent[...], weight[at, :], 1, 1)
            middle_out = dot(post[:, to], weight[at, :], 1, 0)
            act[:, 0:width] += middle_out
            return unused

        if part == 0:
            act[:, 0:width] = middle[...]
        lax.fori_loop(0, steps, up, 0)
    output[...] = act[:, 0:width].astype(BF)

    def back_rows(step, unused):
        at = pl.ds(pl.multiple_of(step * tile, tile), tile)
        e = d_post[at, :]
        n = post[at, :].astype(F32)
        mean_e = jnp.sum(e, axis=1, keepdims=True) / hidden
        mean_en = jnp.sum(e * n, axis=1, keepdims=True) / hidden
        factor = act_factor[at, 0:1]
        grad = factor * (e - mean_e - n * mean_en)
        hidden_grad[at, :] = (grad * slope[at, :].astype(F32)).astype(BF)
        return unused

    lax.fori_loop(0, rows // tile, back_rows, 0)

    mid_acc[...] = jnp.zeros_like(mid_acc)
    for part, weight in enumerate((expand_a, expand_b)):
        def down(step, unused, weight=weight, part=part):
            at = pl.ds(pl.multiple_of(step * chunk, chunk), chunk)
            to = pl.ds(pl.multiple_of(part * half + step * chunk, chunk), chunk)
            mid_acc[...] += dot(hidden_grad[:, to], weight[at, :], 1, 0)
            return unused

        lax.fori_loop(0, steps, down, 0)

    ffn_sum[...] = jnp.zeros_like(ffn_sum)

    def middle_rows(step, unused):
        at = pl.ds(pl.multiple_of(step * tile, tile), tile)
        n, factor = norm_tile(at)
        grad = mid_acc[at, :]
        cross = grad * n
        for part in range(tile // 8):
            ffn_sum[...] += cross[part * 8 : (part + 1) * 8]
        e = grad * gain_row
        back = factor * (
            e
            - jnp.mean(e, axis=1, keepdims=True)
            - n * jnp.mean(e * n, axis=1, keepdims=True)
        )
        full = cotangent[at, :].astype(F32) + back
        middle_grad[at, :] = full
        branch_grad[at, :] = full.astype(BF)
        return unused

    lax.fori_loop(0, rows // tile, middle_rows, 0)

    grad_sum = jnp.zeros((1, rows), F32)
    cross_sum = jnp.zeros((1, rows), F32)
    for place in range(n_own):
        e = dot(w_out[place][...], branch_grad[...], 1, 1)
        act[0:local, place * rows : (place + 1) * rows] = e
        grad_sum = grad_sum + jnp.sum(e, axis=0, keepdims=True)
        hat = (att[place][...].astype(F32) - average) * inner_factor
        cross_sum = cross_sum + jnp.sum(e * hat, axis=0, keepdims=True)
    for place in range(n_own):
        e = act[0:local, place * rows : (place + 1) * rows]
        hat = (att[place][...].astype(F32) - average) * inner_factor
        grad = inner_factor * (e - grad_sum / width - hat * (cross_sum / width))
        grads[place][...] = grad.astype(BF)


def feed_forward(att, w_out, tokens, cotangent, gain_ffn, expand, reduced):
    rows, width = tokens.shape
    hidden = 2 * expand[0].shape[0]
    n_own = len(att)
    local = att[0].shape[0]
    return pl.pallas_call(
        partial(feed_forward_kernel, n_own=n_own),
        out_shape=(
            jax.ShapeDtypeStruct((rows, width), BF),
            jax.ShapeDtypeStruct((rows, width), F32),
            jax.ShapeDtypeStruct((rows, hidden), BF),
            jax.ShapeDtypeStruct((rows, hidden), BF),
            jax.ShapeDtypeStruct((rows, width), BF),
            jax.ShapeDtypeStruct((n_own * local, rows), BF),
            jax.ShapeDtypeStruct((rows, width), BF),
            jax.ShapeDtypeStruct((8, width), F32),
        )
        + (jax.ShapeDtypeStruct((local, rows), BF),) * n_own,
        in_specs=[vmem()] * (2 * n_own + 7),
        out_specs=[vmem()] * (8 + n_own),
        scratch_shapes=[
            pltpu.VMEM((rows, width), F32),
            pltpu.VMEM((rows, hidden), F32),
            pltpu.VMEM((rows, hidden), BF),
            pltpu.VMEM((rows, hidden), F32),
            pltpu.VMEM((rows, width), F32),
        ],
        compiler_params=params(),
        cost_estimate=cost(20_000_000_000, 22_000_000, 4_000_000),
        name="feed_forward",
    )(*att, *w_out, tokens, cotangent, gain_ffn, *expand, *reduced)


def input_gradient_kernel(first, second, third, tokens, gain, middle_grad, out):
    width = first.shape[0]
    total = first[...].astype(F32) + second[...].astype(F32) + third[...].astype(F32)
    x = tokens[...].astype(F32)
    centred = x - jnp.mean(x, axis=1, keepdims=True)
    factor = lax.rsqrt(jnp.mean(centred * centred, axis=1, keepdims=True) + EPSILON)
    n = centred * factor
    e = total.T * gain[...].astype(F32)
    back = factor * (
        e - jnp.mean(e, axis=1, keepdims=True) - n * jnp.mean(e * n, axis=1, keepdims=True)
    )
    out[...] = (middle_grad[...] + back).astype(BF)


def input_gradient(terms, tokens, gain, middle_grad):
    return pl.pallas_call(
        input_gradient_kernel,
        out_shape=jax.ShapeDtypeStruct(tokens.shape, BF),
        in_specs=[vmem()] * 6,
        out_specs=vmem(),
        compiler_params=params(),
        cost_estimate=cost(10_000_000, 6_000_000),
        name="input_gradient",
    )(*terms, tokens, gain, middle_grad)


def body(
    tokens,
    w_query,
    w_key,
    w_value,
    w_output,
    gain_attn,
    gain_inner,
    gain_ffn,
    w_expand,
    w_reduce,
    gain_hidden,
    cotangent,
    seq_length,
    seq_group,
):
    n_batch, n_own = lax.axis_size("batch"), lax.axis_size("heads")
    n_all = n_batch * n_own
    mine = lax.axis_index("heads")
    quarter = cotangent.shape[0]
    width = tokens.shape[1]
    local = w_query.shape[1]

    def swap(value, bit):
        return lax.ppermute(value, AXES, [(i, i ^ bit) for i in range(n_all)])

    is_long = jnp.any((seq_group == lax.axis_index("batch")) & (seq_length > SHORT))
    flags = jnp.stack([is_long.astype(jnp.int32), mine.astype(jnp.int32)])

    def gathered(value, order):
        bits = [1 << b for b in range(n_all.bit_length() - 2, -1, -1)]
        value = value.reshape((1,) * (len(bits) - 1) + value.shape)
        for bit in order:
            value = jnp.concatenate([value, swap(value, bit)], axis=bits.index(bit))
        value = value.reshape(-1, value.shape[-1])
        return value, swap(value, 1)

    def scattered(kept, sent, order):
        bits = [1 << b for b in range(n_all.bit_length() - 2, -1, -1)]
        value = kept.astype(F32) + swap(sent, 1).astype(F32)
        value = value.reshape((2,) * (len(bits) - 1) + (-1, value.shape[-1]))
        for bit in reversed(order):
            axis = bits.index(bit)
            keep, send = (lax.slice_in_dim(value, i, i + 1, axis=axis) for i in (0, 1))
            value = keep + swap(send.astype(BF), bit).astype(F32)
        return value.reshape(-1, value.shape[-1])

    down = [1 << b for b in range(n_all.bit_length() - 2, 0, -1)]
    order_expand = down
    order_reduce = [2] + [b for b in down if b > 4] + [4]
    w_reduce_scaled = (w_reduce.astype(F32) * gain_hidden.astype(F32)[:, None]).astype(BF)
    w_output_scaled = (w_output.astype(F32) * gain_inner.astype(F32)[:, None]).astype(BF)
    expand = gathered(w_expand, order_expand)
    reduced = gathered(w_reduce_scaled, order_reduce)
    w_out = [w_output_scaled] + [swap(w_output_scaled, k) for k in range(1, n_own)]
    gain_attn_row = gain_attn[None, :]
    pre, qkv, lse, *pieces = attention_forward(
        flags, tokens, w_query, w_key, w_value, gain_attn_row, n_own
    )
    att = [pieces[0]] + [swap(pieces[k], k) for k in range(1, n_own)]
    own_tokens = lax.dynamic_slice_in_dim(tokens, mine * quarter, quarter, 0)
    (
        output,
        middle_grad,
        post,
        hidden_grad,
        mid_low,
        inner_t,
        branch_grad,
        ffn_sum,
        *att_grads,
    ) = feed_forward(att, w_out, own_tokens, cotangent, gain_ffn[None, :], expand, reduced)
    grads = [att_grads[0]] + [swap(att_grads[k], k) for k in range(1, n_own)]

    half = post.shape[1] // 2

    def outer(left, right):
        return dot(left, right, 0, 0).astype(BF)

    d_reduce = scattered(
        outer(post[:, :half], cotangent), outer(post[:, half:], cotangent), order_reduce
    )
    d_expand = scattered(
        outer(hidden_grad[:, :half], mid_low), outer(hidden_grad[:, half:], mid_low), order_expand
    )
    d_out = [
        dot(inner_t[k * local : (k + 1) * local], branch_grad, 1, 0) for k in range(n_own)
    ]
    d_own = d_out[0]
    for k in range(1, n_own):
        d_own = d_own + swap(d_out[k].astype(BF), k).astype(F32)

    d_qkv, attn_sum, sent, kept = attention_backward(
        flags, qkv, lse, pre, w_query, w_key, w_value, pieces, grads
    )
    came = swap(sent, 1)
    second = swap((kept[1].astype(F32) + came[1].astype(F32)).astype(BF), 2)
    grad_tokens = input_gradient(
        (kept[0], came[0], second), own_tokens, gain_attn_row, middle_grad
    )

    weights = jnp.concatenate([d_qkv, d_own.astype(BF)], axis=0)
    batch_bits = [b for b in (1 << i for i in range(n_all.bit_length() - 1)) if b >= n_own]
    share = weights.reshape((2,) * len(batch_bits) + (-1, width)).astype(F32)
    for axis, bit in enumerate(batch_bits):
        keep, send = (lax.slice_in_dim(share, i, i + 1, axis=axis) for i in (0, 1))
        index = (lax.axis_index("batch") >> axis) & 1
        keep, send = jnp.where(index == 0, keep, send), jnp.where(index == 0, send, keep)
        share = keep + swap(send.astype(BF), bit).astype(F32)
    share = share.astype(BF)
    for axis, bit in reversed(list(enumerate(batch_bits))):
        other = swap(share, bit)
        index = (lax.axis_index("batch") >> axis) & 1
        share = jnp.where(
            index == 0,
            jnp.concatenate([share, other], axis=axis),
            jnp.concatenate([other, share], axis=axis),
        )
    total = share.reshape(-1, width).astype(F32)
    small = jnp.stack([attn_sum[0], jnp.sum(ffn_sum, axis=0)])
    for bit in [1 << i for i in range(n_all.bit_length() - 1)]:
        small = small + swap(small, bit)
    g_out = total[3 * local :]
    return (
        output,
        grad_tokens,
        total[:local].T,
        total[local : 2 * local].T,
        total[2 * local : 3 * local].T,
        g_out * gain_inner.astype(F32)[:, None],
        small[0] / gain_attn.astype(F32),
        jnp.sum(g_out * w_output.astype(F32), axis=1),
        small[1],
        d_expand,
        d_reduce * gain_hidden.astype(F32)[:, None],
        jnp.sum(d_reduce * w_reduce.astype(F32), axis=1),
    )


def solution(mesh):
    both = P(AXES, None)
    return jax.shard_map(
        body,
        mesh=mesh,
        in_specs=(
            P("batch", None),
            P(None, "heads"),
            P(None, "heads"),
            P(None, "heads"),
            P("heads", None),
            P(),
            P("heads"),
            P(),
            both,
            both,
            P(AXES),
            both,
            P(),
            P(),
        ),
        out_specs=(
            both,
            both,
            P(None, "heads"),
            P(None, "heads"),
            P(None, "heads"),
            P("heads", None),
            P(),
            P("heads"),
            P(),
            both,
            both,
            P(AXES),
        ),
        check_vma=False,
    )
```

```python
from functools import partial

import jax
import jax.numpy as jnp
from jax import lax
from jax.experimental import pallas as pl
from jax.experimental.pallas import tpu as pltpu
from jax.sharding import PartitionSpec as P

HD = 64
SHORT = 512
EPSILON = 1e-05
MASKED = -1e30
AXES = ("batch", "heads")
BF = jnp.bfloat16
F32 = jnp.float32
VMEM_LIMIT = 60 * 1024 * 1024


def dot(left, right, left_dim, right_dim):
    return lax.dot_general(
        left, right, (((left_dim,), (right_dim,)), ((), ())), preferred_element_type=F32
    )


def params(limit=VMEM_LIMIT):
    return pltpu.CompilerParams(vmem_limit_bytes=limit)


def vmem():
    return pl.BlockSpec(memory_space=pltpu.VMEM)


def smem():
    return pl.BlockSpec(memory_space=pltpu.SMEM)


def anywhere():
    return pl.BlockSpec(memory_space=pl.ANY)


def cost(flops, moved, special=0):
    return pl.CostEstimate(flops=flops, bytes_accessed=moved, transcendentals=special)


def project_kernel(n_after, tokens, w_t, gain, *rest):
    pre, qkv = rest[n_after:]
    rows = tokens.shape[0]
    local = w_t.shape[0] // 3
    gain_row = gain[...].astype(F32)
    for block in range(rows // SHORT):
        at = slice(block * SHORT, (block + 1) * SHORT)
        low = (row_norm(tokens[at, :].astype(F32))[0] * gain_row).astype(BF)
        pre[at, :] = low
        product = dot(w_t[...], low, 1, 1)
        qkv[0:local, at] = (product[0:local] * HD ** (-0.5)).astype(BF)
        qkv[local:, at] = product[local:].astype(BF)


def project(tokens, w_t, gain, after):
    rows, width = tokens.shape
    return pl.pallas_call(
        partial(project_kernel, len(after)),
        out_shape=(
            jax.ShapeDtypeStruct((rows, width), BF),
            jax.ShapeDtypeStruct((w_t.shape[0], rows), BF),
        ),
        in_specs=[vmem()] * 3 + [anywhere()] * len(after),
        out_specs=[vmem()] * 2,
        compiler_params=params(),
        cost_estimate=cost(7000000000, 21000000),
        name="project",
    )(tokens, w_t, gain, *after)


def column_max(values):
    return jnp.max(values.reshape(values.shape[0] // 8, 8, SHORT), axis=0)


def column_sum(values):
    return jnp.sum(values.reshape(values.shape[0] // 8, 8, SHORT), axis=0)


def attend_kernel(n_after, n_out, flags, qkv, *rest):
    lse, *outs, att = rest[n_after:]
    local = qkv.shape[0] // 3
    heads = local // HD
    blocks = qkv.shape[1] // SHORT
    is_long, mine = flags[0], flags[1]
    key_place = lax.broadcasted_iota(jnp.int32, (SHORT, SHORT), 0)
    query_place = lax.broadcasted_iota(jnp.int32, (SHORT, SHORT), 1)

    def run_path(long_path):
        def one_head(head, unused):
            at = pl.ds(pl.multiple_of(head * HD, HD), HD)
            k_at = pl.ds(pl.multiple_of(local + head * HD, HD), HD)
            v_at = pl.ds(pl.multiple_of(2 * local + head * HD, HD), HD)
            for block in range(blocks):
                q_t = qkv[at, block * SHORT : (block + 1) * SHORT]
                keys = [
                    slice(index * SHORT, (index + 1) * SHORT)
                    for index in range(0 if long_path else block, block + 1)
                ]
                parts = [dot(qkv[k_at, key], q_t, 0, 0) for key in keys]
                parts[-1] = jnp.where(key_place <= query_place, parts[-1], MASKED)
                largest = column_max(parts[0])
                for s in parts[1:]:
                    largest = jnp.maximum(largest, column_max(s))
                top = jnp.max(largest, axis=0, keepdims=True)
                total, out = 0.0, 0.0
                for key, s in zip(keys, parts):
                    p = jnp.exp(s - top)
                    total = total + column_sum(p)
                    out = out + dot(qkv[v_at, key], p.astype(BF), 1, 0)
                total = jnp.sum(total, axis=0, keepdims=True)
                att[block, at, :] = (out / total).astype(BF)
                lse[head, block] = jnp.broadcast_to(top + jnp.log(total), (8, SHORT))
            return unused

        lax.fori_loop(0, heads, one_head, 0)

    pl.when(is_long > 0)(lambda: run_path(True))
    pl.when(is_long == 0)(lambda: run_path(False))
    for place in range(n_out):
        outs[place][...] = att[mine ^ place]


def attend(flags, qkv, n_out, after):
    rows = qkv.shape[1]
    blocks = rows // SHORT
    local = qkv.shape[0] // 3
    return pl.pallas_call(
        partial(attend_kernel, len(after), n_out),
        out_shape=(jax.ShapeDtypeStruct((local // HD, blocks, 8, SHORT), F32),)
        + (jax.ShapeDtypeStruct((local, SHORT), BF),) * n_out,
        in_specs=[smem(), vmem()] + [anywhere()] * len(after),
        out_specs=[vmem()] * (1 + n_out),
        scratch_shapes=[pltpu.VMEM((blocks, local, SHORT), BF)],
        compiler_params=params(),
        cost_estimate=cost(15000000000, 45000000),
        name="attend",
    )(flags, qkv, *after)


def attend_back_kernel(
    n_own, n_after, flags, q_all, k_all, v_all, lse, pre, w_q, w_k, w_v, *rest
):
    att, grads = rest[:n_own], rest[n_own : 2 * n_own]
    d_qkv, d_weight, attn_sum, ag, delta = rest[2 * n_own + n_after :]
    rows, width = pre.shape
    blocks = rows // SHORT
    is_long, mine = flags[0], flags[1]

    for place in range(n_own):
        grad = grads[place][...]
        ag[mine ^ place] = grad
        product = grad.astype(F32) * att[place][...].astype(F32)
        delta[mine ^ place] = jnp.broadcast_to(jnp.sum(product, axis=0, keepdims=True), (8, SHORT))

    key_place = lax.broadcasted_iota(jnp.int32, (SHORT, SHORT), 0)
    query_place = lax.broadcasted_iota(jnp.int32, (SHORT, SHORT), 1)

    def run_path(long_path):
        d_q = [None] * blocks
        for block in range(blocks):
            k_cols = slice(block * SHORT, (block + 1) * SHORT)
            k_t = k_all[:, k_cols]
            v_t = v_all[:, k_cols]
            d_k = d_v = None
            for index in range(block, blocks if long_path else block + 1):
                q_t = q_all[:, index * SHORT : (index + 1) * SHORT]
                grad = ag[index]
                p = jnp.exp(dot(k_t, q_t, 0, 0) - lse[0, index][0:1])
                if index == block:
                    p = jnp.where(key_place <= query_place, p, 0.0)
                d_p = dot(v_t, grad, 0, 0)
                d_s = (p * (d_p - delta[index][0:1])).astype(BF)
                p = p.astype(BF)
                add = dot(k_t, d_s, 1, 0)
                d_q[index] = add if d_q[index] is None else d_q[index] + add
                add = dot(q_t, d_s, 1, 1)
                d_k = add if d_k is None else d_k + add
                add = dot(grad, p, 1, 1)
                d_v = add if d_v is None else d_v + add
            d_qkv[HD : 2 * HD, k_cols] = d_k.astype(BF)
            d_qkv[2 * HD :, k_cols] = d_v.astype(BF)
        for block in range(blocks):
            d_qkv[0:HD, block * SHORT : (block + 1) * SHORT] = (d_q[block] * HD ** (-0.5)).astype(BF)

    pl.when(is_long > 0)(lambda: run_path(True))
    pl.when(is_long == 0)(lambda: run_path(False))
    product = dot(d_qkv[...], pre[...], 1, 0)
    d_weight[...] = product.astype(BF)
    cross = jnp.zeros((8, width), F32)
    for place, weight in enumerate((w_q, w_k, w_v)):
        part = product[place * HD : (place + 1) * HD] * weight[...].astype(F32)
        cross = cross + jnp.sum(part.reshape(HD // 8, 8, width), axis=0)
    attn_sum[...] = cross


def attend_back(flags, qkv, head, lse, pre, w_t, att, grads, after):
    rows, width = pre.shape
    blocks = rows // SHORT
    heads = qkv.shape[0] // (3 * HD)
    n_own = len(att)

    def part(place, columns):
        return pl.BlockSpec((HD, columns), lambda i, at=place: (at, 0))

    def whole(struct):
        return pl.BlockSpec(struct.shape, lambda i, n=len(struct.shape): (0,) * n)

    outs = (
        jax.ShapeDtypeStruct((3 * HD, rows), BF),
        jax.ShapeDtypeStruct((3 * HD, width), BF),
        jax.ShapeDtypeStruct((8, width), F32),
    )
    return pl.pallas_call(
        partial(attend_back_kernel, n_own, len(after)),
        grid=(1,),
        out_shape=outs,
        in_specs=[smem()]
        + [part(place * heads + head, rows) for place in range(3)]
        + [pl.BlockSpec((1,) + lse.shape[1:], lambda i: (head, 0, 0, 0)), whole(pre)]
        + [part(place * heads + head, width) for place in range(3)]
        + [part(head, SHORT)] * (2 * n_own)
        + [anywhere()] * len(after),
        out_specs=[whole(o) for o in outs],
        scratch_shapes=[
            pltpu.VMEM((blocks, HD, SHORT), BF),
            pltpu.VMEM((blocks, 8, SHORT), F32),
        ],
        compiler_params=params(),
        cost_estimate=cost(11500000000, 34500000),
        name="attend_back",
    )(flags, qkv, qkv, qkv, lse, pre, w_t, w_t, w_t, *att, *grads, *after)


def pre_gradient_kernel(flags, w_t, *rest):
    d_qkv, (sent, kept) = rest[:-2], rest[-2:]
    mine = flags[1]
    n_own = sent.shape[0] + kept.shape[0]
    for place in range(n_own):
        cols = pl.ds(pl.multiple_of((mine ^ place) * SHORT, SHORT), SHORT)
        joined = [d[i * HD : (i + 1) * HD, cols] for i in range(3) for d in d_qkv]
        grad = dot(w_t[...], jnp.concatenate(joined, axis=0), 0, 0)
        target = sent if place % 2 else kept
        target[place // 2] = grad.astype(BF)


def pre_gradient(flags, w_t, d_qkv, n_own):
    width = w_t.shape[1]
    shape = jax.ShapeDtypeStruct((n_own // 2, width, SHORT), BF)
    return pl.pallas_call(
        pre_gradient_kernel,
        out_shape=(shape, shape),
        in_specs=[smem()] + [vmem()] * (1 + len(d_qkv)),
        out_specs=[vmem()] * 2,
        compiler_params=params(),
        cost_estimate=cost(6000000000, 18000000),
        name="pre_gradient",
    )(flags, w_t, *d_qkv)


def gelu_parts(h):
    phi = jnp.exp(h * h * (-0.5)) * 0.3989422804014327
    big = 0.5 * lax.erf(h * 0.7071067811865476) + 0.5
    return h * big, big + h * phi


def inner_stats(att, width):
    total = sum(jnp.sum(piece[...].astype(F32), axis=0, keepdims=True) for piece in att)
    average = total / width
    square = 0.0
    for piece in att:
        centred = piece[...].astype(F32) - average
        square = square + jnp.sum(centred * centred, axis=0, keepdims=True)
    return average, lax.rsqrt(square / width + EPSILON)


def row_norm(x):
    centred = x - jnp.mean(x, axis=1, keepdims=True)
    factor = lax.rsqrt(jnp.mean(centred * centred, axis=1, keepdims=True) + EPSILON)
    return centred * factor, factor


def fetch(pieces, places, target, sems):
    copies = [
        pltpu.make_async_copy(
            pieces[number].at[pl.ds(start, rows), :], target.at[pl.ds(to, rows), :], sems.at[i]
        )
        for i, (number, start, to, rows) in enumerate(places)
    ]
    for copy in copies:
        copy.start()

    def wait():
        for copy in copies:
            copy.wait()

    return wait


def outer(left, right, outs):
    half = left.shape[1] // 2
    step = half // 2
    for number, out in enumerate(outs):
        for start in range(0, half, step):
            at = slice(number * half + start, number * half + start + step)
            out[start : start + step, :] = dot(left[:, at], right[...], 0, 0).astype(BF)


def expand_kernel(n_own, n_piece, places, *refs):
    att, w_out = refs[:n_own], refs[n_own : 2 * n_own]
    tokens, cotangent, gain_ffn = refs[2 * n_own : 2 * n_own + 3]
    pieces, rest = refs[2 * n_own + 3 : 2 * n_own + 3 + n_piece], refs[2 * n_own + 3 + n_piece :]
    post, slope, factors, middle, mid_low, inner_t, kept, sent, weight, act, sems = rest
    rows, width = tokens.shape
    local = att[0].shape[0]
    hidden = weight.shape[0]
    chunk = width
    wait = fetch(pieces, places, weight, sems)

    average, inner_factor = inner_stats(att, width)
    for place, piece in enumerate(att):
        hat = (piece[...].astype(F32) - average) * inner_factor
        inner_t[place * local : (place + 1) * local, :] = hat.astype(BF)
    branch = dot(inner_t[0:local, :], w_out[0][...], 0, 0)
    for place in range(1, n_own):
        branch += dot(inner_t[place * local : (place + 1) * local, :], w_out[place][...], 0, 0)
    total = tokens[...].astype(F32) + branch
    middle[...] = total
    mid_low[...] = (row_norm(total)[0] * gain_ffn[...].astype(F32)).astype(BF)
    wait()
    for start in range(0, hidden, chunk):
        to = slice(start, start + chunk)
        a, s = gelu_parts(dot(mid_low[...], weight[to, :], 1, 1))
        act[:, to] = a
        slope[:, to] = s.astype(BF)
    n, factor = row_norm(act[...])
    post[...] = n.astype(BF)
    factors[...] = jnp.broadcast_to(factor, (rows, 128))
    outer(post, cotangent, (kept, sent))


def expand_ffn(att, w_out, tokens, cotangent, gain_ffn, expand, places):
    rows, width = tokens.shape
    hidden = sum(e.shape[0] for e in expand)
    n_own = len(att)
    local = att[0].shape[0]
    return pl.pallas_call(
        partial(expand_kernel, n_own, len(expand), places),
        out_shape=(
            jax.ShapeDtypeStruct((rows, hidden), BF),
            jax.ShapeDtypeStruct((rows, hidden), BF),
            jax.ShapeDtypeStruct((rows, 128), F32),
            jax.ShapeDtypeStruct((rows, width), F32),
            jax.ShapeDtypeStruct((rows, width), BF),
            jax.ShapeDtypeStruct((n_own * local, rows), BF),
            jax.ShapeDtypeStruct((hidden // 2, width), BF),
            jax.ShapeDtypeStruct((hidden // 2, width), BF),
        ),
        in_specs=[vmem()] * (2 * n_own + 3) + [anywhere()] * len(expand),
        out_specs=[vmem()] * 8,
        scratch_shapes=[
            pltpu.VMEM((hidden, width), BF),
            pltpu.VMEM((rows, hidden), F32),
            pltpu.SemaphoreType.DMA((len(places),)),
        ],
        compiler_params=params(),
        cost_estimate=cost(12000000000, 36000000),
        name="expand_ffn",
    )(*att, *w_out, tokens, cotangent, gain_ffn, *expand)


def reduce_kernel(n_piece, places, post, slope, factors, middle, cotangent, *rest):
    pieces, (output, hidden_grad, weight, d_post, sems) = rest[:n_piece], rest[n_piece:]
    hidden, width = weight.shape
    chunk = width
    fetch(pieces, places, weight, sems)()
    total = middle[...]
    for start in range(0, hidden, chunk):
        to = slice(start, start + chunk)
        d_post[:, to] = dot(cotangent[...], weight[to, :], 1, 1)
        total = total + dot(post[:, to], weight[to, :], 1, 0)
    output[...] = total.astype(BF)
    e = d_post[...]
    n = post[...].astype(F32)
    mean_e = jnp.sum(e, axis=1, keepdims=True) / hidden
    mean_en = jnp.sum(e * n, axis=1, keepdims=True) / hidden
    grad = factors[:, 0:1] * (e - mean_e - n * mean_en)
    hidden_grad[...] = (grad * slope[...].astype(F32)).astype(BF)


def reduce_ffn(post, slope, factors, middle, cotangent, reduced, places):
    rows, width = middle.shape
    hidden = post.shape[1]
    return pl.pallas_call(
        partial(reduce_kernel, len(reduced), places),
        out_shape=(
            jax.ShapeDtypeStruct((rows, width), BF),
            jax.ShapeDtypeStruct((rows, hidden), BF),
        ),
        in_specs=[vmem()] * 5 + [anywhere()] * len(reduced),
        out_specs=[vmem()] * 2,
        scratch_shapes=[
            pltpu.VMEM((hidden, width), BF),
            pltpu.VMEM((rows, hidden), F32),
            pltpu.SemaphoreType.DMA((len(places),)),
        ],
        compiler_params=params(),
        cost_estimate=cost(15000000000, 45000000),
        name="reduce_ffn",
    )(post, slope, factors, middle, cotangent, *reduced)


def middle_kernel(n_own, n_piece, places, *refs):
    att, w_out = refs[:n_own], refs[n_own : 2 * n_own]
    hidden_grad, middle, mid_low, cotangent, gain_ffn = refs[2 * n_own : 2 * n_own + 5]
    rest = refs[2 * n_own + 5 :]
    pieces, rest = rest[:n_piece], rest[n_piece:]
    middle_grad, branch_grad, ffn_sum, kept, sent = rest[:5]
    grads = rest[5 : 5 + n_own]
    weight, e_buf, sems = rest[5 + n_own :]
    rows, width = middle.shape
    gain_row = gain_ffn[...].astype(F32)
    wait = fetch(pieces, places, weight, sems)
    n, factor = row_norm(middle[...])
    average, inner_factor = inner_stats(att, width)
    wait()
    grad = dot(hidden_grad[...], weight[...], 1, 0)
    ffn_sum[...] = jnp.sum((grad * n).reshape(rows // 8, 8, width), axis=0)
    e = grad * gain_row
    back = factor * (
        e - jnp.mean(e, axis=1, keepdims=True) - n * jnp.mean(e * n, axis=1, keepdims=True)
    )
    full = cotangent[...].astype(F32) + back
    middle_grad[...] = full
    branch_grad[...] = full.astype(BF)

    grad_sum = jnp.zeros((1, rows), F32)
    cross_sum = jnp.zeros((1, rows), F32)
    for place in range(n_own):
        e = dot(w_out[place][...], branch_grad[...], 1, 1)
        e_buf[place] = e
        grad_sum = grad_sum + jnp.sum(e, axis=0, keepdims=True)
        hat = (att[place][...].astype(F32) - average) * inner_factor
        cross_sum = cross_sum + jnp.sum(e * hat, axis=0, keepdims=True)
    for place in range(n_own):
        hat = (att[place][...].astype(F32) - average) * inner_factor
        grad = inner_factor * (e_buf[place] - grad_sum / width - hat * (cross_sum / width))
        grads[place][...] = grad.astype(BF)
    outer(hidden_grad, mid_low, (kept, sent))


def middle_back(att, w_out, hidden_grad, middle, mid_low, cotangent, gain_ffn, expand, places):
    rows, width = middle.shape
    hidden = hidden_grad.shape[1]
    n_own = len(att)
    local = att[0].shape[0]
    return pl.pallas_call(
        partial(middle_kernel, n_own, len(expand), places),
        out_shape=(
            jax.ShapeDtypeStruct((rows, width), F32),
            jax.ShapeDtypeStruct((rows, width), BF),
            jax.ShapeDtypeStruct((8, width), F32),
            jax.ShapeDtypeStruct((hidden // 2, width), BF),
            jax.ShapeDtypeStruct((hidden // 2, width), BF),
        )
        + (jax.ShapeDtypeStruct((local, rows), BF),) * n_own,
        in_specs=[vmem()] * (2 * n_own + 5) + [anywhere()] * len(expand),
        out_specs=[vmem()] * (5 + n_own),
        scratch_shapes=[
            pltpu.VMEM((hidden, width), BF),
            pltpu.VMEM((n_own, local, rows), F32),
            pltpu.SemaphoreType.DMA((len(places),)),
        ],
        compiler_params=params(),
        cost_estimate=cost(12500000000, 37500000),
        name="middle_back",
    )(*att, *w_out, hidden_grad, middle, mid_low, cotangent, gain_ffn, *expand)


def input_gradient_kernel(first, second, third, tokens, gain, middle_grad, out):
    width = first.shape[0]
    total = first[...].astype(F32) + second[...].astype(F32) + third[...].astype(F32)
    x = tokens[...].astype(F32)
    centred = x - jnp.mean(x, axis=1, keepdims=True)
    factor = lax.rsqrt(jnp.mean(centred * centred, axis=1, keepdims=True) + EPSILON)
    n = centred * factor
    e = total.T * gain[...].astype(F32)
    back = factor * (
        e - jnp.mean(e, axis=1, keepdims=True) - n * jnp.mean(e * n, axis=1, keepdims=True)
    )
    out[...] = (middle_grad[...] + back).astype(BF)


def input_gradient(terms, tokens, gain, middle_grad):
    return pl.pallas_call(
        input_gradient_kernel,
        out_shape=jax.ShapeDtypeStruct(tokens.shape, BF),
        in_specs=[vmem()] * 6,
        out_specs=vmem(),
        compiler_params=params(),
        cost_estimate=cost(4500000000, 13500000),
        name="input_gradient",
    )(*terms, tokens, gain, middle_grad)


def body(
    tokens,
    w_query,
    w_key,
    w_value,
    w_output,
    gain_attn,
    gain_inner,
    gain_ffn,
    w_expand,
    w_reduce,
    gain_hidden,
    cotangent,
    seq_length,
    seq_group,
):
    n_batch, n_own = lax.axis_size("batch"), lax.axis_size("heads")
    n_all = n_batch * n_own
    mine = lax.axis_index("heads")
    quarter = cotangent.shape[0]
    width = tokens.shape[1]
    local = w_query.shape[1]
    n_heads = local // HD

    def swap(value, bit):
        return lax.ppermute(value, AXES, [(i, i ^ bit) for i in range(n_all)])

    is_long = jnp.any((seq_group == lax.axis_index("batch")) & (seq_length > SHORT))
    flags = jnp.stack([is_long.astype(jnp.int32), mine.astype(jnp.int32)])
    far = [1 << b for b in range(3, n_all.bit_length() - 1)]
    near = (2, 4, 6)

    def parts(value, offsets):
        return [value] + [swap(value, off) for off in offsets]

    def around(value, offsets):
        return jnp.concatenate(parts(value, offsets), axis=0)

    def far_steps(value):
        for bit in reversed(far):
            value = around(value, (bit,))
            yield value

    def far_sums(value):
        for bit in far:
            value = value.reshape(2, -1, width)
            value = value[0] + swap(value[1].astype(BF), bit).astype(F32)
            yield value

    def near_terms(kept, came):
        at = [slice(i * kept.shape[0] // 4, (i + 1) * kept.shape[0] // 4) for i in range(4)]
        terms = [(kept[a].astype(F32) + came[a].astype(F32)).astype(BF) for a in at[1:]]
        return [(kept[at[0]], came[at[0]])] + terms

    def near_sum(own, came):
        return sum(c.astype(F32) for c in [*own, *came])

    phase = lax.optimization_barrier

    def sum_begin(value):
        rows = value.shape[0]
        value = lax.all_to_all(value, "batch", 0, 0, tiled=True)
        return value.reshape(n_batch, rows // n_batch, width)

    def sum_middle(value):
        return jnp.sum(value.astype(F32), axis=0)

    def sum_end(share):
        share = jnp.broadcast_to(share.astype(BF)[None], (n_batch,) + share.shape)
        return lax.all_to_all(share, "batch", 0, 0, tiled=True)

    def last(steps):
        *_, value = steps
        return value

    w_t = jnp.concatenate([w_query.T, w_key.T, w_value.T], axis=0)
    w_reduce_scaled = (w_reduce.astype(F32) * gain_hidden.astype(F32)[:, None]).astype(BF)
    w_output_scaled = (w_output.astype(F32) * gain_inner.astype(F32)[:, None]).astype(BF)
    gain_attn_row = gain_attn[None, :]

    half = w_reduce.shape[0] // 2
    n_far = n_batch // 2
    if len(far) == 2:
        expand_far = parts(w_expand, (far[1], far[0], far[0] | far[1]))
    else:
        expand_far = [last(far_steps(w_expand))]
    reduce_1 = w_reduce_scaled[:half]
    reduce_2 = around(around(w_reduce_scaled[half:], (2,)), (4,))
    w_out_y = swap(w_output_scaled, 2)
    pre, qkv = project(tokens, w_t, gain_attn_row, [])
    expand_far, reduce_1, reduce_2, w_out_y, pre, qkv = phase(
        (expand_far, reduce_1, reduce_2, w_out_y, pre, qkv)
    )

    expand = parts(jnp.concatenate(expand_far), near)
    reduce_1, reduce_2 = parts(reduce_1, far[-1:]), parts(reduce_2, far[-1:])
    w_out_c = swap(jnp.stack([w_output_scaled, w_out_y]), 1)
    w_out = [w_output_scaled, w_out_c[0], w_out_y, w_out_c[1]]
    lse, *pieces = attend(flags, qkv, n_own, [])
    expand, reduce_1, reduce_2, w_out, lse, pieces = phase(
        (expand, reduce_1, reduce_2, w_out, lse, pieces)
    )

    expand, reduce_1, reduce_2 = (jnp.concatenate(v) for v in (expand, reduce_1, reduce_2))
    for bit in far[-2::-1]:
        reduce_1 = around(reduce_1, (bit,))
    att = [pieces[0]] + [swap(pieces[k], k) for k in range(1, n_own)]
    expand = [expand, swap(expand, 1)]
    own_tokens = lax.dynamic_slice_in_dim(tokens, mine * quarter, quarter, 0)
    att, expand, reduce_1, reduce_2, own_tokens = phase(
        (att, expand, reduce_1, reduce_2, own_tokens)
    )

    def stacked(parts):
        starts = [sum(p.shape[0] for p in parts[:i]) for i in range(len(parts))]
        return [(i, 0, start, p.shape[0]) for i, (start, p) in enumerate(zip(starts, parts))]

    places = stacked(expand)
    reduce_1 = parts(reduce_1, near)
    for bit in far[-2:0:-1]:
        reduce_2 = around(reduce_2, (bit,))
    reduce_2 = parts(reduce_2, far[:1])
    post, slope, factors, middle, mid_low, inner_t, kept_r, sent_r = expand_ffn(
        att, w_out, own_tokens, cotangent, gain_ffn[None, :], expand, places
    )
    reduce_1, reduce_2, post, slope, factors, middle, mid_low, inner_t, kept_r, sent_r = phase(
        (reduce_1, reduce_2, post, slope, factors, middle, mid_low, inner_t, kept_r, sent_r)
    )

    reduce_1 = jnp.stack(reduce_1).reshape(4, n_far, half, width)
    reduce_2 = jnp.concatenate(reduce_2).reshape(n_far, 4, half, width).swapaxes(0, 1)
    reduced = jnp.concatenate([reduce_1, reduce_2], axis=2).reshape(-1, width)
    reduced = [reduced, swap(reduced, 1)]
    reduced, post = phase((reduced, post))

    came_r = swap(sent_r, 1)
    output, hidden_grad = reduce_ffn(post, slope, factors, middle, cotangent, reduced, stacked(reduced))
    came_r, output, hidden_grad = phase((came_r, output, hidden_grad))

    d_reduce = near_terms(kept_r, came_r)
    came_r = [swap(d_reduce[1], 2), swap(d_reduce[2], 4)]
    middle_grad, branch_grad, ffn_sum, kept_e, sent_e, *att_grads = middle_back(
        att, w_out, hidden_grad, middle, mid_low, cotangent, gain_ffn[None, :], expand, places
    )
    came_r, d_reduce, middle_grad, branch_grad, ffn_sum, kept_e, sent_e, att_grads = phase(
        (came_r, d_reduce, middle_grad, branch_grad, ffn_sum, kept_e, sent_e, att_grads)
    )

    grads = [att_grads[0]] + [swap(att_grads[k], k) for k in range(1, n_own)]
    d_out = [dot(inner_t[k * local : (k + 1) * local], branch_grad, 1, 0) for k in range(n_own)]
    sent_e, grads, d_out = phase((sent_e, grads, d_out))

    def back(head):
        return attend_back(flags, qkv, head, lse, pre, w_t, pieces, grads, [])

    came_r.append(swap(d_reduce[3], 6))
    came_e = swap(sent_e, 1)
    came = swap(jnp.stack([d_out[1], d_out[3]]).astype(BF), 1).astype(F32)
    d_own = d_out[0] + came[0] + swap((d_out[2] + came[1]).astype(BF), 2).astype(F32)
    back_0 = back(0)
    back_0, d_own, came_r, came_e, grads = phase((back_0, d_own, came_r, came_e, grads))

    sums_r = far_sums(near_sum(d_reduce[0], came_r))
    d_expand = near_terms(kept_e, came_e)
    came_e = [swap(d_expand[1], 2), swap(d_expand[2], 4)]
    share_0 = sum_begin(jnp.concatenate([back_0[1], d_own.astype(BF)], axis=0))
    d_reduce = next(sums_r)
    back_1 = back(1)
    back_1, came_e, d_expand, d_reduce, share_0, grads = phase(
        (back_1, came_e, d_expand, d_reduce, share_0, grads)
    )

    came_e.append(swap(d_expand[3], 6))
    for bit in far[1:]:
        d_reduce = d_reduce.reshape(2, -1, width)
        d_reduce = d_reduce[0] + swap(d_reduce[1].astype(BF), bit).astype(F32)
    back_2 = back(2)
    back_2, came_e, d_reduce = phase((back_2, came_e, d_reduce))

    d_expand = last(far_sums(near_sum(d_expand[0], came_e)))
    share_1 = sum_begin(jnp.concatenate([back_1[1], back_2[1]], axis=0))
    small = jnp.sum(jnp.stack([back_0[2] + back_1[2] + back_2[2], ffn_sum]), axis=1)
    small = small + swap(small, 1)
    small = small + swap(small, 2)
    sent, kept = pre_gradient(flags, w_t, [back_0[0], back_1[0], back_2[0]], n_own)
    share_0, share_1 = sum_middle(share_0), sum_middle(share_1)
    total = sum_end(jnp.concatenate([share_0, share_1, small], axis=0)).astype(F32)
    count_0, count = share_0.shape[0], share_0.shape[0] + share_1.shape[0]
    small = jnp.sum(total[:, count:], axis=0)
    total_0 = total[:, :count_0].reshape(-1, width)
    total_1 = total[:, count_0:count].reshape(-1, width)
    totals = [total_0, total_1[: 3 * HD], total_1[3 * HD :]]
    came = swap(sent, 1)
    second = swap((kept[1].astype(F32) + came[1].astype(F32)).astype(BF), 2)
    grad_tokens = input_gradient((kept[0], came[0], second), own_tokens, gain_attn_row, middle_grad)

    def weight_grad(place):
        at = slice(place * HD, (place + 1) * HD)
        return jnp.concatenate([t[at] for t in totals], axis=0).T

    g_out = totals[0][3 * HD :]
    return (
        output,
        grad_tokens,
        weight_grad(0),
        weight_grad(1),
        weight_grad(2),
        g_out * gain_inner.astype(F32)[:, None],
        small[0] / gain_attn.astype(F32),
        jnp.sum(g_out * w_output.astype(F32), axis=1),
        small[1],
        d_expand,
        d_reduce * gain_hidden.astype(F32)[:, None],
        jnp.sum(d_reduce * w_reduce.astype(F32), axis=1),
    )


def solution(mesh):
    both = P(AXES, None)
    return jax.shard_map(
        body,
        mesh=mesh,
        in_specs=(
            P("batch", None),
            P(None, "heads"),
            P(None, "heads"),
            P(None, "heads"),
            P("heads", None),
            P(),
            P("heads"),
            P(),
            both,
            both,
            P(AXES),
            both,
            P(),
            P(),
        ),
        out_specs=(
            both,
            both,
            P(None, "heads"),
            P(None, "heads"),
            P(None, "heads"),
            P("heads", None),
            P(),
            P("heads"),
            P(),
            both,
            both,
            P(AXES),
        ),
        check_vma=False,
    )
```

```python
from functools import partial

import jax
import jax.numpy as jnp
from jax import lax
from jax.experimental import pallas as pl
from jax.experimental.pallas import tpu as pltpu
from jax.sharding import PartitionSpec as P

HD = 64
SHORT = 512
EPSILON = 1e-05
MASKED = -1e30
AXES = ("batch", "heads")
BF = jnp.bfloat16
F32 = jnp.float32
VMEM_LIMIT = 60 * 1024 * 1024


def dot(left, right, left_dim, right_dim):
    return lax.dot_general(
        left, right, (((left_dim,), (right_dim,)), ((), ())), preferred_element_type=F32
    )


def params(limit=VMEM_LIMIT):
    return pltpu.CompilerParams(vmem_limit_bytes=limit)


def vmem():
    return pl.BlockSpec(memory_space=pltpu.VMEM)


def smem():
    return pl.BlockSpec(memory_space=pltpu.SMEM)


def anywhere():
    return pl.BlockSpec(memory_space=pl.ANY)


def cost(flops, moved, special=0):
    return pl.CostEstimate(flops=flops, bytes_accessed=moved, transcendentals=special)


def project_kernel(n_after, tokens, w_t, gain, *rest):
    pre, qkv = rest[n_after:]
    rows = tokens.shape[0]
    local = w_t.shape[0] // 3
    gain_row = gain[...].astype(F32)
    for block in range(rows // SHORT):
        at = slice(block * SHORT, (block + 1) * SHORT)
        low = (row_norm(tokens[at, :].astype(F32))[0] * gain_row).astype(BF)
        pre[at, :] = low
        product = dot(w_t[...], low, 1, 1)
        qkv[0:local, at] = (product[0:local] * HD ** (-0.5)).astype(BF)
        qkv[local:, at] = product[local:].astype(BF)


def project(tokens, w_t, gain, after):
    rows, width = tokens.shape
    return pl.pallas_call(
        partial(project_kernel, len(after)),
        out_shape=(
            jax.ShapeDtypeStruct((rows, width), BF),
            jax.ShapeDtypeStruct((w_t.shape[0], rows), BF),
        ),
        in_specs=[vmem()] * 3 + [anywhere()] * len(after),
        out_specs=[vmem()] * 2,
        compiler_params=params(),
        cost_estimate=cost(7000000000, 21000000),
        name="project",
    )(tokens, w_t, gain, *after)


def column_max(values):
    return jnp.max(values.reshape(values.shape[0] // 8, 8, SHORT), axis=0)


def column_sum(values):
    return jnp.sum(values.reshape(values.shape[0] // 8, 8, SHORT), axis=0)


def attend_kernel(n_after, n_out, flags, qkv, *rest):
    lse, *outs, att = rest[n_after:]
    local = qkv.shape[0] // 3
    heads = local // HD
    blocks = qkv.shape[1] // SHORT
    is_long, mine = flags[0], flags[1]
    key_place = lax.broadcasted_iota(jnp.int32, (SHORT, SHORT), 0)
    query_place = lax.broadcasted_iota(jnp.int32, (SHORT, SHORT), 1)

    def run_path(long_path):
        def one_head(head, unused):
            at = pl.ds(pl.multiple_of(head * HD, HD), HD)
            k_at = pl.ds(pl.multiple_of(local + head * HD, HD), HD)
            v_at = pl.ds(pl.multiple_of(2 * local + head * HD, HD), HD)
            for block in range(blocks):
                q_t = qkv[at, block * SHORT : (block + 1) * SHORT]
                keys = [
                    slice(index * SHORT, (index + 1) * SHORT)
                    for index in range(0 if long_path else block, block + 1)
                ]
                parts = [dot(qkv[k_at, key], q_t, 0, 0) for key in keys]
                parts[-1] = jnp.where(key_place <= query_place, parts[-1], MASKED)
                largest = column_max(parts[0])
                for s in parts[1:]:
                    largest = jnp.maximum(largest, column_max(s))
                top = jnp.max(largest, axis=0, keepdims=True)
                total, out = 0.0, 0.0
                for key, s in zip(keys, parts):
                    p = jnp.exp(s - top)
                    total = total + column_sum(p)
                    out = out + dot(qkv[v_at, key], p.astype(BF), 1, 0)
                total = jnp.sum(total, axis=0, keepdims=True)
                att[block, at, :] = (out / total).astype(BF)
                lse[head, block] = jnp.broadcast_to(top + jnp.log(total), (8, SHORT))
            return unused

        lax.fori_loop(0, heads, one_head, 0)

    pl.when(is_long > 0)(lambda: run_path(True))
    pl.when(is_long == 0)(lambda: run_path(False))
    for place in range(n_out):
        outs[place][...] = att[mine ^ place]


def attend(flags, qkv, n_out, after):
    rows = qkv.shape[1]
    blocks = rows // SHORT
    local = qkv.shape[0] // 3
    return pl.pallas_call(
        partial(attend_kernel, len(after), n_out),
        out_shape=(jax.ShapeDtypeStruct((local // HD, blocks, 8, SHORT), F32),)
        + (jax.ShapeDtypeStruct((local, SHORT), BF),) * n_out,
        in_specs=[smem(), vmem()] + [anywhere()] * len(after),
        out_specs=[vmem()] * (1 + n_out),
        scratch_shapes=[pltpu.VMEM((blocks, local, SHORT), BF)],
        compiler_params=params(),
        cost_estimate=cost(15000000000, 45000000),
        name="attend",
    )(flags, qkv, *after)


def attend_back_kernel(n_own, n_terms, n_earlier, *refs):
    flags, q_all, k_all, v_all, lse, pre, w_q, w_k, w_v = refs[:9]
    att, grads, rest = refs[9 : 9 + n_own], refs[9 + n_own : 9 + 2 * n_own], refs[9 + 2 * n_own :]
    terms, rest = rest[:n_terms], rest[n_terms:]
    if n_earlier:
        w_t, d_before, rest = rest[0], rest[1], rest[2:]
        earlier, rest = rest[:n_earlier], rest[n_earlier:]
    d_qkv, d_weight, attn_sum, *rest = rest
    if n_earlier:
        sent, kept, *rest = rest
    ag, delta = rest
    rows, width = pre.shape
    blocks = rows // SHORT
    is_long, mine = flags[0], flags[1]

    for place in range(n_own):
        grad = grads[place][...]
        ag[mine ^ place] = grad
        product = grad.astype(F32) * att[place][...].astype(F32)
        delta[mine ^ place] = jnp.broadcast_to(jnp.sum(product, axis=0, keepdims=True), (8, SHORT))

    key_place = lax.broadcasted_iota(jnp.int32, (SHORT, SHORT), 0)
    query_place = lax.broadcasted_iota(jnp.int32, (SHORT, SHORT), 1)

    def run_path(long_path):
        d_q = [None] * blocks
        for block in range(blocks):
            k_cols = slice(block * SHORT, (block + 1) * SHORT)
            k_t = k_all[:, k_cols]
            v_t = v_all[:, k_cols]
            d_k = d_v = None
            for index in range(block, blocks if long_path else block + 1):
                q_t = q_all[:, index * SHORT : (index + 1) * SHORT]
                grad = ag[index]
                p = jnp.exp(dot(k_t, q_t, 0, 0) - lse[0, index][0:1])
                if index == block:
                    p = jnp.where(key_place <= query_place, p, 0.0)
                d_p = dot(v_t, grad, 0, 0)
                d_s = (p * (d_p - delta[index][0:1])).astype(BF)
                p = p.astype(BF)
                add = dot(k_t, d_s, 1, 0)
                d_q[index] = add if d_q[index] is None else d_q[index] + add
                add = dot(q_t, d_s, 1, 1)
                d_k = add if d_k is None else d_k + add
                add = dot(grad, p, 1, 1)
                d_v = add if d_v is None else d_v + add
            d_qkv[HD : 2 * HD, k_cols] = d_k.astype(BF)
            d_qkv[2 * HD :, k_cols] = d_v.astype(BF)
        for block in range(blocks):
            d_qkv[0:HD, block * SHORT : (block + 1) * SHORT] = (d_q[block] * HD ** (-0.5)).astype(BF)

    pl.when(is_long > 0)(lambda: run_path(True))
    pl.when(is_long == 0)(lambda: run_path(False))
    product = dot(d_qkv[...], pre[...], 1, 0)
    start = d_before.shape[0] if n_earlier else 0
    d_weight[start : start + 3 * HD, :] = product.astype(BF)
    if n_earlier:
        d_weight[0:start, :] = d_before[...]
    if n_terms:
        d_weight[3 * HD :, :] = sum(t[...].astype(F32) for t in terms).astype(BF)
    cross = jnp.zeros((8, width), F32)
    for place, weight in enumerate((w_q, w_k, w_v)):
        part = product[place * HD : (place + 1) * HD] * weight[...].astype(F32)
        cross = cross + jnp.sum(part.reshape(HD // 8, 8, width), axis=0)
    attn_sum[...] = cross
    if n_earlier:
        for place in range(n_own):
            cols = pl.ds(pl.multiple_of((mine ^ place) * SHORT, SHORT), SHORT)
            joined = [d[i * HD : (i + 1) * HD, cols] for i in range(3) for d in (*earlier, d_qkv)]
            grad = dot(w_t[...], jnp.concatenate(joined, axis=0), 0, 0)
            target = sent if place % 2 else kept
            target[place // 2] = grad.astype(BF)


def attend_back(flags, qkv, head, lse, pre, w_t, att, grads, terms=(), d_before=None, earlier=()):
    rows, width = pre.shape
    blocks = rows // SHORT
    heads = qkv.shape[0] // (3 * HD)
    n_own = len(att)

    def part(place, columns):
        return pl.BlockSpec((HD, columns), lambda i, at=place: (at, 0))

    def whole(struct):
        return pl.BlockSpec(struct.shape, lambda i, n=len(struct.shape): (0,) * n)

    more = [w_t, d_before, *earlier] if earlier else []
    weight_rows = 3 * HD + sum(v.shape[0] for v in [*terms[:1], *more[1:2]])
    outs = (
        jax.ShapeDtypeStruct((3 * HD, rows), BF),
        jax.ShapeDtypeStruct((weight_rows, width), BF),
        jax.ShapeDtypeStruct((8, width), F32),
    )
    if earlier:
        outs += (jax.ShapeDtypeStruct((n_own // 2, width, SHORT), BF),) * 2
    return pl.pallas_call(
        partial(attend_back_kernel, n_own, len(terms), len(earlier)),
        grid=(1,),
        out_shape=outs,
        in_specs=[smem()]
        + [part(place * heads + head, rows) for place in range(3)]
        + [pl.BlockSpec((1,) + lse.shape[1:], lambda i: (head, 0, 0, 0)), whole(pre)]
        + [part(place * heads + head, width) for place in range(3)]
        + [part(head, SHORT)] * (2 * n_own)
        + [whole(v) for v in [*terms, *more]],
        out_specs=[whole(o) for o in outs],
        scratch_shapes=[
            pltpu.VMEM((blocks, HD, SHORT), BF),
            pltpu.VMEM((blocks, 8, SHORT), F32),
        ],
        compiler_params=params(),
        cost_estimate=cost(11_500_000_000, 34_500_000),
        name="attend_back",
    )(flags, qkv, qkv, qkv, lse, pre, w_t, w_t, w_t, *att, *grads, *terms, *more)


def gelu_parts(h):
    phi = jnp.exp(h * h * (-0.5)) * 0.3989422804014327
    big = 0.5 * lax.erf(h * 0.7071067811865476) + 0.5
    return h * big, big + h * phi


def inner_stats(att, width):
    total = sum(jnp.sum(piece[...].astype(F32), axis=0, keepdims=True) for piece in att)
    average = total / width
    square = 0.0
    for piece in att:
        centred = piece[...].astype(F32) - average
        square = square + jnp.sum(centred * centred, axis=0, keepdims=True)
    return average, lax.rsqrt(square / width + EPSILON)


def row_norm(x):
    centred = x - jnp.mean(x, axis=1, keepdims=True)
    factor = lax.rsqrt(jnp.mean(centred * centred, axis=1, keepdims=True) + EPSILON)
    return centred * factor, factor


def fetch(pieces, places, target, sems):
    copies = [
        pltpu.make_async_copy(
            pieces[number].at[pl.ds(start, rows), :], target.at[pl.ds(to, rows), :], sems.at[i]
        )
        for i, (number, start, to, rows) in enumerate(places)
    ]
    for copy in copies:
        copy.start()

    def wait():
        for copy in copies:
            copy.wait()

    return wait


def outer_kernel(left, left_came, right, right_came, *outs):
    size = outs[0].shape[0]
    for number, out in enumerate(outs):
        at = slice(number * size, (number + 1) * size)
        product = dot(left[:, at], right[...], 0, 0)
        out[...] = (product + dot(left_came[:, at], right_came[...], 0, 0)).astype(BF)


def outer(left, left_came, right, right_came):
    out = jax.ShapeDtypeStruct((left.shape[1] // 4, right.shape[1]), BF)
    return pl.pallas_call(
        outer_kernel,
        out_shape=(out,) * 4,
        in_specs=[vmem()] * 4,
        out_specs=[vmem()] * 4,
        compiler_params=params(),
        cost_estimate=cost(5_000_000_000, 15_000_000),
        name="outer",
    )(left, left_came, right, right_came)


def expand_kernel(n_own, n_piece, places, flags, *refs):
    att, w_out = refs[:n_own], refs[n_own : 2 * n_own]
    tokens, gain_ffn = refs[2 * n_own : 2 * n_own + 2]
    pieces, rest = refs[2 * n_own + 2 : 2 * n_own + 2 + n_piece], refs[2 * n_own + 2 + n_piece :]
    *posts, slope, factors, middle, mid_low, inner_t, weight, act, own, sems, own_sem = rest
    rows, width = middle.shape
    start = pl.multiple_of(flags[1] * rows, rows)
    own_copy = pltpu.make_async_copy(tokens.at[pl.ds(start, rows), :], own, own_sem)
    own_copy.start()
    local = att[0].shape[0]
    hidden = weight.shape[0]
    chunk = width
    wait = fetch(pieces, places, weight, sems)

    average, inner_factor = inner_stats(att, width)
    for place, piece in enumerate(att):
        hat = (piece[...].astype(F32) - average) * inner_factor
        inner_t[place * local : (place + 1) * local, :] = hat.astype(BF)
    branch = dot(inner_t[0:local, :], w_out[0][...], 0, 0)
    for place in range(1, n_own):
        branch += dot(inner_t[place * local : (place + 1) * local, :], w_out[place][...], 0, 0)
    own_copy.wait()
    total = own[...].astype(F32) + branch
    middle[...] = total
    mid_low[...] = (row_norm(total)[0] * gain_ffn[...].astype(F32)).astype(BF)
    wait()
    for start in range(0, hidden, chunk):
        to = slice(start, start + chunk)
        a, s = gelu_parts(dot(mid_low[...], weight[to, :], 1, 1))
        act[:, to] = a
        slope[:, to] = s.astype(BF)
    n, factor = row_norm(act[...])
    for number, post in enumerate(posts):
        post[...] = n[:, number * hidden // 2 : (number + 1) * hidden // 2].astype(BF)
    factors[...] = jnp.broadcast_to(factor, (rows, 128))


def expand_ffn(flags, att, w_out, tokens, gain_ffn, expand, places):
    rows, width = att[0].shape[1], tokens.shape[1]
    hidden = sum(e.shape[0] for e in expand)
    n_own = len(att)
    local = att[0].shape[0]
    return pl.pallas_call(
        partial(expand_kernel, n_own, len(expand), places),
        out_shape=(
            jax.ShapeDtypeStruct((rows, hidden // 2), BF),
            jax.ShapeDtypeStruct((rows, hidden // 2), BF),
            jax.ShapeDtypeStruct((rows, hidden), BF),
            jax.ShapeDtypeStruct((rows, 128), F32),
            jax.ShapeDtypeStruct((rows, width), F32),
            jax.ShapeDtypeStruct((rows, width), BF),
            jax.ShapeDtypeStruct((n_own * local, rows), BF),
        ),
        in_specs=[smem()]
        + [vmem()] * (2 * n_own)
        + [anywhere(), vmem()]
        + [anywhere()] * len(expand),
        out_specs=[vmem()] * 7,
        scratch_shapes=[
            pltpu.VMEM((hidden, width), BF),
            pltpu.VMEM((rows, hidden), F32),
            pltpu.VMEM((rows, width), BF),
            pltpu.SemaphoreType.DMA((len(places),)),
            pltpu.SemaphoreType.DMA,
        ],
        compiler_params=params(),
        cost_estimate=cost(12000000000, 36000000),
        name="expand_ffn",
    )(flags, *att, *w_out, tokens, gain_ffn, *expand)


def reduce_kernel(n_piece, places, *refs):
    posts, (slope, factors, middle, cotangent), rest = refs[:2], refs[2:6], refs[6:]
    pieces, (output, *grads, weight, d_post, sems) = rest[:n_piece], rest[n_piece:]
    hidden, width = weight.shape
    half = hidden // 2
    fetch(pieces, places, weight, sems)()
    total = middle[...]
    for start in range(0, hidden, width):
        at = slice(start % half, start % half + width)
        rows = slice(start, start + width)
        d_post[:, rows] = dot(cotangent[...], weight[rows, :], 1, 1)
        total = total + dot(posts[start // half][:, at], weight[rows, :], 1, 0)
    output[...] = total.astype(BF)
    mean_e, mean_en = 0.0, 0.0
    for number, post in enumerate(posts):
        e = d_post[:, number * half : (number + 1) * half]
        mean_e = mean_e + jnp.sum(e, axis=1, keepdims=True) / hidden
        mean_en = mean_en + jnp.sum(e * post[...].astype(F32), axis=1, keepdims=True) / hidden
    for number, (post, grad) in enumerate(zip(posts, grads)):
        at = slice(number * half, (number + 1) * half)
        back = d_post[:, at] - mean_e - post[...].astype(F32) * mean_en
        grad[...] = (factors[:, 0:1] * back * slope[:, at].astype(F32)).astype(BF)


def reduce_ffn(posts, slope, factors, middle, cotangent, reduced, places):
    rows, width = middle.shape
    hidden = slope.shape[1]
    return pl.pallas_call(
        partial(reduce_kernel, len(reduced), places),
        out_shape=(
            jax.ShapeDtypeStruct((rows, width), BF),
            jax.ShapeDtypeStruct((rows, hidden // 2), BF),
            jax.ShapeDtypeStruct((rows, hidden // 2), BF),
        ),
        in_specs=[vmem()] * 6 + [anywhere()] * len(reduced),
        out_specs=[vmem()] * 3,
        scratch_shapes=[
            pltpu.VMEM((hidden, width), BF),
            pltpu.VMEM((rows, hidden), F32),
            pltpu.SemaphoreType.DMA((len(places),)),
        ],
        compiler_params=params(),
        cost_estimate=cost(15_000_000_000, 45_000_000),
        name="reduce_ffn",
    )(*posts, slope, factors, middle, cotangent, *reduced)


def middle_kernel(n_own, n_piece, places, *refs):
    att, w_out = refs[:n_own], refs[n_own : 2 * n_own]
    *hidden_grads, middle, cotangent, inner_t, gain_ffn = refs[2 * n_own : 2 * n_own + 6]
    rest = refs[2 * n_own + 6 :]
    pieces, rest = rest[:n_piece], rest[n_piece:]
    middle_grad, ffn_sum, sent, kept = rest[:4]
    grads = rest[4 : 4 + n_own]
    weight, branch_grad, e_buf, sems = rest[4 + n_own :]
    rows, width = middle.shape
    local = att[0].shape[0]
    half = weight.shape[0] // 2
    gain_row = gain_ffn[...].astype(F32)
    wait = fetch(pieces, places, weight, sems)
    n, factor = row_norm(middle[...])
    average, inner_factor = inner_stats(att, width)
    wait()
    grad = dot(hidden_grads[0][...], weight[0:half, :], 1, 0)
    grad = grad + dot(hidden_grads[1][...], weight[half:, :], 1, 0)
    ffn_sum[...] = jnp.sum((grad * n).reshape(rows // 8, 8, width), axis=0)
    e = grad * gain_row
    back = factor * (
        e - jnp.mean(e, axis=1, keepdims=True) - n * jnp.mean(e * n, axis=1, keepdims=True)
    )
    full = cotangent[...].astype(F32) + back
    middle_grad[...] = full
    branch_grad[...] = full.astype(BF)

    grad_sum = jnp.zeros((1, rows), F32)
    cross_sum = jnp.zeros((1, rows), F32)
    for place in range(n_own):
        e = dot(w_out[place][...], branch_grad[...], 1, 1)
        e_buf[place] = e
        grad_sum = grad_sum + jnp.sum(e, axis=0, keepdims=True)
        hat = (att[place][...].astype(F32) - average) * inner_factor
        cross_sum = cross_sum + jnp.sum(e * hat, axis=0, keepdims=True)
    for place in range(n_own):
        hat = (att[place][...].astype(F32) - average) * inner_factor
        grad = inner_factor * (e_buf[place] - grad_sum / width - hat * (cross_sum / width))
        grads[place][...] = grad.astype(BF)
        target = sent if place % 2 else kept
        at = slice(place * local, (place + 1) * local)
        target[place // 2] = dot(inner_t[at, :], branch_grad[...], 1, 0).astype(BF)


def middle_back(att, w_out, hidden_grads, middle, cotangent, inner_t, gain_ffn, expand, places):
    rows, width = middle.shape
    hidden = 2 * hidden_grads[0].shape[1]
    n_own = len(att)
    local = att[0].shape[0]
    return pl.pallas_call(
        partial(middle_kernel, n_own, len(expand), places),
        out_shape=(
            jax.ShapeDtypeStruct((rows, width), F32),
            jax.ShapeDtypeStruct((8, width), F32),
            jax.ShapeDtypeStruct((n_own // 2, local, width), BF),
            jax.ShapeDtypeStruct((n_own // 2, local, width), BF),
        )
        + (jax.ShapeDtypeStruct((local, rows), BF),) * n_own,
        in_specs=[vmem()] * (2 * n_own + 6) + [anywhere()] * len(expand),
        out_specs=[vmem()] * (4 + n_own),
        scratch_shapes=[
            pltpu.VMEM((hidden, width), BF),
            pltpu.VMEM((rows, width), BF),
            pltpu.VMEM((n_own, local, rows), F32),
            pltpu.SemaphoreType.DMA((len(places),)),
        ],
        compiler_params=params(),
        cost_estimate=cost(12_500_000_000, 37_500_000),
        name="middle_back",
    )(*att, *w_out, *hidden_grads, middle, cotangent, inner_t, gain_ffn, *expand)


def input_gradient_kernel(flags, first, second, third, tokens, gain, middle_grad, out, own, sem):
    rows = out.shape[0]
    start = pl.multiple_of(flags[1] * rows, rows)
    copy = pltpu.make_async_copy(tokens.at[pl.ds(start, rows), :], own, sem)
    copy.start()
    total = first[...].astype(F32) + second[...].astype(F32) + third[...].astype(F32)
    e = total.T * gain[...].astype(F32)
    copy.wait()
    n, factor = row_norm(own[...].astype(F32))
    back = factor * (
        e - jnp.mean(e, axis=1, keepdims=True) - n * jnp.mean(e * n, axis=1, keepdims=True)
    )
    out[...] = (middle_grad[...] + back).astype(BF)


def input_gradient(flags, terms, tokens, gain, middle_grad):
    return pl.pallas_call(
        input_gradient_kernel,
        out_shape=jax.ShapeDtypeStruct(middle_grad.shape, BF),
        in_specs=[smem()] + [vmem()] * 3 + [anywhere()] + [vmem()] * 2,
        out_specs=vmem(),
        scratch_shapes=[pltpu.VMEM(middle_grad.shape, BF), pltpu.SemaphoreType.DMA],
        compiler_params=params(),
        cost_estimate=cost(4500000000, 13500000),
        name="input_gradient",
    )(flags, *terms, tokens, gain, middle_grad)


def body(
    tokens,
    w_query,
    w_key,
    w_value,
    w_output,
    gain_attn,
    gain_inner,
    gain_ffn,
    w_expand,
    w_reduce,
    gain_hidden,
    cotangent,
    seq_length,
    seq_group,
):
    n_batch, n_own = lax.axis_size("batch"), lax.axis_size("heads")
    n_all = n_batch * n_own
    mine = lax.axis_index("heads")
    quarter = cotangent.shape[0]
    width = tokens.shape[1]
    local = w_query.shape[1]
    n_heads = local // HD

    def swap(value, bit):
        return lax.ppermute(value, AXES, [(i, i ^ bit) for i in range(n_all)])

    is_long = jnp.any((seq_group == lax.axis_index("batch")) & (seq_length > SHORT))
    flags = jnp.stack([is_long.astype(jnp.int32), mine.astype(jnp.int32)])
    far = [1 << b for b in range(3, n_all.bit_length() - 1)]
    near = (2, 4, 6)

    def parts(value, offsets):
        return [value] + [swap(value, off) for off in offsets]

    def around(value, offsets):
        return jnp.concatenate(parts(value, offsets), axis=0)

    def far_steps(value):
        for bit in reversed(far):
            value = around(value, (bit,))
            yield value

    def add(values):
        return sum(v.astype(F32) for v in values)

    phase = lax.optimization_barrier

    def sum_begin(value):
        rows = value.shape[0]
        value = lax.all_to_all(value, "batch", 0, 0, tiled=True)
        return value.reshape(n_batch, rows // n_batch, width)

    def sum_middle(value):
        return jnp.sum(value.astype(F32), axis=0)

    def sum_end(share):
        share = jnp.broadcast_to(share.astype(BF)[None], (n_batch,) + share.shape)
        return lax.all_to_all(share, "batch", 0, 0, tiled=True)

    def last(steps):
        *_, value = steps
        return value

    w_t = jnp.concatenate([w_query.T, w_key.T, w_value.T], axis=0)
    w_reduce_scaled = (w_reduce.astype(F32) * gain_hidden.astype(F32)[:, None]).astype(BF)
    w_output_scaled = (w_output.astype(F32) * gain_inner.astype(F32)[:, None]).astype(BF)
    gain_attn_row = gain_attn[None, :]

    if len(far) == 2:
        expand_far = parts(w_expand, (far[1], far[0], far[0] | far[1]))
    else:
        expand_far = [last(far_steps(w_expand))]
    reduced = w_reduce_scaled
    for bit in far[:0:-1]:
        reduced = parts(jnp.concatenate(reduced) if isinstance(reduced, list) else reduced, (bit,))
    w_out_y = swap(w_output_scaled, 2)
    cot_came = swap(cotangent, 1)
    pre, qkv = project(tokens, w_t, gain_attn_row, [])
    expand_far, reduced, w_out_y, pre, qkv = phase((expand_far, reduced, w_out_y, pre, qkv))

    expand = parts(jnp.concatenate(expand_far), near)
    reduced = parts(jnp.concatenate(reduced), (far[0],))
    w_out_c = swap(jnp.stack([w_output_scaled, w_out_y]), 1)
    lse, *pieces = attend(flags, qkv, n_own, [])
    expand, reduced, w_out_c, lse, pieces = phase((expand, reduced, w_out_c, lse, pieces))

    att = [pieces[0]] + [swap(pieces[k], k) for k in range(1, n_own)]
    expand = jnp.concatenate(expand)
    expand = [expand, swap(expand, 1)]
    reduced = jnp.concatenate(reduced)
    reduced = [reduced[: reduced.shape[0] // 2], reduced[reduced.shape[0] // 2 :]]
    first = [swap(reduced[0], 4), swap(reduced[1], 2)]
    w_out = [w_output_scaled, w_out_c[0], w_out_y, w_out_c[1]]
    att, expand, reduced, first, w_out, cot_came = phase(
        (att, expand, reduced, first, w_out, cot_came)
    )

    def stacked(parts):
        starts = [sum(p.shape[0] for p in parts[:i]) for i in range(len(parts))]
        return [(i, 0, start, p.shape[0]) for i, (start, p) in enumerate(zip(starts, parts))]

    places = stacked(expand)
    second = [
        swap(jnp.stack([reduced[0], first[0]]), 2),
        swap(jnp.stack([reduced[1], first[1]]), 4),
    ]
    *posts, slope, factors, middle, mid_low, inner_t = expand_ffn(
        flags, att, w_out, tokens, gain_ffn[None, :], expand, places
    )
    reduced, first, second, posts, slope, factors, middle, mid_low, inner_t = phase(
        (reduced, first, second, posts, slope, factors, middle, mid_low, inner_t)
    )

    (own_a, own_b), (x_a, y_b), ((y_a, xy_a), (x_b, xy_b)) = reduced, first, second
    reduced = jnp.concatenate([own_a, own_b, y_a, y_b, x_a, x_b, xy_a, xy_b])
    reduced = [reduced, swap(reduced, 1)]
    reduced, posts = phase((reduced, posts))

    post_came, mid_came = swap(posts[1], 1), swap(mid_low, 1)
    output, *hidden_grads = reduce_ffn(
        posts, slope, factors, middle, cotangent, reduced, stacked(reduced)
    )
    d_reduce = outer(posts[0], post_came, cotangent, cot_came)
    output, hidden_grads, d_reduce, mid_came = phase((output, hidden_grads, d_reduce, mid_came))

    part_r = swap(d_reduce[2], 4)
    grad_came = swap(hidden_grads[1], 1)
    middle_grad, ffn_sum, d_sent, d_kept, *att_grads = middle_back(
        att, w_out, hidden_grads, middle, cotangent, inner_t, gain_ffn[None, :], expand, places
    )
    part_r, grad_came, d_reduce, middle_grad, ffn_sum, d_sent, d_kept, att_grads = phase(
        (part_r, grad_came, d_reduce, middle_grad, ffn_sum, d_sent, d_kept, att_grads)
    )

    grads = [att_grads[0]] + [swap(att_grads[k], k) for k in range(1, n_own)]
    more_r = swap(d_reduce[3], 4)
    d_came = swap(d_sent, 1)
    d_last = swap(add((d_kept[1], d_came[1])).astype(BF), 2)
    d_expand = outer(hidden_grads[0], grad_came, mid_low, mid_came)
    d_own = (d_kept[0], d_came[0], d_last)
    more_r, grads, d_expand, d_own = phase((more_r, grads, d_expand, d_own))

    back = partial(attend_back, flags, qkv)

    def far_sum(value, bit):
        value = value.reshape(2, -1, width)
        return value[0], swap(value[1].astype(BF), bit)

    part_e = swap(d_expand[2], 4)
    came_r = swap(add((d_reduce[1], more_r)).astype(BF), 2)
    back_0 = back(0, lse, pre, w_t, pieces, grads, d_own)
    back_0, d_reduce, part_r, came_r, part_e, d_expand, grads = phase(
        (back_0, d_reduce, part_r, came_r, part_e, d_expand, grads)
    )

    share_0 = sum_begin(back_0[1])
    d_reduce = far_sum(add((d_reduce[0], part_r, came_r)), far[0])
    more_e = swap(d_expand[3], 4)
    back_1 = back(1, lse, pre, w_t, pieces, grads)
    back_1, part_e, more_e, d_expand, d_reduce, share_0, grads = phase(
        (back_1, part_e, more_e, d_expand, d_reduce, share_0, grads)
    )

    batch_bits = [1 << b for b in range(n_batch.bit_length() - 1)][::-1]

    def gather_step(value, bit):
        return value, swap(value, bit * n_own)

    def joined(pair, bit):
        axis = batch_bits.index(bit)
        mine_first = (lax.axis_index("batch") & bit) == 0
        return jnp.where(
            mine_first, jnp.concatenate(pair, axis), jnp.concatenate(pair[::-1], axis)
        )

    came_e = swap(add((d_expand[1], more_e)).astype(BF), 2)
    for bit in far[1:]:
        d_reduce = far_sum(add(d_reduce), bit)
    share_0 = sum_middle(share_0).astype(BF)
    share_0 = gather_step(share_0.reshape((1,) * len(batch_bits) + share_0.shape), batch_bits[0])
    earlier = (back_0[0], back_1[0])
    back_2 = back(2, lse, pre, w_t, pieces, grads, d_before=back_1[1], earlier=earlier)
    back_2, came_e, d_reduce, share_0 = phase((back_2, came_e, d_reduce, share_0))

    share_1 = sum_begin(back_2[1])
    sent, kept = back_2[3:]
    came = swap(sent, 1)
    second = swap(add((kept[1], came[1])).astype(BF), 2)
    small = jnp.sum(jnp.stack([back_0[2] + back_1[2] + back_2[2], ffn_sum]), axis=1)
    small = small + swap(small, 1)
    small = small + swap(small, 2)
    d_expand = far_sum(add((d_expand[0], part_e, came_e)), far[0])
    d_reduce = add(d_reduce)
    g_hidden = jnp.sum(d_reduce * w_reduce.astype(F32), axis=1)
    d_reduce = d_reduce * gain_hidden.astype(F32)[:, None]
    share_1, small, came, d_reduce, g_hidden = phase((share_1, small, came, d_reduce, g_hidden))

    share_1 = sum_middle(share_1)
    count = share_1.shape[0]
    total_1 = sum_end(jnp.concatenate([share_1, small], axis=0))
    for bit, later in zip(batch_bits, batch_bits[1:]):
        share_0 = gather_step(joined(share_0, bit), later)
    for bit in far[1:]:
        d_expand = far_sum(add(d_expand), bit)
    grad_tokens = input_gradient(
        flags, (kept[0], came[0], second), tokens, gain_attn_row, middle_grad
    )
    total_1, share_0, d_expand = phase((total_1, share_0, d_expand))

    d_expand = add(d_expand)
    total_0 = joined(share_0, batch_bits[-1]).astype(F32).reshape(-1, width)
    total_1 = total_1.astype(F32)
    small = jnp.sum(total_1[:, count:], axis=0)
    total_1 = total_1[:, :count].reshape(-1, width)
    totals = [total_0, total_1[: 3 * HD], total_1[3 * HD :]]
    def weight_grad(place):
        at = slice(place * HD, (place + 1) * HD)
        return jnp.concatenate([t[at] for t in totals], axis=0).T

    g_out = totals[0][3 * HD :]
    return (
        output,
        grad_tokens,
        weight_grad(0),
        weight_grad(1),
        weight_grad(2),
        g_out * gain_inner.astype(F32)[:, None],
        small[0] / gain_attn.astype(F32),
        jnp.sum(g_out * w_output.astype(F32), axis=1),
        small[1],
        d_expand,
        d_reduce,
        g_hidden,
    )


def solution(mesh):
    both = P(AXES, None)
    return jax.shard_map(
        body,
        mesh=mesh,
        in_specs=(
            P("batch", None),
            P(None, "heads"),
            P(None, "heads"),
            P(None, "heads"),
            P("heads", None),
            P(),
            P("heads"),
            P(),
            both,
            both,
            P(AXES),
            both,
            P(),
            P(),
        ),
        out_specs=(
            both,
            both,
            P(None, "heads"),
            P(None, "heads"),
            P(None, "heads"),
            P("heads", None),
            P(),
            P("heads"),
            P(),
            both,
            both,
            P(AXES),
        ),
        check_vma=False,
    )
```

```python
from functools import partial

import jax
import jax.numpy as jnp
from jax import lax
from jax.experimental import pallas as pl
from jax.experimental.pallas import tpu as pltpu
from jax.sharding import PartitionSpec as P

HD = 64
SHORT = 512
EPSILON = 1e-05
MASKED = -1e30
AXES = ("batch", "heads")
BF = jnp.bfloat16
F32 = jnp.float32
VMEM_LIMIT = 60 * 1024 * 1024


def dot(left, right, left_dim, right_dim):
    return lax.dot_general(
        left, right, (((left_dim,), (right_dim,)), ((), ())), preferred_element_type=F32
    )


def params(limit=VMEM_LIMIT):
    return pltpu.CompilerParams(vmem_limit_bytes=limit)


def vmem():
    return pl.BlockSpec(memory_space=pltpu.VMEM)


def smem():
    return pl.BlockSpec(memory_space=pltpu.SMEM)


def anywhere():
    return pl.BlockSpec(memory_space=pl.ANY)


def cost(flops, moved, special=0):
    return pl.CostEstimate(flops=flops, bytes_accessed=moved, transcendentals=special)


def project_kernel(n_after, tokens, w_t, gain, *rest):
    pre, qkv = rest[n_after:]
    rows = tokens.shape[0]
    local = w_t.shape[0] // 3
    gain_row = gain[...].astype(F32)
    for block in range(rows // SHORT):
        at = slice(block * SHORT, (block + 1) * SHORT)
        low = (row_norm(tokens[at, :].astype(F32))[0] * gain_row).astype(BF)
        pre[at, :] = low
        product = dot(w_t[...], low, 1, 1)
        qkv[0:local, at] = (product[0:local] * HD ** (-0.5)).astype(BF)
        qkv[local:, at] = product[local:].astype(BF)


def project(tokens, w_t, gain, after):
    rows, width = tokens.shape
    return pl.pallas_call(
        partial(project_kernel, len(after)),
        out_shape=(
            jax.ShapeDtypeStruct((rows, width), BF),
            jax.ShapeDtypeStruct((w_t.shape[0], rows), BF),
        ),
        in_specs=[vmem()] * 3 + [anywhere()] * len(after),
        out_specs=[vmem()] * 2,
        compiler_params=params(),
        cost_estimate=cost(7000000000, 21000000),
        name="project",
    )(tokens, w_t, gain, *after)


def column_max(values):
    return jnp.max(values.reshape(values.shape[0] // 8, 8, SHORT), axis=0)


def column_sum(values):
    return jnp.sum(values.reshape(values.shape[0] // 8, 8, SHORT), axis=0)


def attend_kernel(n_after, n_out, flags, qkv, *rest):
    lse, *outs, att = rest[n_after:]
    local = qkv.shape[0] // 3
    heads = local // HD
    blocks = qkv.shape[1] // SHORT
    is_long, mine = flags[0], flags[1]
    key_place = lax.broadcasted_iota(jnp.int32, (SHORT, SHORT), 0)
    query_place = lax.broadcasted_iota(jnp.int32, (SHORT, SHORT), 1)

    def run_path(long_path):
        def one_head(head, unused):
            at = pl.ds(pl.multiple_of(head * HD, HD), HD)
            k_at = pl.ds(pl.multiple_of(local + head * HD, HD), HD)
            v_at = pl.ds(pl.multiple_of(2 * local + head * HD, HD), HD)
            for block in range(blocks):
                q_t = qkv[at, block * SHORT : (block + 1) * SHORT]
                keys = [
                    slice(index * SHORT, (index + 1) * SHORT)
                    for index in range(0 if long_path else block, block + 1)
                ]
                parts = [dot(qkv[k_at, key], q_t, 0, 0) for key in keys]
                parts[-1] = jnp.where(key_place <= query_place, parts[-1], MASKED)
                largest = column_max(parts[0])
                for s in parts[1:]:
                    largest = jnp.maximum(largest, column_max(s))
                top = jnp.max(largest, axis=0, keepdims=True)
                total, out = 0.0, 0.0
                for key, s in zip(keys, parts):
                    p = jnp.exp(s - top)
                    total = total + column_sum(p)
                    out = out + dot(qkv[v_at, key], p.astype(BF), 1, 0)
                total = jnp.sum(total, axis=0, keepdims=True)
                att[block, at, :] = (out / total).astype(BF)
                lse[head, block] = jnp.broadcast_to(top + jnp.log(total), (8, SHORT))
            return unused

        lax.fori_loop(0, heads, one_head, 0)

    pl.when(is_long > 0)(lambda: run_path(True))
    pl.when(is_long == 0)(lambda: run_path(False))
    for place in range(n_out):
        outs[place][...] = att[mine ^ place]


def attend(flags, qkv, n_out, after):
    rows = qkv.shape[1]
    blocks = rows // SHORT
    local = qkv.shape[0] // 3
    return pl.pallas_call(
        partial(attend_kernel, len(after), n_out),
        out_shape=(jax.ShapeDtypeStruct((local // HD, blocks, 8, SHORT), F32),)
        + (jax.ShapeDtypeStruct((local, SHORT), BF),) * n_out,
        in_specs=[smem(), vmem()] + [anywhere()] * len(after),
        out_specs=[vmem()] * (1 + n_out),
        scratch_shapes=[pltpu.VMEM((blocks, local, SHORT), BF)],
        compiler_params=params(),
        cost_estimate=cost(15000000000, 45000000),
        name="attend",
    )(flags, qkv, *after)


def attend_back_kernel(n_own, n_terms, n_earlier, *refs):
    flags, q_all, k_all, v_all, lse, pre, w_q, w_k, w_v = refs[:9]
    att, grads, rest = refs[9 : 9 + n_own], refs[9 + n_own : 9 + 2 * n_own], refs[9 + 2 * n_own :]
    terms, rest = rest[:n_terms], rest[n_terms:]
    if n_earlier:
        w_t, d_before, rest = rest[0], rest[1], rest[2:]
        earlier, rest = rest[:n_earlier], rest[n_earlier:]
    d_qkv, d_weight, attn_sum, *rest = rest
    if n_earlier:
        sent, kept, *rest = rest
    ag, delta = rest
    rows, width = pre.shape
    blocks = rows // SHORT
    is_long, mine = flags[0], flags[1]

    for place in range(n_own):
        grad = grads[place][...]
        ag[mine ^ place] = grad
        product = grad.astype(F32) * att[place][...].astype(F32)
        delta[mine ^ place] = jnp.broadcast_to(jnp.sum(product, axis=0, keepdims=True), (8, SHORT))

    key_place = lax.broadcasted_iota(jnp.int32, (SHORT, SHORT), 0)
    query_place = lax.broadcasted_iota(jnp.int32, (SHORT, SHORT), 1)

    def run_path(long_path):
        d_q = [None] * blocks
        for block in range(blocks):
            k_cols = slice(block * SHORT, (block + 1) * SHORT)
            k_t = k_all[:, k_cols]
            v_t = v_all[:, k_cols]
            d_k = d_v = None
            for index in range(block, blocks if long_path else block + 1):
                q_t = q_all[:, index * SHORT : (index + 1) * SHORT]
                grad = ag[index]
                p = jnp.exp(dot(k_t, q_t, 0, 0) - lse[0, index][0:1])
                if index == block:
                    p = jnp.where(key_place <= query_place, p, 0.0)
                d_p = dot(v_t, grad, 0, 0)
                d_s = (p * (d_p - delta[index][0:1])).astype(BF)
                p = p.astype(BF)
                add = dot(k_t, d_s, 1, 0)
                d_q[index] = add if d_q[index] is None else d_q[index] + add
                add = dot(q_t, d_s, 1, 1)
                d_k = add if d_k is None else d_k + add
                add = dot(grad, p, 1, 1)
                d_v = add if d_v is None else d_v + add
            d_qkv[HD : 2 * HD, k_cols] = d_k.astype(BF)
            d_qkv[2 * HD :, k_cols] = d_v.astype(BF)
        for block in range(blocks):
            d_qkv[0:HD, block * SHORT : (block + 1) * SHORT] = (d_q[block] * HD ** (-0.5)).astype(BF)

    pl.when(is_long > 0)(lambda: run_path(True))
    pl.when(is_long == 0)(lambda: run_path(False))
    product = dot(d_qkv[...], pre[...], 1, 0)
    start = d_before.shape[0] if n_earlier else 0
    d_weight[start : start + 3 * HD, :] = product.astype(BF)
    if n_earlier:
        d_weight[0:start, :] = d_before[...]
    if n_terms:
        d_weight[3 * HD :, :] = sum(t[...].astype(F32) for t in terms).astype(BF)
    cross = jnp.zeros((8, width), F32)
    for place, weight in enumerate((w_q, w_k, w_v)):
        part = product[place * HD : (place + 1) * HD] * weight[...].astype(F32)
        cross = cross + jnp.sum(part.reshape(HD // 8, 8, width), axis=0)
    attn_sum[...] = cross
    if n_earlier:
        for place in range(n_own):
            cols = pl.ds(pl.multiple_of((mine ^ place) * SHORT, SHORT), SHORT)
            joined = [d[i * HD : (i + 1) * HD, cols] for i in range(3) for d in (*earlier, d_qkv)]
            grad = dot(w_t[...], jnp.concatenate(joined, axis=0), 0, 0)
            target = sent if place % 2 else kept
            target[place // 2] = grad.astype(BF)


def attend_back(flags, qkv, head, lse, pre, w_t, att, grads, terms=(), d_before=None, earlier=()):
    rows, width = pre.shape
    blocks = rows // SHORT
    heads = qkv.shape[0] // (3 * HD)
    n_own = len(att)

    def part(place, columns):
        return pl.BlockSpec((HD, columns), lambda i, at=place: (at, 0))

    def whole(struct):
        return pl.BlockSpec(struct.shape, lambda i, n=len(struct.shape): (0,) * n)

    more = [w_t, d_before, *earlier] if earlier else []
    weight_rows = 3 * HD + sum(v.shape[0] for v in [*terms[:1], *more[1:2]])
    outs = (
        jax.ShapeDtypeStruct((3 * HD, rows), BF),
        jax.ShapeDtypeStruct((weight_rows, width), BF),
        jax.ShapeDtypeStruct((8, width), F32),
    )
    if earlier:
        outs += (jax.ShapeDtypeStruct((n_own // 2, width, SHORT), BF),) * 2
    return pl.pallas_call(
        partial(attend_back_kernel, n_own, len(terms), len(earlier)),
        grid=(1,),
        out_shape=outs,
        in_specs=[smem()]
        + [part(place * heads + head, rows) for place in range(3)]
        + [pl.BlockSpec((1,) + lse.shape[1:], lambda i: (head, 0, 0, 0)), whole(pre)]
        + [part(place * heads + head, width) for place in range(3)]
        + [part(head, SHORT)] * (2 * n_own)
        + [whole(v) for v in [*terms, *more]],
        out_specs=[whole(o) for o in outs],
        scratch_shapes=[
            pltpu.VMEM((blocks, HD, SHORT), BF),
            pltpu.VMEM((blocks, 8, SHORT), F32),
        ],
        compiler_params=params(),
        cost_estimate=cost(11_500_000_000, 34_500_000),
        name="attend_back",
    )(flags, qkv, qkv, qkv, lse, pre, w_t, w_t, w_t, *att, *grads, *terms, *more)


def gelu_parts(h):
    phi = jnp.exp(h * h * (-0.5)) * 0.3989422804014327
    big = 0.5 * lax.erf(h * 0.7071067811865476) + 0.5
    return h * big, big + h * phi


def inner_stats(att, width):
    total = sum(jnp.sum(piece[...].astype(F32), axis=0, keepdims=True) for piece in att)
    average = total / width
    square = 0.0
    for piece in att:
        centred = piece[...].astype(F32) - average
        square = square + jnp.sum(centred * centred, axis=0, keepdims=True)
    return average, lax.rsqrt(square / width + EPSILON)


def row_norm(x):
    centred = x - jnp.mean(x, axis=1, keepdims=True)
    factor = lax.rsqrt(jnp.mean(centred * centred, axis=1, keepdims=True) + EPSILON)
    return centred * factor, factor


def fetch(pieces, places, target, sems):
    copies = [
        pltpu.make_async_copy(
            pieces[number].at[pl.ds(start, rows), :], target.at[pl.ds(to, rows), :], sems.at[i]
        )
        for i, (number, start, to, rows) in enumerate(places)
    ]
    for copy in copies:
        copy.start()

    def wait():
        for copy in copies:
            copy.wait()

    return wait


def outer_kernel(left, left_came, right, right_came, over_2, over_4, own, first, second):
    size = own.shape[0]
    half = size // 2
    places = [
        ((own, 0), (own, half)),
        ((over_2, 0), (second, 0)),
        ((first, 0), (over_4, 0)),
        ((over_2, half), (over_4, half)),
    ]
    for number, pair in enumerate(places):
        at = slice(number * size, (number + 1) * size)
        product = dot(left[:, at], right[...], 0, 0) + dot(left_came[:, at], right_came[...], 0, 0)
        for part, (out, start) in enumerate(pair):
            out[start : start + half, :] = product[part * half : (part + 1) * half].astype(BF)


def outer(left, left_came, right, right_came):
    size, width = left.shape[1] // 4, right.shape[1]
    whole, half = (jax.ShapeDtypeStruct((rows, width), BF) for rows in (size, size // 2))
    return pl.pallas_call(
        outer_kernel,
        out_shape=(whole, whole, whole, half, half),
        in_specs=[vmem()] * 4,
        out_specs=[vmem()] * 5,
        compiler_params=params(),
        cost_estimate=cost(5_000_000_000, 15_000_000),
        name="outer",
    )(left, left_came, right, right_came)


def expand_kernel(n_own, n_piece, places, flags, *refs):
    att, w_out = refs[:n_own], refs[n_own : 2 * n_own]
    tokens, gain_ffn = refs[2 * n_own : 2 * n_own + 2]
    pieces, rest = refs[2 * n_own + 2 : 2 * n_own + 2 + n_piece], refs[2 * n_own + 2 + n_piece :]
    *posts, slope, factors, middle, mid_low, inner_t, weight, act, own, sems, own_sem = rest
    rows, width = middle.shape
    start = pl.multiple_of(flags[1] * rows, rows)
    own_copy = pltpu.make_async_copy(tokens.at[pl.ds(start, rows), :], own, own_sem)
    own_copy.start()
    local = att[0].shape[0]
    hidden = weight.shape[0]
    chunk = width
    wait = fetch(pieces, places, weight, sems)

    average, inner_factor = inner_stats(att, width)
    for place, piece in enumerate(att):
        hat = (piece[...].astype(F32) - average) * inner_factor
        inner_t[place * local : (place + 1) * local, :] = hat.astype(BF)
    branch = dot(inner_t[0:local, :], w_out[0][...], 0, 0)
    for place in range(1, n_own):
        branch += dot(inner_t[place * local : (place + 1) * local, :], w_out[place][...], 0, 0)
    own_copy.wait()
    total = own[...].astype(F32) + branch
    middle[...] = total
    mid_low[...] = (row_norm(total)[0] * gain_ffn[...].astype(F32)).astype(BF)
    wait()
    for start in range(0, hidden, chunk):
        to = slice(start, start + chunk)
        a, s = gelu_parts(dot(mid_low[...], weight[to, :], 1, 1))
        act[:, to] = a
        slope[:, to] = s.astype(BF)
    n, factor = row_norm(act[...])
    for number, post in enumerate(posts):
        post[...] = n[:, number * hidden // 2 : (number + 1) * hidden // 2].astype(BF)
    factors[...] = jnp.broadcast_to(factor, (rows, 128))


def expand_ffn(flags, att, w_out, tokens, gain_ffn, expand, places):
    rows, width = att[0].shape[1], tokens.shape[1]
    hidden = sum(e.shape[0] for e in expand)
    n_own = len(att)
    local = att[0].shape[0]
    return pl.pallas_call(
        partial(expand_kernel, n_own, len(expand), places),
        out_shape=(
            jax.ShapeDtypeStruct((rows, hidden // 2), BF),
            jax.ShapeDtypeStruct((rows, hidden // 2), BF),
            jax.ShapeDtypeStruct((rows, hidden), BF),
            jax.ShapeDtypeStruct((rows, 128), F32),
            jax.ShapeDtypeStruct((rows, width), F32),
            jax.ShapeDtypeStruct((rows, width), BF),
            jax.ShapeDtypeStruct((n_own * local, rows), BF),
        ),
        in_specs=[smem()]
        + [vmem()] * (2 * n_own)
        + [anywhere(), vmem()]
        + [anywhere()] * len(expand),
        out_specs=[vmem()] * 7,
        scratch_shapes=[
            pltpu.VMEM((hidden, width), BF),
            pltpu.VMEM((rows, hidden), F32),
            pltpu.VMEM((rows, width), BF),
            pltpu.SemaphoreType.DMA((len(places),)),
            pltpu.SemaphoreType.DMA,
        ],
        compiler_params=params(),
        cost_estimate=cost(12000000000, 36000000),
        name="expand_ffn",
    )(flags, *att, *w_out, tokens, gain_ffn, *expand)


def reduce_kernel(n_piece, places, *refs):
    posts, (slope, factors, middle, cotangent), rest = refs[:2], refs[2:6], refs[6:]
    pieces, (output, *grads, weight, d_post, sems) = rest[:n_piece], rest[n_piece:]
    hidden, width = weight.shape
    half = hidden // 2
    fetch(pieces, places, weight, sems)()
    total = middle[...]
    for start in range(0, hidden, width):
        at = slice(start % half, start % half + width)
        rows = slice(start, start + width)
        d_post[:, rows] = dot(cotangent[...], weight[rows, :], 1, 1)
        total = total + dot(posts[start // half][:, at], weight[rows, :], 1, 0)
    output[...] = total.astype(BF)
    mean_e, mean_en = 0.0, 0.0
    for number, post in enumerate(posts):
        e = d_post[:, number * half : (number + 1) * half]
        mean_e = mean_e + jnp.sum(e, axis=1, keepdims=True) / hidden
        mean_en = mean_en + jnp.sum(e * post[...].astype(F32), axis=1, keepdims=True) / hidden
    for number, (post, grad) in enumerate(zip(posts, grads)):
        at = slice(number * half, (number + 1) * half)
        back = d_post[:, at] - mean_e - post[...].astype(F32) * mean_en
        grad[...] = (factors[:, 0:1] * back * slope[:, at].astype(F32)).astype(BF)


def reduce_ffn(posts, slope, factors, middle, cotangent, reduced, places):
    rows, width = middle.shape
    hidden = slope.shape[1]
    return pl.pallas_call(
        partial(reduce_kernel, len(reduced), places),
        out_shape=(
            jax.ShapeDtypeStruct((rows, width), BF),
            jax.ShapeDtypeStruct((rows, hidden // 2), BF),
            jax.ShapeDtypeStruct((rows, hidden // 2), BF),
        ),
        in_specs=[vmem()] * 6 + [anywhere()] * len(reduced),
        out_specs=[vmem()] * 3,
        scratch_shapes=[
            pltpu.VMEM((hidden, width), BF),
            pltpu.VMEM((rows, hidden), F32),
            pltpu.SemaphoreType.DMA((len(places),)),
        ],
        compiler_params=params(),
        cost_estimate=cost(15_000_000_000, 45_000_000),
        name="reduce_ffn",
    )(*posts, slope, factors, middle, cotangent, *reduced)


def middle_kernel(n_own, n_piece, places, *refs):
    att, w_out = refs[:n_own], refs[n_own : 2 * n_own]
    *hidden_grads, middle, cotangent, inner_t, gain_ffn = refs[2 * n_own : 2 * n_own + 6]
    rest = refs[2 * n_own + 6 :]
    pieces, rest = rest[:n_piece], rest[n_piece:]
    middle_grad, ffn_sum, sent, kept = rest[:4]
    grads = rest[4 : 4 + n_own]
    weight, branch_grad, e_buf, sems = rest[4 + n_own :]
    rows, width = middle.shape
    local = att[0].shape[0]
    half = weight.shape[0] // 2
    gain_row = gain_ffn[...].astype(F32)
    wait = fetch(pieces, places, weight, sems)
    n, factor = row_norm(middle[...])
    average, inner_factor = inner_stats(att, width)
    wait()
    grad = dot(hidden_grads[0][...], weight[0:half, :], 1, 0)
    grad = grad + dot(hidden_grads[1][...], weight[half:, :], 1, 0)
    ffn_sum[...] = jnp.sum((grad * n).reshape(rows // 8, 8, width), axis=0)
    e = grad * gain_row
    back = factor * (
        e - jnp.mean(e, axis=1, keepdims=True) - n * jnp.mean(e * n, axis=1, keepdims=True)
    )
    full = cotangent[...].astype(F32) + back
    middle_grad[...] = full
    branch_grad[...] = full.astype(BF)

    grad_sum = jnp.zeros((1, rows), F32)
    cross_sum = jnp.zeros((1, rows), F32)
    for place in range(n_own):
        e = dot(w_out[place][...], branch_grad[...], 1, 1)
        e_buf[place] = e
        grad_sum = grad_sum + jnp.sum(e, axis=0, keepdims=True)
        hat = (att[place][...].astype(F32) - average) * inner_factor
        cross_sum = cross_sum + jnp.sum(e * hat, axis=0, keepdims=True)
    for place in range(n_own):
        hat = (att[place][...].astype(F32) - average) * inner_factor
        grad = inner_factor * (e_buf[place] - grad_sum / width - hat * (cross_sum / width))
        grads[place][...] = grad.astype(BF)
        target = sent if place % 2 else kept
        at = slice(place * local, (place + 1) * local)
        target[place // 2] = dot(inner_t[at, :], branch_grad[...], 1, 0).astype(BF)


def middle_back(att, w_out, hidden_grads, middle, cotangent, inner_t, gain_ffn, expand, places):
    rows, width = middle.shape
    hidden = 2 * hidden_grads[0].shape[1]
    n_own = len(att)
    local = att[0].shape[0]
    return pl.pallas_call(
        partial(middle_kernel, n_own, len(expand), places),
        out_shape=(
            jax.ShapeDtypeStruct((rows, width), F32),
            jax.ShapeDtypeStruct((8, width), F32),
            jax.ShapeDtypeStruct((n_own // 2, local, width), BF),
            jax.ShapeDtypeStruct((n_own // 2, local, width), BF),
        )
        + (jax.ShapeDtypeStruct((local, rows), BF),) * n_own,
        in_specs=[vmem()] * (2 * n_own + 6) + [anywhere()] * len(expand),
        out_specs=[vmem()] * (4 + n_own),
        scratch_shapes=[
            pltpu.VMEM((hidden, width), BF),
            pltpu.VMEM((rows, width), BF),
            pltpu.VMEM((n_own, local, rows), F32),
            pltpu.SemaphoreType.DMA((len(places),)),
        ],
        compiler_params=params(),
        cost_estimate=cost(12_500_000_000, 37_500_000),
        name="middle_back",
    )(*att, *w_out, *hidden_grads, middle, cotangent, inner_t, gain_ffn, *expand)


def input_gradient_kernel(
    flags, kept, came, first, second, tokens, gain, middle_grad, out, own, sem
):
    rows = out.shape[0]
    start = pl.multiple_of(flags[1] * rows, rows)
    copy = pltpu.make_async_copy(tokens.at[pl.ds(start, rows), :], own, sem)
    copy.start()
    last = jnp.concatenate([first[...], second[...]], axis=0)
    total = kept[0].astype(F32) + came[0].astype(F32) + last.astype(F32)
    e = total.T * gain[...].astype(F32)
    copy.wait()
    n, factor = row_norm(own[...].astype(F32))
    back = factor * (
        e - jnp.mean(e, axis=1, keepdims=True) - n * jnp.mean(e * n, axis=1, keepdims=True)
    )
    out[...] = (middle_grad[...] + back).astype(BF)


def input_gradient(flags, terms, tokens, gain, middle_grad):
    kept, came, first, second = terms
    block = pl.BlockSpec((1,) + kept.shape[1:], lambda i: (0, 0, 0))

    def whole(v):
        return pl.BlockSpec(v.shape, lambda i: (0, 0))

    return pl.pallas_call(
        input_gradient_kernel,
        grid=(1,),
        out_shape=jax.ShapeDtypeStruct(middle_grad.shape, BF),
        in_specs=[smem(), block, block, whole(first), whole(second), anywhere()]
        + [whole(gain), whole(middle_grad)],
        out_specs=whole(middle_grad),
        scratch_shapes=[pltpu.VMEM(middle_grad.shape, BF), pltpu.SemaphoreType.DMA],
        compiler_params=params(),
        cost_estimate=cost(4500000000, 13500000),
        name="input_gradient",
    )(flags, *terms, tokens, gain, middle_grad)


def body(
    tokens,
    w_query,
    w_key,
    w_value,
    w_output,
    gain_attn,
    gain_inner,
    gain_ffn,
    w_expand,
    w_reduce,
    gain_hidden,
    cotangent,
    seq_length,
    seq_group,
):
    n_batch, n_own = lax.axis_size("batch"), lax.axis_size("heads")
    n_all = n_batch * n_own
    mine = lax.axis_index("heads")
    quarter = cotangent.shape[0]
    width = tokens.shape[1]
    local = w_query.shape[1]
    n_heads = local // HD

    def swap(value, bit):
        return lax.ppermute(value, AXES, [(i, i ^ bit) for i in range(n_all)])

    is_long = jnp.any((seq_group == lax.axis_index("batch")) & (seq_length > SHORT))
    flags = jnp.stack([is_long.astype(jnp.int32), mine.astype(jnp.int32)])
    far = [1 << b for b in range(3, n_all.bit_length() - 1)]
    near = (2, 4, 6)

    def parts(value, offsets):
        return [value] + [swap(value, off) for off in offsets]

    def around(value, offsets):
        return jnp.concatenate(parts(value, offsets), axis=0)

    def far_steps(value):
        for bit in reversed(far):
            value = around(value, (bit,))
            yield value

    def add(values):
        return sum(v.astype(F32) for v in values)

    phase = lax.optimization_barrier

    def sum_begin(value):
        rows = value.shape[0]
        value = lax.all_to_all(value, "batch", 0, 0, tiled=True)
        return value.reshape(n_batch, rows // n_batch, width)

    def sum_middle(value):
        return jnp.sum(value.astype(F32), axis=0)

    def sum_end(share):
        share = jnp.broadcast_to(share.astype(BF)[None], (n_batch,) + share.shape)
        return lax.all_to_all(share, "batch", 0, 0, tiled=True)

    def last(steps):
        *_, value = steps
        return value

    w_t = jnp.concatenate([w_query.T, w_key.T, w_value.T], axis=0)
    w_reduce_scaled = (w_reduce.astype(F32) * gain_hidden.astype(F32)[:, None]).astype(BF)
    w_output_scaled = (w_output.astype(F32) * gain_inner.astype(F32)[:, None]).astype(BF)
    gain_attn_row = gain_attn[None, :]

    if len(far) == 2:
        expand_far = parts(w_expand, (far[1], far[0], far[0] | far[1]))
    else:
        expand_far = [last(far_steps(w_expand))]
    reduced = w_reduce_scaled
    for bit in far[:0:-1]:
        reduced = parts(jnp.concatenate(reduced) if isinstance(reduced, list) else reduced, (bit,))
    w_out_y = swap(w_output_scaled, 2)
    cot_came = swap(cotangent, 1)
    pre, qkv = project(tokens, w_t, gain_attn_row, [])
    expand_far, reduced, w_out_y, pre, qkv = phase((expand_far, reduced, w_out_y, pre, qkv))

    expand = parts(jnp.concatenate(expand_far), near)
    reduced = parts(jnp.concatenate(reduced), (far[0],))
    w_out_c = swap(jnp.stack([w_output_scaled, w_out_y]), 1)
    lse, *pieces = attend(flags, qkv, n_own, [])
    expand, reduced, w_out_c, lse, pieces = phase((expand, reduced, w_out_c, lse, pieces))

    att = [pieces[0]] + [swap(pieces[k], k) for k in range(1, n_own)]
    expand, att[1] = phase((expand, att[1]))
    expand = jnp.concatenate(expand)
    expand = [expand, swap(expand, 1)]
    reduced = jnp.concatenate(reduced)
    half = reduced.shape[0] // 2
    first = [swap(reduced[:half], 4), swap(reduced[half:], 2)]
    w_out = [w_output_scaled, w_out_c[0], w_out_y, w_out_c[1]]
    att, expand, reduced, first, w_out, cot_came = phase(
        (att, expand, reduced, first, w_out, cot_came)
    )

    def stacked(parts):
        starts = [sum(p.shape[0] for p in parts[:i]) for i in range(len(parts))]
        return [(i, 0, start, p.shape[0]) for i, (start, p) in enumerate(zip(starts, parts))]

    places = stacked(expand)
    second = [
        swap(jnp.concatenate([reduced[:half], first[0]]), 2),
        swap(jnp.concatenate([reduced[half:], first[1]]), 4),
    ]
    *posts, slope, factors, middle, mid_low, inner_t = expand_ffn(
        flags, att, w_out, tokens, gain_ffn[None, :], expand, places
    )
    reduced, posts, slope, factors, middle, mid_low, inner_t = phase(
        ([reduced, *first, *second], posts, slope, factors, middle, mid_low, inner_t)
    )

    starts = [(0, 0, 0), (0, half, 1), (1, 0, 4), (2, 0, 3)]
    starts += [(3, 0, 2), (3, half, 6), (4, 0, 5), (4, half, 7)]
    reduce_places = [
        (number + core * 5, start, core * 8 * half + at * half, half)
        for core in range(2)
        for number, start, at in starts
    ]
    post_came = swap(posts[1], 1)
    reduced = reduced + [swap(r, 1) for r in reduced]
    d_reduce = outer(posts[0], post_came, cotangent, cot_came)
    reduced, posts, mid_low, d_reduce = phase((reduced, posts, mid_low, d_reduce))

    def near_begin(products):
        return swap(products[0], 2), swap(products[1], 4)

    def near_middle(products, came):
        half = came[0].shape[0] // 2
        terms = [add((p, c[half:])).astype(BF) for p, c in zip(products[3:], came)]
        return came, (swap(terms[0], 4), swap(terms[1], 2))

    def near_end(products, begun, came):
        half = came[0].shape[0]
        return [
            add((products[2][i * half : (i + 1) * half], b[:half], c))
            for i, (b, c) in enumerate(zip(begun, came))
        ]

    begun_r = near_begin(d_reduce)
    mid_came = swap(mid_low, 1)
    output, *hidden_grads = reduce_ffn(
        posts, slope, factors, middle, cotangent, reduced, reduce_places
    )
    output, hidden_grads, begun_r, d_reduce, mid_came = phase(
        (output, hidden_grads, begun_r, d_reduce, mid_came)
    )

    begun_r, came_r = near_middle(d_reduce, begun_r)
    grad_came = swap(hidden_grads[1], 1)
    middle_grad, ffn_sum, d_sent, d_kept, *att_grads = middle_back(
        att, w_out, hidden_grads, middle, cotangent, inner_t, gain_ffn[None, :], expand, places
    )
    came_r, grad_came, middle_grad, ffn_sum, d_sent, d_kept, att_grads = phase(
        (came_r, grad_came, middle_grad, ffn_sum, d_sent, d_kept, att_grads)
    )

    def far_sum(value, bit):
        return value[0], swap(value[1].astype(BF), bit)

    def halves(value):
        return value.reshape(2, -1, width)

    grads = [att_grads[0]] + [swap(att_grads[k], k) for k in range(1, n_own)]
    d_came = swap(d_sent, 1)
    d_came, mid_came, begun_r, came_r = phase((d_came, mid_came, begun_r, came_r))
    d_reduce = far_sum(near_end(d_reduce, begun_r, came_r), far[0])
    d_expand = outer(hidden_grads[0], grad_came, mid_low, mid_came)
    d_reduce, grads, d_expand, d_came = phase((d_reduce, grads, d_expand, d_came))

    back = partial(attend_back, flags, qkv)

    begun_e = near_begin(d_expand)
    for bit in far[1:]:
        d_reduce = far_sum(halves(add(d_reduce)), bit)
    d_last = swap(add((d_kept[1], d_came[1])).astype(BF), 2)
    back_0 = back(0, lse, pre, w_t, pieces, grads)
    back_0, d_reduce, begun_e, d_expand, d_last, grads = phase(
        (back_0, d_reduce, begun_e, d_expand, d_last, grads)
    )

    d_own = add((d_kept[0], d_came[0], d_last)).astype(BF)
    share_0 = sum_begin(jnp.concatenate([back_0[1], d_own]))
    begun_e, came_e = near_middle(d_expand, begun_e)
    back_1 = back(1, lse, pre, w_t, pieces, grads)
    back_1, came_e, share_0, grads = phase((back_1, came_e, share_0, grads))

    batch_bits = [1 << b for b in range(n_batch.bit_length() - 1)][::-1]

    def gather_step(value, bit):
        return value, swap(value, bit * n_own)

    def joined(pair, bit):
        axis = batch_bits.index(bit)
        mine_first = (lax.axis_index("batch") & bit) == 0
        return jnp.where(
            mine_first, jnp.concatenate(pair, axis), jnp.concatenate(pair[::-1], axis)
        )

    d_expand = near_end(d_expand, begun_e, came_e)
    if len(far) == 2:
        blocks = [v.astype(BF) for part in d_expand for v in halves(part)]
        offs = (far[1], far[0], far[0] | far[1])
        d_expand = [halves(d_expand[0])[0]] + [swap(b, o) for b, o in zip(blocks[1:], offs)]
    else:
        d_expand = far_sum(d_expand, far[0])
        for bit in far[1:]:
            d_expand = far_sum(halves(add(d_expand)), bit)
    share_0 = sum_middle(share_0).astype(BF)
    share_0 = gather_step(share_0.reshape((1,) * len(batch_bits) + share_0.shape), batch_bits[0])
    earlier = (back_0[0], back_1[0])
    back_2 = back(2, lse, pre, w_t, pieces, grads, d_before=back_1[1], earlier=earlier)
    back_2, d_expand, share_0 = phase((back_2, d_expand, share_0))

    share_1 = sum_begin(back_2[1])
    small = jnp.sum(jnp.stack([back_0[2] + back_1[2] + back_2[2], ffn_sum]), axis=1)
    small = small + swap(small, 1)
    small = small + swap(small, 2)
    sent, kept = back_2[3:]
    came = swap(sent, 1)
    came, kept, small = phase((came, kept, small))
    split = width // 2
    terms = [
        add((kept[1, at], came[1, at])).astype(BF)
        for at in (slice(0, split), slice(split, width))
    ]
    first = swap(terms[0], 2)
    for bit, later in zip(batch_bits[:-1], batch_bits[1:-1]):
        share_0 = gather_step(joined(share_0, bit), later)
    share_1, share_0, first, terms, d_expand = phase((share_1, share_0, first, terms, d_expand))

    second = [first, swap(terms[1], 2)]
    share_1 = sum_middle(share_1)
    count = share_1.shape[0]
    total_1 = sum_end(jnp.concatenate([share_1, small], axis=0))
    share_0 = gather_step(joined(share_0, batch_bits[-2]), batch_bits[-1])
    grad_tokens = input_gradient(
        flags, (kept, came, *second), tokens, gain_attn_row, middle_grad
    )
    grad_tokens, share_0, d_reduce, d_expand = phase((grad_tokens, share_0, d_reduce, d_expand))
    d_expand = add(d_expand)
    d_reduce = add(d_reduce)
    g_hidden = jnp.sum(d_reduce * w_reduce.astype(F32), axis=1)
    d_reduce = d_reduce * gain_hidden.astype(F32)[:, None]

    total_0 = joined(share_0, batch_bits[-1]).astype(F32).reshape(-1, width)
    total_1 = total_1.astype(F32)
    small = jnp.sum(total_1[:, count:], axis=0)
    total_1 = total_1[:, :count].reshape(-1, width)
    totals = [total_0, total_1[: 3 * HD], total_1[3 * HD :]]
    def weight_grad(place):
        at = slice(place * HD, (place + 1) * HD)
        return jnp.concatenate([t[at] for t in totals], axis=0).T

    g_out = totals[0][3 * HD :]
    return (
        output,
        grad_tokens,
        weight_grad(0),
        weight_grad(1),
        weight_grad(2),
        g_out * gain_inner.astype(F32)[:, None],
        small[0] / gain_attn.astype(F32),
        jnp.sum(g_out * w_output.astype(F32), axis=1),
        small[1],
        d_expand,
        d_reduce,
        g_hidden,
    )


def solution(mesh):
    both = P(AXES, None)
    return jax.shard_map(
        body,
        mesh=mesh,
        in_specs=(
            P("batch", None),
            P(None, "heads"),
            P(None, "heads"),
            P(None, "heads"),
            P("heads", None),
            P(),
            P("heads"),
            P(),
            both,
            both,
            P(AXES),
            both,
            P(),
            P(),
        ),
        out_specs=(
            both,
            both,
            P(None, "heads"),
            P(None, "heads"),
            P(None, "heads"),
            P("heads", None),
            P(),
            P("heads"),
            P(),
            both,
            both,
            P(AXES),
        ),
        check_vma=False,
    )
```

```python
from functools import partial

import jax
import jax.numpy as jnp
from jax import lax
from jax.experimental import pallas as pl
from jax.experimental.pallas import tpu as pltpu
from jax.sharding import PartitionSpec as P

HD = 64
SHORT = 512
EPSILON = 1e-05
MASKED = -1e30
AXES = ("batch", "heads")
BF = jnp.bfloat16
F32 = jnp.float32
VMEM_LIMIT = 60 * 1024 * 1024


def dot(left, right, left_dim, right_dim):
    return lax.dot_general(
        left, right, (((left_dim,), (right_dim,)), ((), ())), preferred_element_type=F32
    )


def params(limit=VMEM_LIMIT):
    return pltpu.CompilerParams(vmem_limit_bytes=limit)


def vmem():
    return pl.BlockSpec(memory_space=pltpu.VMEM)


def smem():
    return pl.BlockSpec(memory_space=pltpu.SMEM)


def anywhere():
    return pl.BlockSpec(memory_space=pl.ANY)


def cost(flops, moved, special=0):
    return pl.CostEstimate(flops=flops, bytes_accessed=moved, transcendentals=special)


def project_kernel(n_after, tokens, w_t, gain, *rest):
    pre, qkv = rest[n_after:]
    rows = tokens.shape[0]
    local = w_t.shape[0] // 3
    gain_row = gain[...].astype(F32).reshape(1, -1)
    for block in range(rows // SHORT):
        at = slice(block * SHORT, (block + 1) * SHORT)
        low = (row_norm(tokens[at, :].astype(F32))[0] * gain_row).astype(BF)
        pre[at, :] = low
        product = dot(w_t[...], low, 1, 1)
        qkv[0:local, at] = (product[0:local] * HD ** (-0.5)).astype(BF)
        qkv[local:, at] = product[local:].astype(BF)


def project(tokens, w_t, gain, after):
    rows, width = tokens.shape
    return pl.pallas_call(
        partial(project_kernel, len(after)),
        out_shape=(
            jax.ShapeDtypeStruct((rows, width), BF),
            jax.ShapeDtypeStruct((w_t.shape[0], rows), BF),
        ),
        in_specs=[vmem()] * 3 + [anywhere()] * len(after),
        out_specs=[vmem()] * 2,
        compiler_params=params(),
        cost_estimate=cost(7000000000, 21000000),
        name="project",
    )(tokens, w_t, gain, *after)


def holds_long(flags, seq_length, seq_group):
    def look(i, found):
        here = (seq_group[i] == flags[0]) & (seq_length[i] > SHORT)
        return jnp.where(here, 1, found)

    return lax.fori_loop(0, seq_length.shape[0], look, 0)


def column_max(values):
    return jnp.max(values.reshape(values.shape[0] // 8, 8, SHORT), axis=0)


def column_sum(values):
    return jnp.sum(values.reshape(values.shape[0] // 8, 8, SHORT), axis=0)


def attend_kernel(n_after, n_out, flags, seq_length, seq_group, qkv, *rest):
    lse, *outs, att = rest[n_after:]
    local = qkv.shape[0] // 3
    heads = local // HD
    blocks = qkv.shape[1] // SHORT
    is_long, mine = holds_long(flags, seq_length, seq_group), flags[1]
    key_place = lax.broadcasted_iota(jnp.int32, (SHORT, SHORT), 0)
    query_place = lax.broadcasted_iota(jnp.int32, (SHORT, SHORT), 1)

    def run_path(long_path):
        def one_head(head, unused):
            at = pl.ds(pl.multiple_of(head * HD, HD), HD)
            k_at = pl.ds(pl.multiple_of(local + head * HD, HD), HD)
            v_at = pl.ds(pl.multiple_of(2 * local + head * HD, HD), HD)
            for block in range(blocks):
                q_t = qkv[at, block * SHORT : (block + 1) * SHORT]
                keys = [
                    slice(index * SHORT, (index + 1) * SHORT)
                    for index in range(0 if long_path else block, block + 1)
                ]
                parts = [dot(qkv[k_at, key], q_t, 0, 0) for key in keys]
                parts[-1] = jnp.where(key_place <= query_place, parts[-1], MASKED)
                largest = column_max(parts[0])
                for s in parts[1:]:
                    largest = jnp.maximum(largest, column_max(s))
                top = jnp.max(largest, axis=0, keepdims=True)
                total, out = 0.0, 0.0
                for key, s in zip(keys, parts):
                    p = jnp.exp(s - top)
                    total = total + column_sum(p)
                    out = out + dot(qkv[v_at, key], p.astype(BF), 1, 0)
                total = jnp.sum(total, axis=0, keepdims=True)
                att[block, at, :] = (out / total).astype(BF)
                lse[head, block] = jnp.broadcast_to(top + jnp.log(total), (8, SHORT))
            return unused

        lax.fori_loop(0, heads, one_head, 0)

    pl.when(is_long > 0)(lambda: run_path(True))
    pl.when(is_long == 0)(lambda: run_path(False))
    for place in range(n_out):
        outs[place][...] = att[mine ^ place]


def attend(flags, table, qkv, n_out, after):
    rows = qkv.shape[1]
    blocks = rows // SHORT
    local = qkv.shape[0] // 3
    return pl.pallas_call(
        partial(attend_kernel, len(after), n_out),
        out_shape=(jax.ShapeDtypeStruct((local // HD, blocks, 8, SHORT), F32),)
        + (jax.ShapeDtypeStruct((local, SHORT), BF),) * n_out,
        in_specs=[smem()] * 3 + [vmem()] + [anywhere()] * len(after),
        out_specs=[vmem()] * (1 + n_out),
        scratch_shapes=[pltpu.VMEM((blocks, local, SHORT), BF)],
        compiler_params=params(),
        cost_estimate=cost(15000000000, 45000000),
        name="attend",
    )(flags, *table, qkv, *after)


def attend_back_kernel(n_own, n_terms, n_earlier, *refs):
    flags, seq_length, seq_group, q_all, k_all, v_all, lse, pre, w_q, w_k, w_v = refs[:11]
    att, grads, rest = refs[11 : 11 + n_own], refs[11 + n_own : 11 + 2 * n_own], refs[11 + 2 * n_own :]
    terms, rest = rest[:n_terms], rest[n_terms:]
    if n_earlier:
        w_t, d_before, rest = rest[0], rest[1], rest[2:]
        earlier, rest = rest[:n_earlier], rest[n_earlier:]
    d_qkv, d_weight, attn_sum, *rest = rest
    if n_earlier:
        sent, kept, *rest = rest
    ag, delta = rest
    rows, width = pre.shape
    blocks = rows // SHORT
    is_long, mine = holds_long(flags, seq_length, seq_group), flags[1]

    for place in range(n_own):
        grad = grads[place][...]
        ag[mine ^ place] = grad
        product = grad.astype(F32) * att[place][...].astype(F32)
        delta[mine ^ place] = jnp.broadcast_to(jnp.sum(product, axis=0, keepdims=True), (8, SHORT))

    key_place = lax.broadcasted_iota(jnp.int32, (SHORT, SHORT), 0)
    query_place = lax.broadcasted_iota(jnp.int32, (SHORT, SHORT), 1)

    def run_path(long_path):
        d_q = [None] * blocks
        for block in range(blocks):
            k_cols = slice(block * SHORT, (block + 1) * SHORT)
            k_t = k_all[:, k_cols]
            v_t = v_all[:, k_cols]
            d_k = d_v = None
            for index in range(block, blocks if long_path else block + 1):
                q_t = q_all[:, index * SHORT : (index + 1) * SHORT]
                grad = ag[index]
                p = jnp.exp(dot(k_t, q_t, 0, 0) - lse[0, index][0:1])
                if index == block:
                    p = jnp.where(key_place <= query_place, p, 0.0)
                d_p = dot(v_t, grad, 0, 0)
                d_s = (p * (d_p - delta[index][0:1])).astype(BF)
                p = p.astype(BF)
                add = dot(k_t, d_s, 1, 0)
                d_q[index] = add if d_q[index] is None else d_q[index] + add
                add = dot(q_t, d_s, 1, 1)
                d_k = add if d_k is None else d_k + add
                add = dot(grad, p, 1, 1)
                d_v = add if d_v is None else d_v + add
            d_qkv[HD : 2 * HD, k_cols] = d_k.astype(BF)
            d_qkv[2 * HD :, k_cols] = d_v.astype(BF)
        for block in range(blocks):
            d_qkv[0:HD, block * SHORT : (block + 1) * SHORT] = (d_q[block] * HD ** (-0.5)).astype(BF)

    pl.when(is_long > 0)(lambda: run_path(True))
    pl.when(is_long == 0)(lambda: run_path(False))
    product = dot(d_qkv[...], pre[...], 1, 0)
    start = d_before.shape[0] if n_earlier else 0
    d_weight[start : start + 3 * HD, :] = product.astype(BF)
    if n_earlier:
        d_weight[0:start, :] = d_before[...]
    if n_terms:
        d_weight[3 * HD :, :] = sum(t[...].astype(F32) for t in terms).astype(BF)
    cross = jnp.zeros((8, width), F32)
    for place, weight in enumerate((w_q, w_k, w_v)):
        part = product[place * HD : (place + 1) * HD] * weight[...].astype(F32)
        cross = cross + jnp.sum(part.reshape(HD // 8, 8, width), axis=0)
    attn_sum[...] = cross
    if n_earlier:
        for place in range(n_own):
            cols = pl.ds(pl.multiple_of((mine ^ place) * SHORT, SHORT), SHORT)
            joined = [d[i * HD : (i + 1) * HD, cols] for i in range(3) for d in (*earlier, d_qkv)]
            grad = dot(w_t[...], jnp.concatenate(joined, axis=0), 0, 0)
            target = sent if place % 2 else kept
            target[place // 2] = grad.astype(BF)


def attend_back(flags, table, qkv, head, lse, pre, w_t, att, grads, terms=(), d_before=None, earlier=()):
    rows, width = pre.shape
    blocks = rows // SHORT
    heads = qkv.shape[0] // (3 * HD)
    n_own = len(att)

    def part(place, columns):
        return pl.BlockSpec((HD, columns), lambda i, at=place: (at, 0))

    def whole(struct):
        return pl.BlockSpec(struct.shape, lambda i, n=len(struct.shape): (0,) * n)

    more = [w_t, d_before, *earlier] if earlier else []
    weight_rows = 3 * HD + sum(v.shape[0] for v in [*terms[:1], *more[1:2]])
    outs = (
        jax.ShapeDtypeStruct((3 * HD, rows), BF),
        jax.ShapeDtypeStruct((weight_rows, width), BF),
        jax.ShapeDtypeStruct((8, width), F32),
    )
    if earlier:
        outs += (jax.ShapeDtypeStruct((n_own // 2, width, SHORT), BF),) * 2
    return pl.pallas_call(
        partial(attend_back_kernel, n_own, len(terms), len(earlier)),
        grid=(1,),
        out_shape=outs,
        in_specs=[smem()] * 3
        + [part(place * heads + head, rows) for place in range(3)]
        + [pl.BlockSpec((1,) + lse.shape[1:], lambda i: (head, 0, 0, 0)), whole(pre)]
        + [part(place * heads + head, width) for place in range(3)]
        + [part(head, SHORT)] * (2 * n_own)
        + [whole(v) for v in [*terms, *more]],
        out_specs=[whole(o) for o in outs],
        scratch_shapes=[
            pltpu.VMEM((blocks, HD, SHORT), BF),
            pltpu.VMEM((blocks, 8, SHORT), F32),
        ],
        compiler_params=params(),
        cost_estimate=cost(11_500_000_000, 34_500_000),
        name="attend_back",
    )(flags, *table, qkv, qkv, qkv, lse, pre, w_t, w_t, w_t, *att, *grads, *terms, *more)


def gelu_parts(h):
    phi = jnp.exp(h * h * (-0.5)) * 0.3989422804014327
    big = 0.5 * lax.erf(h * 0.7071067811865476) + 0.5
    return h * big, big + h * phi


def inner_stats(att, width):
    total = sum(jnp.sum(piece[...].astype(F32), axis=0, keepdims=True) for piece in att)
    average = total / width
    square = 0.0
    for piece in att:
        centred = piece[...].astype(F32) - average
        square = square + jnp.sum(centred * centred, axis=0, keepdims=True)
    return average, lax.rsqrt(square / width + EPSILON)


def row_norm(x):
    centred = x - jnp.mean(x, axis=1, keepdims=True)
    factor = lax.rsqrt(jnp.mean(centred * centred, axis=1, keepdims=True) + EPSILON)
    return centred * factor, factor


def fetch(pieces, places, target, sems):
    copies = [
        pltpu.make_async_copy(
            pieces[number].at[pl.ds(start, rows), :], target.at[pl.ds(to, rows), :], sems.at[i]
        )
        for i, (number, start, to, rows) in enumerate(places)
    ]
    for copy in copies:
        copy.start()

    def wait():
        for copy in copies:
            copy.wait()

    return wait


def outer_kernel(left, left_came, right, right_came, over_2, over_4, own, first, second):
    size = own.shape[0]
    half = size // 2
    places = [
        ((own, 0), (own, half)),
        ((over_2, 0), (second, 0)),
        ((first, 0), (over_4, 0)),
        ((over_2, half), (over_4, half)),
    ]
    for number, pair in enumerate(places):
        at = slice(number * size, (number + 1) * size)
        product = dot(left[:, at], right[...], 0, 0) + dot(left_came[:, at], right_came[...], 0, 0)
        for part, (out, start) in enumerate(pair):
            out[start : start + half, :] = product[part * half : (part + 1) * half].astype(BF)


def outer(left, left_came, right, right_came):
    size, width = left.shape[1] // 4, right.shape[1]
    whole, half = (jax.ShapeDtypeStruct((rows, width), BF) for rows in (size, size // 2))
    return pl.pallas_call(
        outer_kernel,
        out_shape=(whole, whole, whole, half, half),
        in_specs=[vmem()] * 4,
        out_specs=[vmem()] * 5,
        compiler_params=params(),
        cost_estimate=cost(5_000_000_000, 15_000_000),
        name="outer",
    )(left, left_came, right, right_came)


def expand_kernel(n_own, n_piece, places, flags, *refs):
    att, w_out = refs[:n_own], refs[n_own : 2 * n_own]
    tokens, gain_ffn = refs[2 * n_own : 2 * n_own + 2]
    pieces, rest = refs[2 * n_own + 2 : 2 * n_own + 2 + n_piece], refs[2 * n_own + 2 + n_piece :]
    *posts, slope, factors, middle, mid_low, inner_t, weight, act, own, sems, own_sem = rest
    rows, width = middle.shape
    start = pl.multiple_of(flags[1] * rows, rows)
    own_copy = pltpu.make_async_copy(tokens.at[pl.ds(start, rows), :], own, own_sem)
    own_copy.start()
    local = att[0].shape[0]
    hidden = weight.shape[0]
    chunk = width
    wait = fetch(pieces, places, weight, sems)

    average, inner_factor = inner_stats(att, width)
    for place, piece in enumerate(att):
        hat = (piece[...].astype(F32) - average) * inner_factor
        inner_t[place * local : (place + 1) * local, :] = hat.astype(BF)
    branch = dot(inner_t[0:local, :], w_out[0][...], 0, 0)
    for place in range(1, n_own):
        branch += dot(inner_t[place * local : (place + 1) * local, :], w_out[place][...], 0, 0)
    own_copy.wait()
    total = own[...].astype(F32) + branch
    middle[...] = total
    mid_low[...] = (row_norm(total)[0] * gain_ffn[...].astype(F32).reshape(1, -1)).astype(BF)
    wait()
    for start in range(0, hidden, chunk):
        to = slice(start, start + chunk)
        a, s = gelu_parts(dot(mid_low[...], weight[to, :], 1, 1))
        act[:, to] = a
        slope[:, to] = s.astype(BF)
    n, factor = row_norm(act[...])
    for number, post in enumerate(posts):
        post[...] = n[:, number * hidden // 2 : (number + 1) * hidden // 2].astype(BF)
    factors[...] = jnp.broadcast_to(factor, (rows, 128))


def expand_ffn(flags, att, w_out, tokens, gain_ffn, expand, places):
    rows, width = att[0].shape[1], tokens.shape[1]
    hidden = sum(e.shape[0] for e in expand)
    n_own = len(att)
    local = att[0].shape[0]
    return pl.pallas_call(
        partial(expand_kernel, n_own, len(expand), places),
        out_shape=(
            jax.ShapeDtypeStruct((rows, hidden // 2), BF),
            jax.ShapeDtypeStruct((rows, hidden // 2), BF),
            jax.ShapeDtypeStruct((rows, hidden), BF),
            jax.ShapeDtypeStruct((rows, 128), F32),
            jax.ShapeDtypeStruct((rows, width), F32),
            jax.ShapeDtypeStruct((rows, width), BF),
            jax.ShapeDtypeStruct((n_own * local, rows), BF),
        ),
        in_specs=[smem()]
        + [vmem()] * (2 * n_own)
        + [anywhere(), vmem()]
        + [anywhere()] * len(expand),
        out_specs=[vmem()] * 7,
        scratch_shapes=[
            pltpu.VMEM((hidden, width), BF),
            pltpu.VMEM((rows, hidden), F32),
            pltpu.VMEM((rows, width), BF),
            pltpu.SemaphoreType.DMA((len(places),)),
            pltpu.SemaphoreType.DMA,
        ],
        compiler_params=params(),
        cost_estimate=cost(12000000000, 36000000),
        name="expand_ffn",
    )(flags, *att, *w_out, tokens, gain_ffn, *expand)


def reduce_kernel(n_piece, places, *refs):
    posts, (slope, factors, middle, cotangent), rest = refs[:2], refs[2:6], refs[6:]
    pieces, (output, *grads, weight, d_post, sems) = rest[:n_piece], rest[n_piece:]
    hidden, width = weight.shape
    half = hidden // 2
    fetch(pieces, places, weight, sems)()
    total = middle[...]
    for start in range(0, hidden, width):
        at = slice(start % half, start % half + width)
        rows = slice(start, start + width)
        d_post[:, rows] = dot(cotangent[...], weight[rows, :], 1, 1)
        total = total + dot(posts[start // half][:, at], weight[rows, :], 1, 0)
    output[...] = total.astype(BF)
    mean_e, mean_en = 0.0, 0.0
    for number, post in enumerate(posts):
        e = d_post[:, number * half : (number + 1) * half]
        mean_e = mean_e + jnp.sum(e, axis=1, keepdims=True) / hidden
        mean_en = mean_en + jnp.sum(e * post[...].astype(F32), axis=1, keepdims=True) / hidden
    for number, (post, grad) in enumerate(zip(posts, grads)):
        at = slice(number * half, (number + 1) * half)
        back = d_post[:, at] - mean_e - post[...].astype(F32) * mean_en
        grad[...] = (factors[:, 0:1] * back * slope[:, at].astype(F32)).astype(BF)


def reduce_ffn(posts, slope, factors, middle, cotangent, reduced, places):
    rows, width = middle.shape
    hidden = slope.shape[1]
    return pl.pallas_call(
        partial(reduce_kernel, len(reduced), places),
        out_shape=(
            jax.ShapeDtypeStruct((rows, width), BF),
            jax.ShapeDtypeStruct((rows, hidden // 2), BF),
            jax.ShapeDtypeStruct((rows, hidden // 2), BF),
        ),
        in_specs=[vmem()] * 6 + [anywhere()] * len(reduced),
        out_specs=[vmem()] * 3,
        scratch_shapes=[
            pltpu.VMEM((hidden, width), BF),
            pltpu.VMEM((rows, hidden), F32),
            pltpu.SemaphoreType.DMA((len(places),)),
        ],
        compiler_params=params(),
        cost_estimate=cost(15_000_000_000, 45_000_000),
        name="reduce_ffn",
    )(*posts, slope, factors, middle, cotangent, *reduced)


def middle_kernel(n_own, n_piece, places, *refs):
    att, w_out = refs[:n_own], refs[n_own : 2 * n_own]
    *hidden_grads, middle, cotangent, inner_t, gain_ffn = refs[2 * n_own : 2 * n_own + 6]
    rest = refs[2 * n_own + 6 :]
    pieces, rest = rest[:n_piece], rest[n_piece:]
    middle_grad, ffn_sum, sent, kept = rest[:4]
    grads = rest[4 : 4 + n_own]
    weight, branch_grad, e_buf, sems = rest[4 + n_own :]
    rows, width = middle.shape
    local = att[0].shape[0]
    half = weight.shape[0] // 2
    gain_row = gain_ffn[...].astype(F32).reshape(1, -1)
    wait = fetch(pieces, places, weight, sems)
    n, factor = row_norm(middle[...])
    average, inner_factor = inner_stats(att, width)
    wait()
    grad = dot(hidden_grads[0][...], weight[0:half, :], 1, 0)
    grad = grad + dot(hidden_grads[1][...], weight[half:, :], 1, 0)
    ffn_sum[...] = jnp.sum((grad * n).reshape(rows // 8, 8, width), axis=0)
    e = grad * gain_row
    back = factor * (
        e - jnp.mean(e, axis=1, keepdims=True) - n * jnp.mean(e * n, axis=1, keepdims=True)
    )
    full = cotangent[...].astype(F32) + back
    middle_grad[...] = full
    branch_grad[...] = full.astype(BF)

    grad_sum = jnp.zeros((1, rows), F32)
    cross_sum = jnp.zeros((1, rows), F32)
    for place in range(n_own):
        e = dot(w_out[place][...], branch_grad[...], 1, 1)
        e_buf[place] = e
        grad_sum = grad_sum + jnp.sum(e, axis=0, keepdims=True)
        hat = (att[place][...].astype(F32) - average) * inner_factor
        cross_sum = cross_sum + jnp.sum(e * hat, axis=0, keepdims=True)
    for place in range(n_own):
        hat = (att[place][...].astype(F32) - average) * inner_factor
        grad = inner_factor * (e_buf[place] - grad_sum / width - hat * (cross_sum / width))
        grads[place][...] = grad.astype(BF)
        target = sent if place % 2 else kept
        at = slice(place * local, (place + 1) * local)
        target[place // 2] = dot(inner_t[at, :], branch_grad[...], 1, 0).astype(BF)


def middle_back(att, w_out, hidden_grads, middle, cotangent, inner_t, gain_ffn, expand, places):
    rows, width = middle.shape
    hidden = 2 * hidden_grads[0].shape[1]
    n_own = len(att)
    local = att[0].shape[0]
    return pl.pallas_call(
        partial(middle_kernel, n_own, len(expand), places),
        out_shape=(
            jax.ShapeDtypeStruct((rows, width), F32),
            jax.ShapeDtypeStruct((8, width), F32),
            jax.ShapeDtypeStruct((n_own // 2, local, width), BF),
            jax.ShapeDtypeStruct((n_own // 2, local, width), BF),
        )
        + (jax.ShapeDtypeStruct((local, rows), BF),) * n_own,
        in_specs=[vmem()] * (2 * n_own + 6) + [anywhere()] * len(expand),
        out_specs=[vmem()] * (4 + n_own),
        scratch_shapes=[
            pltpu.VMEM((hidden, width), BF),
            pltpu.VMEM((rows, width), BF),
            pltpu.VMEM((n_own, local, rows), F32),
            pltpu.SemaphoreType.DMA((len(places),)),
        ],
        compiler_params=params(),
        cost_estimate=cost(12_500_000_000, 37_500_000),
        name="middle_back",
    )(*att, *w_out, *hidden_grads, middle, cotangent, inner_t, gain_ffn, *expand)


def input_gradient_kernel(
    flags, kept, came, first, second, tokens, gain, middle_grad, out, own, sem
):
    rows = out.shape[0]
    start = pl.multiple_of(flags[1] * rows, rows)
    copy = pltpu.make_async_copy(tokens.at[pl.ds(start, rows), :], own, sem)
    copy.start()
    last = jnp.concatenate([first[...], second[...]], axis=0)
    total = kept[0].astype(F32) + came[0].astype(F32) + last.astype(F32)
    e = total.T * gain[...].astype(F32).reshape(1, -1)
    copy.wait()
    n, factor = row_norm(own[...].astype(F32))
    back = factor * (
        e - jnp.mean(e, axis=1, keepdims=True) - n * jnp.mean(e * n, axis=1, keepdims=True)
    )
    out[...] = (middle_grad[...] + back).astype(BF)


def input_gradient(flags, terms, tokens, gain, middle_grad):
    kept, came, first, second = terms
    block = pl.BlockSpec((1,) + kept.shape[1:], lambda i: (0, 0, 0))

    def whole(v):
        return pl.BlockSpec(v.shape, lambda i: (0,) * v.ndim)

    return pl.pallas_call(
        input_gradient_kernel,
        grid=(1,),
        out_shape=jax.ShapeDtypeStruct(middle_grad.shape, BF),
        in_specs=[smem(), block, block, whole(first), whole(second), anywhere()]
        + [whole(gain), whole(middle_grad)],
        out_specs=whole(middle_grad),
        scratch_shapes=[pltpu.VMEM(middle_grad.shape, BF), pltpu.SemaphoreType.DMA],
        compiler_params=params(),
        cost_estimate=cost(4500000000, 13500000),
        name="input_gradient",
    )(flags, *terms, tokens, gain, middle_grad)


def body(
    tokens,
    w_query,
    w_key,
    w_value,
    w_output,
    gain_attn,
    gain_inner,
    gain_ffn,
    w_expand,
    w_reduce,
    gain_hidden,
    cotangent,
    seq_length,
    seq_group,
):
    n_batch, n_own = lax.axis_size("batch"), lax.axis_size("heads")
    n_all = n_batch * n_own
    mine = lax.axis_index("heads")
    quarter = cotangent.shape[0]
    width = tokens.shape[1]
    local = w_query.shape[1]
    n_heads = local // HD

    def swap(value, bit):
        return lax.ppermute(value, AXES, [(i, i ^ bit) for i in range(n_all)])

    flags = jnp.stack([lax.axis_index("batch"), mine]).astype(jnp.int32)
    table = (seq_length, seq_group)
    far = [1 << b for b in range(3, n_all.bit_length() - 1)]
    near = (2, 4, 6)

    def parts(value, offsets):
        return [value] + [swap(value, off) for off in offsets]

    def around(value, offsets):
        return jnp.concatenate(parts(value, offsets), axis=0)

    def far_steps(value):
        for bit in reversed(far):
            value = around(value, (bit,))
            yield value

    def add(values):
        return sum(v.astype(F32) for v in values)

    phase = lax.optimization_barrier

    def sum_begin(value):
        rows = value.shape[0]
        value = lax.all_to_all(value, "batch", 0, 0, tiled=True)
        return value.reshape(n_batch, rows // n_batch, width)

    def sum_middle(value):
        return jnp.sum(value.astype(F32), axis=0)

    def sum_end(share):
        share = jnp.broadcast_to(share.astype(BF)[None], (n_batch,) + share.shape)
        return lax.all_to_all(share, "batch", 0, 0, tiled=True)

    def last(steps):
        *_, value = steps
        return value

    w_t = jnp.concatenate([w_query.T, w_key.T, w_value.T], axis=0)
    w_reduce_scaled = (w_reduce.astype(F32) * gain_hidden.astype(F32)[:, None]).astype(BF)
    w_output_scaled = (w_output.astype(F32) * gain_inner.astype(F32)[:, None]).astype(BF)

    if len(far) == 2:
        expand_far = parts(w_expand, (far[1], far[0], far[0] | far[1]))
    else:
        expand_far = [last(far_steps(w_expand))]
    reduced = w_reduce_scaled
    for bit in far[:0:-1]:
        reduced = parts(jnp.concatenate(reduced) if isinstance(reduced, list) else reduced, (bit,))
    w_out_y = swap(w_output_scaled, 2)
    pre, qkv = project(tokens, w_t, gain_attn, [])
    expand_far, reduced, w_out_y, pre, qkv = phase((expand_far, reduced, w_out_y, pre, qkv))

    expand = parts(jnp.concatenate(expand_far), near)
    reduced = parts(jnp.concatenate(reduced), (far[0],))
    w_out_c = swap(jnp.stack([w_output_scaled, w_out_y]), 1)
    lse, *pieces = attend(flags, table, qkv, n_own, [])
    reduced, w_out_c, lse, pieces = phase((reduced, w_out_c, lse, pieces))

    att = [pieces[0]] + [swap(pieces[k], k) for k in range(1, n_own)]
    expand, att = phase((expand, att))
    expand = jnp.concatenate(expand)
    expand = [expand, swap(expand, 1)]
    reduced = jnp.concatenate(reduced)
    half = reduced.shape[0] // 2
    first = [swap(reduced[:half], 4), swap(reduced[half:], 2)]
    w_out = [w_output_scaled, w_out_c[0], w_out_y, w_out_c[1]]
    att, expand, reduced, first, w_out, cotangent = phase(
        (att, expand, reduced, first, w_out, cotangent)
    )
    cot_came = swap(cotangent, 1)

    def stacked(parts):
        starts = [sum(p.shape[0] for p in parts[:i]) for i in range(len(parts))]
        return [(i, 0, start, p.shape[0]) for i, (start, p) in enumerate(zip(starts, parts))]

    places = stacked(expand)
    second = [
        swap(jnp.concatenate([reduced[:half], first[0]]), 2),
        swap(jnp.concatenate([reduced[half:], first[1]]), 4),
    ]
    *posts, slope, factors, middle, mid_low, inner_t = expand_ffn(
        flags, att, w_out, tokens, gain_ffn, expand, places
    )
    reduced, posts, slope, factors, middle, mid_low, inner_t, cot_came = phase(
        ([reduced, *first, *second], posts, slope, factors, middle, mid_low, inner_t, cot_came)
    )

    starts = [(0, 0, 0), (0, half, 1), (1, 0, 4), (2, 0, 3)]
    starts += [(3, 0, 2), (3, half, 6), (4, 0, 5), (4, half, 7)]
    reduce_places = [
        (number + core * 5, start, core * 8 * half + at * half, half)
        for core in range(2)
        for number, start, at in starts
    ]
    post_came = swap(posts[1], 1)
    reduced = reduced + [swap(r, 1) for r in reduced]
    d_reduce = outer(posts[0], post_came, cotangent, cot_came)
    reduced, posts, mid_low, d_reduce = phase((reduced, posts, mid_low, d_reduce))

    def near_begin(products):
        return swap(products[0], 2), swap(products[1], 4)

    def near_middle(products, came):
        half = came[0].shape[0] // 2
        terms = [add((p, c[half:])).astype(BF) for p, c in zip(products[3:], came)]
        return came, (swap(terms[0], 4), swap(terms[1], 2))

    def near_end(products, begun, came):
        half = came[0].shape[0]
        return [
            add((products[2][i * half : (i + 1) * half], b[:half], c))
            for i, (b, c) in enumerate(zip(begun, came))
        ]

    begun_r = near_begin(d_reduce)
    mid_came = swap(mid_low, 1)
    output, *hidden_grads = reduce_ffn(
        posts, slope, factors, middle, cotangent, reduced, reduce_places
    )
    output, hidden_grads, begun_r, d_reduce, mid_came = phase(
        (output, hidden_grads, begun_r, d_reduce, mid_came)
    )

    begun_r, came_r = near_middle(d_reduce, begun_r)
    grad_came = swap(hidden_grads[1], 1)
    middle_grad, ffn_sum, d_sent, d_kept, *att_grads = middle_back(
        att, w_out, hidden_grads, middle, cotangent, inner_t, gain_ffn, expand, places
    )
    came_r, grad_came, middle_grad, ffn_sum, d_sent, d_kept, att_grads = phase(
        (came_r, grad_came, middle_grad, ffn_sum, d_sent, d_kept, att_grads)
    )

    def far_sum(value, bit):
        return value[0], swap(value[1].astype(BF), bit)

    def halves(value):
        return value.reshape(2, -1, width)

    grads = [att_grads[0]] + [swap(att_grads[k], k) for k in range(1, n_own)]
    d_came = swap(d_sent, 1)
    d_came, mid_came, begun_r, came_r = phase((d_came, mid_came, begun_r, came_r))
    d_reduce = far_sum(near_end(d_reduce, begun_r, came_r), far[0])
    d_expand = outer(hidden_grads[0], grad_came, mid_low, mid_came)
    d_reduce, grads, d_expand, d_came = phase((d_reduce, grads, d_expand, d_came))

    back = partial(attend_back, flags, table, qkv)

    begun_e = near_begin(d_expand)
    for bit in far[1:]:
        d_reduce = far_sum(halves(add(d_reduce)), bit)
    d_last = swap(add((d_kept[1], d_came[1])).astype(BF), 2)
    back_0 = back(0, lse, pre, w_t, pieces, grads)
    back_0, d_reduce, begun_e, d_expand, d_last, grads = phase(
        (back_0, d_reduce, begun_e, d_expand, d_last, grads)
    )

    d_own = add((d_kept[0], d_came[0], d_last)).astype(BF)
    share_0 = sum_begin(jnp.concatenate([back_0[1], d_own]))
    begun_e, came_e = near_middle(d_expand, begun_e)
    back_1 = back(1, lse, pre, w_t, pieces, grads)
    back_1, came_e, share_0, grads = phase((back_1, came_e, share_0, grads))

    batch_bits = [1 << b for b in range(n_batch.bit_length() - 1)][::-1]

    def gather_step(value, bit):
        return value, swap(value, bit * n_own)

    def joined(pair, bit):
        axis = batch_bits.index(bit)
        mine_first = (lax.axis_index("batch") & bit) == 0
        return jnp.where(
            mine_first, jnp.concatenate(pair, axis), jnp.concatenate(pair[::-1], axis)
        )

    d_expand = near_end(d_expand, begun_e, came_e)
    if len(far) == 2:
        blocks = [v.astype(BF) for part in d_expand for v in halves(part)]
        offs = (far[1], far[0], far[0] | far[1])
        d_expand = [halves(d_expand[0])[0]] + [swap(b, o) for b, o in zip(blocks[1:], offs)]
    else:
        d_expand = far_sum(d_expand, far[0])
        for bit in far[1:]:
            d_expand = far_sum(halves(add(d_expand)), bit)
    share_0 = sum_middle(share_0).astype(BF)
    share_0 = gather_step(share_0.reshape((1,) * len(batch_bits) + share_0.shape), batch_bits[0])
    earlier = (back_0[0], back_1[0])
    back_2 = back(2, lse, pre, w_t, pieces, grads, d_before=back_1[1], earlier=earlier)
    back_2, d_expand, share_0 = phase((back_2, d_expand, share_0))

    share_1 = sum_begin(back_2[1])
    small = jnp.sum(jnp.stack([back_0[2] + back_1[2] + back_2[2], ffn_sum]), axis=1)
    small = small + swap(small, 1)
    small = small + swap(small, 2)
    sent, kept = back_2[3:]
    came = swap(sent, 1)
    came, kept, small = phase((came, kept, small))
    split = width // 2
    terms = [
        add((kept[1, at], came[1, at])).astype(BF)
        for at in (slice(0, split), slice(split, width))
    ]
    first = swap(terms[0], 2)
    for bit, later in zip(batch_bits[:-1], batch_bits[1:-1]):
        share_0 = gather_step(joined(share_0, bit), later)
    share_1, share_0, first, terms, d_expand = phase((share_1, share_0, first, terms, d_expand))

    second = [first, swap(terms[1], 2)]
    share_1 = sum_middle(share_1)
    count = share_1.shape[0]
    total_1 = sum_end(jnp.concatenate([share_1, small], axis=0))
    share_0 = gather_step(joined(share_0, batch_bits[-2]), batch_bits[-1])
    grad_tokens = input_gradient(
        flags, (kept, came, *second), tokens, gain_attn, middle_grad
    )
    grad_tokens, share_0, d_reduce, d_expand = phase((grad_tokens, share_0, d_reduce, d_expand))
    d_expand = add(d_expand)
    d_reduce = add(d_reduce)
    g_hidden = jnp.sum(d_reduce * w_reduce.astype(F32), axis=1)
    d_reduce = d_reduce * gain_hidden.astype(F32)[:, None]

    total_0 = joined(share_0, batch_bits[-1]).astype(F32).reshape(-1, width)
    total_1 = total_1.astype(F32)
    small = jnp.sum(total_1[:, count:], axis=0)
    total_1 = total_1[:, :count].reshape(-1, width)
    totals = [total_0, total_1[: 3 * HD], total_1[3 * HD :]]
    def weight_grad(place):
        at = slice(place * HD, (place + 1) * HD)
        return jnp.concatenate([t[at] for t in totals], axis=0).T

    g_out = totals[0][3 * HD :]
    return (
        output,
        grad_tokens,
        weight_grad(0),
        weight_grad(1),
        weight_grad(2),
        g_out * gain_inner.astype(F32)[:, None],
        small[0] / gain_attn.astype(F32),
        jnp.sum(g_out * w_output.astype(F32), axis=1),
        small[1],
        d_expand,
        d_reduce,
        g_hidden,
    )


def solution(mesh):
    both = P(AXES, None)
    return jax.shard_map(
        body,
        mesh=mesh,
        in_specs=(
            P("batch", None),
            P(None, "heads"),
            P(None, "heads"),
            P(None, "heads"),
            P("heads", None),
            P(),
            P("heads"),
            P(),
            both,
            both,
            P(AXES),
            both,
            P(),
            P(),
        ),
        out_specs=(
            both,
            both,
            P(None, "heads"),
            P(None, "heads"),
            P(None, "heads"),
            P("heads", None),
            P(),
            P("heads"),
            P(),
            both,
            both,
            P(AXES),
        ),
        check_vma=False,
    )
```

```python
from functools import partial

import jax
import jax.numpy as jnp
from jax import lax
from jax.experimental import pallas as pl
from jax.experimental.pallas import tpu as pltpu
from jax.sharding import PartitionSpec as P

HD = 64
SHORT = 512
EPSILON = 1e-05
MASKED = -1e30
AXES = ("batch", "heads")
BF = jnp.bfloat16
F32 = jnp.float32
VMEM_LIMIT = 60 * 1024 * 1024


def dot(left, right, left_dim, right_dim):
    return lax.dot_general(
        left, right, (((left_dim,), (right_dim,)), ((), ())), preferred_element_type=F32
    )


def params(limit=VMEM_LIMIT):
    return pltpu.CompilerParams(vmem_limit_bytes=limit)


def vmem():
    return pl.BlockSpec(memory_space=pltpu.VMEM)


def smem():
    return pl.BlockSpec(memory_space=pltpu.SMEM)


def anywhere():
    return pl.BlockSpec(memory_space=pl.ANY)


def cost(flops, moved, special=0):
    return pl.CostEstimate(flops=flops, bytes_accessed=moved, transcendentals=special)


def project_kernel(n_after, tokens, w_t, gain, *rest):
    pre, qkv = rest[n_after:]
    rows = tokens.shape[0]
    local = w_t.shape[0] // 3
    gain_row = gain[...].astype(F32).reshape(1, -1)
    for block in range(rows // SHORT):
        at = slice(block * SHORT, (block + 1) * SHORT)
        low = (row_norm(tokens[at, :].astype(F32))[0] * gain_row).astype(BF)
        pre[at, :] = low
        product = dot(w_t[...], low, 1, 1)
        qkv[0:local, at] = (product[0:local] * HD ** (-0.5)).astype(BF)
        qkv[local:, at] = product[local:].astype(BF)


def project(tokens, w_t, gain, after):
    rows, width = tokens.shape
    return pl.pallas_call(
        partial(project_kernel, len(after)),
        out_shape=(
            jax.ShapeDtypeStruct((rows, width), BF),
            jax.ShapeDtypeStruct((w_t.shape[0], rows), BF),
        ),
        in_specs=[vmem()] * 3 + [anywhere()] * len(after),
        out_specs=[vmem()] * 2,
        compiler_params=params(),
        cost_estimate=cost(7000000000, 21000000),
        name="project",
    )(tokens, w_t, gain, *after)


def holds_long(flags, seq_length, seq_group):
    def look(i, found):
        here = (seq_group[i] == flags[0]) & (seq_length[i] > SHORT)
        return jnp.where(here, 1, found)

    return lax.fori_loop(0, seq_length.shape[0], look, 0)


def column_max(values):
    return jnp.max(values.reshape(values.shape[0] // 8, 8, SHORT), axis=0)


def column_sum(values):
    return jnp.sum(values.reshape(values.shape[0] // 8, 8, SHORT), axis=0)


def attend_kernel(n_after, n_out, flags, seq_length, seq_group, qkv, *rest):
    lse, *outs, att = rest[n_after:]
    local = qkv.shape[0] // 3
    heads = local // HD
    blocks = qkv.shape[1] // SHORT
    is_long, mine = holds_long(flags, seq_length, seq_group), flags[1]
    key_place = lax.broadcasted_iota(jnp.int32, (SHORT, SHORT), 0)
    query_place = lax.broadcasted_iota(jnp.int32, (SHORT, SHORT), 1)

    def run_path(long_path):
        def one_head(head, unused):
            at = pl.ds(pl.multiple_of(head * HD, HD), HD)
            k_at = pl.ds(pl.multiple_of(local + head * HD, HD), HD)
            v_at = pl.ds(pl.multiple_of(2 * local + head * HD, HD), HD)
            for block in range(blocks):
                q_t = qkv[at, block * SHORT : (block + 1) * SHORT]
                keys = [
                    slice(index * SHORT, (index + 1) * SHORT)
                    for index in range(0 if long_path else block, block + 1)
                ]
                parts = [dot(qkv[k_at, key], q_t, 0, 0) for key in keys]
                parts[-1] = jnp.where(key_place <= query_place, parts[-1], MASKED)
                largest = column_max(parts[0])
                for s in parts[1:]:
                    largest = jnp.maximum(largest, column_max(s))
                top = jnp.max(largest, axis=0, keepdims=True)
                total, out = 0.0, 0.0
                for key, s in zip(keys, parts):
                    p = jnp.exp(s - top)
                    total = total + column_sum(p)
                    out = out + dot(qkv[v_at, key], p.astype(BF), 1, 0)
                total = jnp.sum(total, axis=0, keepdims=True)
                att[block, at, :] = (out / total).astype(BF)
                lse[head, block] = jnp.broadcast_to(top + jnp.log(total), (8, SHORT))
            return unused

        lax.fori_loop(0, heads, one_head, 0)

    pl.when(is_long > 0)(lambda: run_path(True))
    pl.when(is_long == 0)(lambda: run_path(False))
    for place in range(n_out):
        outs[place][...] = att[mine ^ place]


def attend(flags, table, qkv, n_out, after):
    rows = qkv.shape[1]
    blocks = rows // SHORT
    local = qkv.shape[0] // 3
    return pl.pallas_call(
        partial(attend_kernel, len(after), n_out),
        out_shape=(jax.ShapeDtypeStruct((local // HD, blocks, 8, SHORT), F32),)
        + (jax.ShapeDtypeStruct((local, SHORT), BF),) * n_out,
        in_specs=[smem()] * 3 + [vmem()] + [anywhere()] * len(after),
        out_specs=[vmem()] * (1 + n_out),
        scratch_shapes=[pltpu.VMEM((blocks, local, SHORT), BF)],
        compiler_params=params(),
        cost_estimate=cost(15000000000, 45000000),
        name="attend",
    )(flags, *table, qkv, *after)


def attend_back_kernel(n_own, n_late, *refs):
    flags, seq_length, seq_group, q_all, k_all, v_all, lse, w_q, w_k, w_v = refs[:10]
    att, grads, rest = refs[10 : 10 + n_own], refs[10 + n_own : 10 + 2 * n_own], refs[10 + 2 * n_own :]
    late, (d_qkv, d_weight, attn_sum, *rest) = rest[:n_late], rest[n_late:]
    if n_late > 1:
        sent, kept, *rest = rest
    ag, delta, sems, *here = rest
    copies = [pltpu.make_async_copy(v, h, sems.at[n]) for n, (v, h) in enumerate(zip(late, here))]
    for copy in copies:
        copy.start()
    pre, *here = here
    rows, width = pre.shape
    blocks = rows // SHORT
    is_long, mine = holds_long(flags, seq_length, seq_group), flags[1]

    for place in range(n_own):
        grad = grads[place][...]
        ag[mine ^ place] = grad
        product = grad.astype(F32) * att[place][...].astype(F32)
        delta[mine ^ place] = jnp.broadcast_to(jnp.sum(product, axis=0, keepdims=True), (8, SHORT))

    half = SHORT // 2

    def pair(k_t, v_t, index, first, masked):
        q_t = q_all[:, index * SHORT + first : (index + 1) * SHORT]
        grad = ag[index][:, first:]
        p = jnp.exp(dot(k_t, q_t, 0, 0) - lse[0, index][0:1, first:])
        if masked:
            key_place = lax.broadcasted_iota(jnp.int32, p.shape, 0)
            p = jnp.where(key_place <= lax.broadcasted_iota(jnp.int32, p.shape, 1), p, 0.0)
        d_p = dot(v_t, grad, 0, 0)
        d_s = (p * (d_p - delta[index][0:1, first:])).astype(BF)
        p = p.astype(BF)
        return dot(k_t, d_s, 1, 0), dot(q_t, d_s, 1, 1), dot(grad, p, 1, 1)

    def run_path(long_path):
        d_q = [None] * blocks
        for block in range(blocks):
            k_cols = slice(block * SHORT, (block + 1) * SHORT)
            k_t = k_all[:, k_cols]
            v_t = v_all[:, k_cols]
            q_1, k_1, v_1 = pair(k_t[:, :half], v_t[:, :half], block, 0, True)
            q_2, k_2, v_2 = pair(k_t[:, half:], v_t[:, half:], block, half, True)
            add = jnp.concatenate([q_1[:, :half], q_1[:, half:] + q_2], axis=1)
            d_q[block] = add if d_q[block] is None else d_q[block] + add
            d_k = jnp.concatenate([k_1, k_2], axis=1)
            d_v = jnp.concatenate([v_1, v_2], axis=1)
            for index in range(block + 1, blocks if long_path else block + 1):
                add_q, add_k, add_v = pair(k_t, v_t, index, 0, False)
                d_q[index] = add_q if d_q[index] is None else d_q[index] + add_q
                d_k = d_k + add_k
                d_v = d_v + add_v
            d_qkv[HD : 2 * HD, k_cols] = d_k.astype(BF)
            d_qkv[2 * HD :, k_cols] = d_v.astype(BF)
        for block in range(blocks):
            d_qkv[0:HD, block * SHORT : (block + 1) * SHORT] = (d_q[block] * HD ** (-0.5)).astype(BF)

    pl.when(is_long > 0)(lambda: run_path(True))
    pl.when(is_long == 0)(lambda: run_path(False))
    for copy in copies:
        copy.wait()
    product = dot(d_qkv[...], pre[...], 1, 0)
    start = d_weight.shape[0] - 3 * HD
    d_weight[start:, :] = product.astype(BF)
    cross = jnp.zeros((8, width), F32)
    for place, weight in enumerate((w_q, w_k, w_v)):
        part = product[place * HD : (place + 1) * HD] * weight[...].astype(F32)
        cross = cross + jnp.sum(part.reshape(HD // 8, 8, width), axis=0)
    attn_sum[...] = cross
    if n_late > 1:
        w_t, d_before, *earlier = here
        d_weight[0:start, :] = d_before[...]
        for place in range(n_own):
            cols = pl.ds(pl.multiple_of((mine ^ place) * SHORT, SHORT), SHORT)
            joined = [d[i * HD : (i + 1) * HD, cols] for i in range(3) for d in (*earlier, d_qkv)]
            grad = dot(w_t[...], jnp.concatenate(joined, axis=0), 0, 0)
            target = sent if place % 2 else kept
            target[place // 2] = grad.astype(BF)


def attend_back(flags, table, qkv, head, lse, pre, w_t, att, grads, d_before=None, earlier=()):
    rows, width = pre.shape
    blocks = rows // SHORT
    heads = qkv.shape[0] // (3 * HD)
    n_own = len(att)

    def part(place, columns):
        return pl.BlockSpec((HD, columns), lambda i, at=place: (at, 0))

    def whole(struct):
        return pl.BlockSpec(struct.shape, lambda i, n=len(struct.shape): (0,) * n)

    late = [pre, *([w_t, d_before, *earlier] if earlier else [])]
    weight_rows = 3 * HD + (d_before.shape[0] if earlier else 0)
    outs = (
        jax.ShapeDtypeStruct((3 * HD, rows), BF),
        jax.ShapeDtypeStruct((weight_rows, width), BF),
        jax.ShapeDtypeStruct((8, width), F32),
    )
    if earlier:
        outs += (jax.ShapeDtypeStruct((n_own // 2, width, SHORT), BF),) * 2
    return pl.pallas_call(
        partial(attend_back_kernel, n_own, len(late)),
        grid=(1,),
        out_shape=outs,
        in_specs=[smem()] * 3
        + [part(place * heads + head, rows) for place in range(3)]
        + [pl.BlockSpec((1,) + lse.shape[1:], lambda i: (head, 0, 0, 0))]
        + [part(place * heads + head, width) for place in range(3)]
        + [part(head, SHORT)] * (2 * n_own)
        + [anywhere()] * len(late),
        out_specs=[whole(o) for o in outs],
        scratch_shapes=[
            pltpu.VMEM((blocks, HD, SHORT), BF),
            pltpu.VMEM((blocks, 8, SHORT), F32),
            pltpu.SemaphoreType.DMA((len(late),)),
        ]
        + [pltpu.VMEM(v.shape, BF) for v in late],
        compiler_params=params(),
        cost_estimate=cost(11_500_000_000, 34_500_000),
        name="attend_back",
    )(flags, *table, qkv, qkv, qkv, lse, w_t, w_t, w_t, *att, *grads, *late)


def gelu_parts(h):
    phi = jnp.exp(h * h * (-0.5)) * 0.3989422804014327
    big = 0.5 * lax.erf(h * 0.7071067811865476) + 0.5
    return h * big, big + h * phi


def inner_stats(att, width):
    total = sum(jnp.sum(piece[...].astype(F32), axis=0, keepdims=True) for piece in att)
    average = total / width
    square = 0.0
    for piece in att:
        centred = piece[...].astype(F32) - average
        square = square + jnp.sum(centred * centred, axis=0, keepdims=True)
    return average, lax.rsqrt(square / width + EPSILON)


def row_norm(x):
    centred = x - jnp.mean(x, axis=1, keepdims=True)
    factor = lax.rsqrt(jnp.mean(centred * centred, axis=1, keepdims=True) + EPSILON)
    return centred * factor, factor


def fetch(pieces, places, target, sems):
    copies = [
        pltpu.make_async_copy(
            pieces[number].at[pl.ds(start, rows), :], target.at[pl.ds(to, rows), :], sems.at[i]
        )
        for i, (number, start, to, rows) in enumerate(places)
    ]
    for copy in copies:
        copy.start()

    def wait():
        for copy in copies:
            copy.wait()

    return wait


def outer_kernel(left, left_came, right, right_came, over_2, over_4, own, first, second):
    size = own.shape[0]
    half = size // 2
    places = [
        ((own, 0), (own, half)),
        ((over_2, 0), (second, 0)),
        ((first, 0), (over_4, 0)),
        ((over_2, half), (over_4, half)),
    ]
    for number, pair in enumerate(places):
        at = slice(number * size, (number + 1) * size)
        product = dot(left[:, at], right[...], 0, 0) + dot(left_came[:, at], right_came[...], 0, 0)
        for part, (out, start) in enumerate(pair):
            out[start : start + half, :] = product[part * half : (part + 1) * half].astype(BF)


def outer(left, left_came, right, right_came):
    size, width = left.shape[1] // 4, right.shape[1]
    whole, half = (jax.ShapeDtypeStruct((rows, width), BF) for rows in (size, size // 2))
    return pl.pallas_call(
        outer_kernel,
        out_shape=(whole, whole, whole, half, half),
        in_specs=[vmem()] * 4,
        out_specs=[vmem()] * 5,
        compiler_params=params(),
        cost_estimate=cost(5_000_000_000, 15_000_000),
        name="outer",
    )(left, left_came, right, right_came)


def start_copies(pairs, sems):
    copies = [pltpu.make_async_copy(a, b, sems.at[i]) for i, (a, b) in enumerate(pairs)]
    for copy in copies:
        copy.start()

    def wait():
        for copy in copies:
            copy.wait()

    return wait


def expand_kernel(n_own, n_piece, places, flags, *refs):
    att, w_out = refs[:n_own], refs[n_own : 2 * n_own]
    tokens, gain_ffn = refs[2 * n_own : 2 * n_own + 2]
    pieces, rest = refs[2 * n_own + 2 : 2 * n_own + 2 + n_piece], refs[2 * n_own + 2 + n_piece :]
    *posts, factors, slope_out, middle_out, mid_out, inner_out = rest[:7]
    weight, act, own, slope, middle, mid_low, inner_t, sems, own_sem, *out_sems = rest[7:]
    rows, width = middle.shape
    start = pl.multiple_of(flags[1] * rows, rows)
    own_copy = pltpu.make_async_copy(tokens.at[pl.ds(start, rows), :], own, own_sem)
    own_copy.start()
    local = att[0].shape[0]
    hidden = weight.shape[0]
    chunk = width
    wait = fetch(pieces, places, weight, sems)

    average, inner_factor = inner_stats(att, width)
    for place, piece in enumerate(att):
        hat = (piece[...].astype(F32) - average) * inner_factor
        inner_t[place * local : (place + 1) * local, :] = hat.astype(BF)
    waits = [start_copies([(inner_t, inner_out)], out_sems[0])]
    branch = dot(inner_t[0:local, :], w_out[0][...], 0, 0)
    for place in range(1, n_own):
        branch += dot(inner_t[place * local : (place + 1) * local, :], w_out[place][...], 0, 0)
    own_copy.wait()
    total = own[...].astype(F32) + branch
    middle[...] = total
    mid_low[...] = (row_norm(total)[0] * gain_ffn[...].astype(F32).reshape(1, -1)).astype(BF)
    waits.append(start_copies([(middle, middle_out), (mid_low, mid_out)], out_sems[1]))
    wait()
    for start in range(0, hidden, chunk):
        to = slice(start, start + chunk)
        a, s = gelu_parts(dot(mid_low[...], weight[to, :], 1, 1))
        act[:, to] = a
        slope[:, to] = s.astype(BF)
    waits.append(start_copies([(slope, slope_out)], out_sems[2]))
    n, factor = row_norm(act[...])
    for number, post in enumerate(posts):
        post[...] = n[:, number * hidden // 2 : (number + 1) * hidden // 2].astype(BF)
    factors[...] = jnp.broadcast_to(factor, (rows, 128))
    for wait in waits:
        wait()


def expand_ffn(flags, att, w_out, tokens, gain_ffn, expand, places):
    rows, width = att[0].shape[1], tokens.shape[1]
    hidden = sum(e.shape[0] for e in expand)
    n_own = len(att)
    local = att[0].shape[0]
    return pl.pallas_call(
        partial(expand_kernel, n_own, len(expand), places),
        out_shape=(
            jax.ShapeDtypeStruct((rows, hidden // 2), BF),
            jax.ShapeDtypeStruct((rows, hidden // 2), BF),
            jax.ShapeDtypeStruct((rows, 128), F32),
            jax.ShapeDtypeStruct((rows, hidden), BF),
            jax.ShapeDtypeStruct((rows, width), F32),
            jax.ShapeDtypeStruct((rows, width), BF),
            jax.ShapeDtypeStruct((n_own * local, rows), BF),
        ),
        in_specs=[smem()]
        + [vmem()] * (2 * n_own)
        + [anywhere(), vmem()]
        + [anywhere()] * len(expand),
        out_specs=[vmem()] * 3 + [anywhere()] * 4,
        scratch_shapes=[
            pltpu.VMEM((hidden, width), BF),
            pltpu.VMEM((rows, hidden), F32),
            pltpu.VMEM((rows, width), BF),
            pltpu.VMEM((rows, hidden), BF),
            pltpu.VMEM((rows, width), F32),
            pltpu.VMEM((rows, width), BF),
            pltpu.VMEM((n_own * local, rows), BF),
            pltpu.SemaphoreType.DMA((len(places),)),
            pltpu.SemaphoreType.DMA,
            pltpu.SemaphoreType.DMA((1,)),
            pltpu.SemaphoreType.DMA((2,)),
            pltpu.SemaphoreType.DMA((1,)),
        ],
        compiler_params=params(),
        cost_estimate=cost(12000000000, 36000000),
        name="expand_ffn",
    )(flags, *att, *w_out, tokens, gain_ffn, *expand)


def reduce_kernel(n_piece, places, *refs):
    posts, (slope, factors, middle, cotangent), rest = refs[:2], refs[2:6], refs[6:]
    pieces, (output, *grads, weight, d_post, sems) = rest[:n_piece], rest[n_piece:]
    hidden, width = weight.shape
    half = hidden // 2
    fetch(pieces, places, weight, sems)()
    total = middle[...]
    for start in range(0, hidden, width):
        at = slice(start % half, start % half + width)
        rows = slice(start, start + width)
        d_post[:, rows] = dot(cotangent[...], weight[rows, :], 1, 1)
        total = total + dot(posts[start // half][:, at], weight[rows, :], 1, 0)
    output[...] = total.astype(BF)
    mean_e, mean_en = 0.0, 0.0
    for number, post in enumerate(posts):
        e = d_post[:, number * half : (number + 1) * half]
        mean_e = mean_e + jnp.sum(e, axis=1, keepdims=True) / hidden
        mean_en = mean_en + jnp.sum(e * post[...].astype(F32), axis=1, keepdims=True) / hidden
    for number, (post, grad) in enumerate(zip(posts, grads)):
        at = slice(number * half, (number + 1) * half)
        back = d_post[:, at] - mean_e - post[...].astype(F32) * mean_en
        grad[...] = (factors[:, 0:1] * back * slope[:, at].astype(F32)).astype(BF)


def reduce_ffn(posts, slope, factors, middle, cotangent, reduced, places):
    rows, width = middle.shape
    hidden = slope.shape[1]
    return pl.pallas_call(
        partial(reduce_kernel, len(reduced), places),
        out_shape=(
            jax.ShapeDtypeStruct((rows, width), BF),
            jax.ShapeDtypeStruct((rows, hidden // 2), BF),
            jax.ShapeDtypeStruct((rows, hidden // 2), BF),
        ),
        in_specs=[vmem()] * 6 + [anywhere()] * len(reduced),
        out_specs=[vmem()] * 3,
        scratch_shapes=[
            pltpu.VMEM((hidden, width), BF),
            pltpu.VMEM((rows, hidden), F32),
            pltpu.SemaphoreType.DMA((len(places),)),
        ],
        compiler_params=params(),
        cost_estimate=cost(15_000_000_000, 45_000_000),
        name="reduce_ffn",
    )(*posts, slope, factors, middle, cotangent, *reduced)


def middle_kernel(n_own, n_piece, places, *refs):
    att, w_out = refs[:n_own], refs[n_own : 2 * n_own]
    *hidden_grads, middle, cotangent, inner_t, gain_ffn = refs[2 * n_own : 2 * n_own + 6]
    rest = refs[2 * n_own + 6 :]
    pieces, rest = rest[:n_piece], rest[n_piece:]
    middle_grad, ffn_sum, sent, kept = rest[:4]
    grads = rest[4 : 4 + n_own]
    weight, branch_grad, e_buf, sems = rest[4 + n_own :]
    rows, width = middle.shape
    local = att[0].shape[0]
    half = weight.shape[0] // 2
    gain_row = gain_ffn[...].astype(F32).reshape(1, -1)
    wait = fetch(pieces, places, weight, sems)
    n, factor = row_norm(middle[...])
    average, inner_factor = inner_stats(att, width)
    wait()
    grad = dot(hidden_grads[0][...], weight[0:half, :], 1, 0)
    grad = grad + dot(hidden_grads[1][...], weight[half:, :], 1, 0)
    ffn_sum[...] = jnp.sum((grad * n).reshape(rows // 8, 8, width), axis=0)
    e = grad * gain_row
    back = factor * (
        e - jnp.mean(e, axis=1, keepdims=True) - n * jnp.mean(e * n, axis=1, keepdims=True)
    )
    full = cotangent[...].astype(F32) + back
    middle_grad[...] = full
    branch_grad[...] = full.astype(BF)

    grad_sum = jnp.zeros((1, rows), F32)
    cross_sum = jnp.zeros((1, rows), F32)
    for place in range(n_own):
        e = dot(w_out[place][...], branch_grad[...], 1, 1)
        e_buf[place] = e
        grad_sum = grad_sum + jnp.sum(e, axis=0, keepdims=True)
        hat = (att[place][...].astype(F32) - average) * inner_factor
        cross_sum = cross_sum + jnp.sum(e * hat, axis=0, keepdims=True)
    for place in range(n_own):
        hat = (att[place][...].astype(F32) - average) * inner_factor
        grad = inner_factor * (e_buf[place] - grad_sum / width - hat * (cross_sum / width))
        grads[place][...] = grad.astype(BF)
        target = sent if place % 2 else kept
        at = slice(place * local, (place + 1) * local)
        target[place // 2] = dot(inner_t[at, :], branch_grad[...], 1, 0).astype(BF)


def middle_back(att, w_out, hidden_grads, middle, cotangent, inner_t, gain_ffn, expand, places):
    rows, width = middle.shape
    hidden = 2 * hidden_grads[0].shape[1]
    n_own = len(att)
    local = att[0].shape[0]
    return pl.pallas_call(
        partial(middle_kernel, n_own, len(expand), places),
        out_shape=(
            jax.ShapeDtypeStruct((rows, width), F32),
            jax.ShapeDtypeStruct((8, width), F32),
            jax.ShapeDtypeStruct((n_own // 2, local, width), BF),
            jax.ShapeDtypeStruct((n_own // 2, local, width), BF),
        )
        + (jax.ShapeDtypeStruct((local, rows), BF),) * n_own,
        in_specs=[vmem()] * (2 * n_own + 6) + [anywhere()] * len(expand),
        out_specs=[vmem()] * (4 + n_own),
        scratch_shapes=[
            pltpu.VMEM((hidden, width), BF),
            pltpu.VMEM((rows, width), BF),
            pltpu.VMEM((n_own, local, rows), F32),
            pltpu.SemaphoreType.DMA((len(places),)),
        ],
        compiler_params=params(),
        cost_estimate=cost(12_500_000_000, 37_500_000),
        name="middle_back",
    )(*att, *w_out, *hidden_grads, middle, cotangent, inner_t, gain_ffn, *expand)


def input_gradient_kernel(
    flags, kept, came, first, second, tokens, gain, middle_grad, out, own, sem
):
    rows = out.shape[0]
    start = pl.multiple_of(flags[1] * rows, rows)
    copy = pltpu.make_async_copy(tokens.at[pl.ds(start, rows), :], own, sem)
    copy.start()
    last = jnp.concatenate([first[...], second[...]], axis=0)
    total = kept[0].astype(F32) + came[0].astype(F32) + last.astype(F32)
    e = total.T * gain[...].astype(F32).reshape(1, -1)
    copy.wait()
    n, factor = row_norm(own[...].astype(F32))
    back = factor * (
        e - jnp.mean(e, axis=1, keepdims=True) - n * jnp.mean(e * n, axis=1, keepdims=True)
    )
    out[...] = (middle_grad[...] + back).astype(BF)


def input_gradient(flags, terms, tokens, gain, middle_grad):
    kept, came, first, second = terms
    block = pl.BlockSpec((1,) + kept.shape[1:], lambda i: (0, 0, 0))

    def whole(v):
        return pl.BlockSpec(v.shape, lambda i: (0,) * v.ndim)

    return pl.pallas_call(
        input_gradient_kernel,
        grid=(1,),
        out_shape=jax.ShapeDtypeStruct(middle_grad.shape, BF),
        in_specs=[smem(), block, block, whole(first), whole(second), anywhere()]
        + [whole(gain), whole(middle_grad)],
        out_specs=whole(middle_grad),
        scratch_shapes=[pltpu.VMEM(middle_grad.shape, BF), pltpu.SemaphoreType.DMA],
        compiler_params=params(),
        cost_estimate=cost(4500000000, 13500000),
        name="input_gradient",
    )(flags, *terms, tokens, gain, middle_grad)


def body(
    tokens,
    w_query,
    w_key,
    w_value,
    w_output,
    gain_attn,
    gain_inner,
    gain_ffn,
    w_expand,
    w_reduce,
    gain_hidden,
    cotangent,
    seq_length,
    seq_group,
):
    n_batch, n_own = lax.axis_size("batch"), lax.axis_size("heads")
    n_all = n_batch * n_own
    mine = lax.axis_index("heads")
    quarter = cotangent.shape[0]
    width = tokens.shape[1]
    local = w_query.shape[1]
    n_heads = local // HD

    def swap(value, bit):
        return lax.ppermute(value, AXES, [(i, i ^ bit) for i in range(n_all)])

    flags = jnp.stack([lax.axis_index("batch"), mine]).astype(jnp.int32)
    table = (seq_length, seq_group)
    far = [1 << b for b in range(3, n_all.bit_length() - 1)]
    near = (2, 4, 6)

    def parts(value, offsets):
        return [value] + [swap(value, off) for off in offsets]

    def around(value, offsets):
        return jnp.concatenate(parts(value, offsets), axis=0)

    def far_steps(value):
        for bit in reversed(far):
            value = around(value, (bit,))
            yield value

    def add(values):
        return sum(v.astype(F32) for v in values)

    phase = lax.optimization_barrier

    def sum_begin(value):
        rows = value.shape[0]
        value = lax.all_to_all(value, "batch", 0, 0, tiled=True)
        return value.reshape(n_batch, rows // n_batch, width)

    def sum_middle(value):
        return jnp.sum(value.astype(F32), axis=0)

    def sum_end(share):
        share = jnp.broadcast_to(share.astype(BF)[None], (n_batch,) + share.shape)
        return lax.all_to_all(share, "batch", 0, 0, tiled=True)

    def last(steps):
        *_, value = steps
        return value

    w_t = jnp.concatenate([w_query.T, w_key.T, w_value.T], axis=0)
    w_reduce_scaled = (w_reduce.astype(F32) * gain_hidden.astype(F32)[:, None]).astype(BF)
    w_output_scaled = (w_output.astype(F32) * gain_inner.astype(F32)[:, None]).astype(BF)

    if len(far) == 2:
        expand_far = parts(w_expand, (far[1], far[0], far[0] | far[1]))
    else:
        expand_far = [last(far_steps(w_expand))]
    reduced = w_reduce_scaled
    for bit in far[:0:-1]:
        reduced = parts(jnp.concatenate(reduced) if isinstance(reduced, list) else reduced, (bit,))
    w_out_y = swap(w_output_scaled, 2)
    pre, qkv = project(tokens, w_t, gain_attn, [])
    expand_far, reduced, w_out_y, pre, qkv = phase((expand_far, reduced, w_out_y, pre, qkv))

    expand = parts(jnp.concatenate(expand_far), near)
    reduced = parts(jnp.concatenate(reduced), (far[0],))
    w_out_c = swap(jnp.stack([w_output_scaled, w_out_y]), 1)
    lse, *pieces = attend(flags, table, qkv, n_own, [])
    reduced, w_out_c, lse, pieces = phase((reduced, w_out_c, lse, pieces))

    att = [pieces[0]] + [swap(pieces[k], k) for k in range(1, n_own)]
    expand, att = phase((expand, att))
    expand = jnp.concatenate(expand)
    expand = [expand, swap(expand, 1)]
    reduced = jnp.concatenate(reduced)
    half = reduced.shape[0] // 2
    first = [swap(reduced[:half], 4), swap(reduced[half:], 2)]
    w_out = [w_output_scaled, w_out_c[0], w_out_y, w_out_c[1]]
    att, expand, reduced, first, w_out, cotangent = phase(
        (att, expand, reduced, first, w_out, cotangent)
    )
    cot_came = swap(cotangent, 1)

    def stacked(parts):
        starts = [sum(p.shape[0] for p in parts[:i]) for i in range(len(parts))]
        return [(i, 0, start, p.shape[0]) for i, (start, p) in enumerate(zip(starts, parts))]

    places = stacked(expand)
    second = [
        swap(jnp.concatenate([reduced[:half], first[0]]), 2),
        swap(jnp.concatenate([reduced[half:], first[1]]), 4),
    ]
    *posts, factors, slope, middle, mid_low, inner_t = expand_ffn(
        flags, att, w_out, tokens, gain_ffn, expand, places
    )
    reduced, posts, slope, factors, middle, mid_low, inner_t, cot_came = phase(
        ([reduced, *first, *second], posts, slope, factors, middle, mid_low, inner_t, cot_came)
    )

    starts = [(0, 0, 0), (0, half, 1), (1, 0, 4), (2, 0, 3)]
    starts += [(3, 0, 2), (3, half, 6), (4, 0, 5), (4, half, 7)]
    reduce_places = [
        (number + core * 5, start, core * 8 * half + at * half, half)
        for core in range(2)
        for number, start, at in starts
    ]
    post_came = swap(posts[1], 1)
    reduced = reduced + [swap(r, 1) for r in reduced]
    d_reduce = outer(posts[0], post_came, cotangent, cot_came)
    reduced, posts, mid_low, d_reduce = phase((reduced, posts, mid_low, d_reduce))

    def near_begin(products):
        return swap(products[0], 2), swap(products[1], 4)

    def near_middle(products, came):
        half = came[0].shape[0] // 2
        terms = [add((p, c[half:])).astype(BF) for p, c in zip(products[3:], came)]
        return came, (swap(terms[0], 4), swap(terms[1], 2))

    def near_end(products, begun, came):
        half = came[0].shape[0]
        return [
            add((products[2][i * half : (i + 1) * half], b[:half], c))
            for i, (b, c) in enumerate(zip(begun, came))
        ]

    begun_r = near_begin(d_reduce)
    mid_came = swap(mid_low, 1)
    output, *hidden_grads = reduce_ffn(
        posts, slope, factors, middle, cotangent, reduced, reduce_places
    )
    output, hidden_grads, begun_r, d_reduce, mid_came = phase(
        (output, hidden_grads, begun_r, d_reduce, mid_came)
    )

    begun_r, came_r = near_middle(d_reduce, begun_r)
    grad_came = swap(hidden_grads[1], 1)
    middle_grad, ffn_sum, d_sent, d_kept, *att_grads = middle_back(
        att, w_out, hidden_grads, middle, cotangent, inner_t, gain_ffn, expand, places
    )
    came_r, grad_came, middle_grad, ffn_sum, d_sent, d_kept, att_grads = phase(
        (came_r, grad_came, middle_grad, ffn_sum, d_sent, d_kept, att_grads)
    )

    def far_sum(value, bit):
        return value[0], swap(value[1].astype(BF), bit)

    def halves(value):
        return value.reshape(2, -1, width)

    grads = [att_grads[0]] + [swap(att_grads[k], k) for k in range(1, n_own)]
    d_came = swap(d_sent, 1)
    d_came, mid_came, begun_r, came_r = phase((d_came, mid_came, begun_r, came_r))
    d_reduce = far_sum(near_end(d_reduce, begun_r, came_r), far[0])
    d_expand = outer(hidden_grads[0], grad_came, mid_low, mid_came)
    d_reduce, grads, d_expand, d_came = phase((d_reduce, grads, d_expand, d_came))

    back = partial(attend_back, flags, table, qkv)

    begun_e = near_begin(d_expand)
    for bit in far[1:]:
        d_reduce = far_sum(halves(add(d_reduce)), bit)
    d_last = swap(add((d_kept[1], d_came[1])).astype(BF), 2)
    back_0 = back(0, lse, pre, w_t, pieces, grads)
    back_0, d_reduce, begun_e, d_expand, d_last, grads = phase(
        (back_0, d_reduce, begun_e, d_expand, d_last, grads)
    )

    d_own = add((d_kept[0], d_came[0], d_last)).astype(BF)
    share_0 = sum_begin(jnp.concatenate([back_0[1], d_own]))
    begun_e, came_e = near_middle(d_expand, begun_e)
    back_1 = back(1, lse, pre, w_t, pieces, grads)
    back_1, came_e, share_0, grads = phase((back_1, came_e, share_0, grads))

    batch_bits = [1 << b for b in range(n_batch.bit_length() - 1)][::-1]

    def gather_step(value, bit):
        return value, swap(value, bit * n_own)

    def joined(pair, bit):
        axis = batch_bits.index(bit)
        mine_first = (lax.axis_index("batch") & bit) == 0
        return jnp.where(
            mine_first, jnp.concatenate(pair, axis), jnp.concatenate(pair[::-1], axis)
        )

    d_expand = near_end(d_expand, begun_e, came_e)
    if len(far) == 2:
        blocks = [v.astype(BF) for part in d_expand for v in halves(part)]
        offs = (far[1], far[0], far[0] | far[1])
        d_expand = [halves(d_expand[0])[0]] + [swap(b, o) for b, o in zip(blocks[1:], offs)]
    else:
        d_expand = far_sum(d_expand, far[0])
        for bit in far[1:]:
            d_expand = far_sum(halves(add(d_expand)), bit)
    share_0 = sum_middle(share_0).astype(BF)
    share_0 = gather_step(share_0.reshape((1,) * len(batch_bits) + share_0.shape), batch_bits[0])
    earlier = (back_0[0], back_1[0])
    back_2 = back(2, lse, pre, w_t, pieces, grads, d_before=back_1[1], earlier=earlier)
    back_2, d_expand, share_0 = phase((back_2, d_expand, share_0))

    share_1 = sum_begin(back_2[1])
    small = jnp.sum(jnp.stack([back_0[2] + back_1[2] + back_2[2], ffn_sum]), axis=1)
    small = small + swap(small, 1)
    small = small + swap(small, 2)
    sent, kept = back_2[3:]
    came = swap(sent, 1)
    came, kept, small = phase((came, kept, small))
    split = width // 2
    terms = [
        add((kept[1, at], came[1, at])).astype(BF)
        for at in (slice(0, split), slice(split, width))
    ]
    first = swap(terms[0], 2)
    for bit, later in zip(batch_bits[:-1], batch_bits[1:-1]):
        share_0 = gather_step(joined(share_0, bit), later)
    share_1, share_0, first, terms, d_expand = phase((share_1, share_0, first, terms, d_expand))

    second = [first, swap(terms[1], 2)]
    share_1 = sum_middle(share_1)
    count = share_1.shape[0]
    total_1 = sum_end(jnp.concatenate([share_1, small], axis=0))
    share_0 = gather_step(joined(share_0, batch_bits[-2]), batch_bits[-1])
    grad_tokens = input_gradient(
        flags, (kept, came, *second), tokens, gain_attn, middle_grad
    )
    grad_tokens, share_0, d_reduce, d_expand = phase((grad_tokens, share_0, d_reduce, d_expand))
    d_expand = add(d_expand)
    d_reduce = add(d_reduce)
    g_hidden = jnp.sum(d_reduce * w_reduce.astype(F32), axis=1)
    d_reduce = d_reduce * gain_hidden.astype(F32)[:, None]

    total_0 = joined(share_0, batch_bits[-1]).astype(F32).reshape(-1, width)
    total_1 = total_1.astype(F32)
    small = jnp.sum(total_1[:, count:], axis=0)
    total_1 = total_1[:, :count].reshape(-1, width)
    totals = [total_0, total_1[: 3 * HD], total_1[3 * HD :]]
    def weight_grad(place):
        at = slice(place * HD, (place + 1) * HD)
        return jnp.concatenate([t[at] for t in totals], axis=0).T

    g_out = totals[0][3 * HD :]
    return (
        output,
        grad_tokens,
        weight_grad(0),
        weight_grad(1),
        weight_grad(2),
        g_out * gain_inner.astype(F32)[:, None],
        small[0] / gain_attn.astype(F32),
        jnp.sum(g_out * w_output.astype(F32), axis=1),
        small[1],
        d_expand,
        d_reduce,
        g_hidden,
    )


def solution(mesh):
    both = P(AXES, None)
    return jax.shard_map(
        body,
        mesh=mesh,
        in_specs=(
            P("batch", None),
            P(None, "heads"),
            P(None, "heads"),
            P(None, "heads"),
            P("heads", None),
            P(),
            P("heads"),
            P(),
            both,
            both,
            P(AXES),
            both,
            P(),
            P(),
        ),
        out_specs=(
            both,
            both,
            P(None, "heads"),
            P(None, "heads"),
            P(None, "heads"),
            P("heads", None),
            P(),
            P("heads"),
            P(),
            both,
            both,
            P(AXES),
        ),
        check_vma=False,
    )
```

```python
from functools import partial

import jax
import jax.numpy as jnp
from jax import lax
from jax.experimental import pallas as pl
from jax.experimental.pallas import tpu as pltpu
from jax.sharding import PartitionSpec as P

HD = 64
SHORT = 512
EPSILON = 1e-05
MASKED = -1e30
AXES = ("batch", "heads")
BF = jnp.bfloat16
F32 = jnp.float32
VMEM_LIMIT = 60 * 1024 * 1024


def dot(left, right, left_dim, right_dim):
    return lax.dot_general(
        left, right, (((left_dim,), (right_dim,)), ((), ())), preferred_element_type=F32
    )


def params(limit=VMEM_LIMIT):
    return pltpu.CompilerParams(vmem_limit_bytes=limit)


def vmem():
    return pl.BlockSpec(memory_space=pltpu.VMEM)


def smem():
    return pl.BlockSpec(memory_space=pltpu.SMEM)


def anywhere():
    return pl.BlockSpec(memory_space=pl.ANY)


def cost(flops, moved, special=0):
    return pl.CostEstimate(flops=flops, bytes_accessed=moved, transcendentals=special)


def project_kernel(n_after, tokens, w_t, gain, *rest):
    pre, qkv = rest[n_after:]
    rows = tokens.shape[0]
    local = w_t.shape[0] // 3
    gain_row = gain[...].astype(F32).reshape(1, -1)
    for block in range(rows // SHORT):
        at = slice(block * SHORT, (block + 1) * SHORT)
        low = (row_norm(tokens[at, :].astype(F32))[0] * gain_row).astype(BF)
        pre[at, :] = low
        product = dot(w_t[...], low, 1, 1)
        qkv[0:local, at] = (product[0:local] * HD ** (-0.5)).astype(BF)
        qkv[local:, at] = product[local:].astype(BF)


def project(tokens, w_t, gain, after):
    rows, width = tokens.shape
    return pl.pallas_call(
        partial(project_kernel, len(after)),
        out_shape=(
            jax.ShapeDtypeStruct((rows, width), BF),
            jax.ShapeDtypeStruct((w_t.shape[0], rows), BF),
        ),
        in_specs=[vmem()] * 3 + [anywhere()] * len(after),
        out_specs=[vmem()] * 2,
        compiler_params=params(),
        cost_estimate=cost(7000000000, 21000000),
        name="project",
    )(tokens, w_t, gain, *after)


def holds_long(flags, seq_length, seq_group):
    def look(i, found):
        here = (seq_group[i] == flags[0]) & (seq_length[i] > SHORT)
        return jnp.where(here, 1, found)

    return lax.fori_loop(0, seq_length.shape[0], look, 0)


def column_max(values):
    return jnp.max(values.reshape(values.shape[0] // 8, 8, SHORT), axis=0)


def column_sum(values):
    return jnp.sum(values.reshape(values.shape[0] // 8, 8, SHORT), axis=0)


def attend_kernel(n_after, n_out, flags, seq_length, seq_group, qkv, *rest):
    lse, *outs, att = rest[n_after:]
    local = qkv.shape[0] // 3
    heads = local // HD
    blocks = qkv.shape[1] // SHORT
    is_long, mine = holds_long(flags, seq_length, seq_group), flags[1]
    key_place = lax.broadcasted_iota(jnp.int32, (SHORT, SHORT), 0)
    query_place = lax.broadcasted_iota(jnp.int32, (SHORT, SHORT), 1)

    def run_path(long_path):
        def one_head(head, unused):
            at = pl.ds(pl.multiple_of(head * HD, HD), HD)
            k_at = pl.ds(pl.multiple_of(local + head * HD, HD), HD)
            v_at = pl.ds(pl.multiple_of(2 * local + head * HD, HD), HD)
            for block in range(blocks):
                q_t = qkv[at, block * SHORT : (block + 1) * SHORT]
                keys = [
                    slice(index * SHORT, (index + 1) * SHORT)
                    for index in range(0 if long_path else block, block + 1)
                ]
                parts = [dot(qkv[k_at, key], q_t, 0, 0) for key in keys]
                parts[-1] = jnp.where(key_place <= query_place, parts[-1], MASKED)
                largest = column_max(parts[0])
                for s in parts[1:]:
                    largest = jnp.maximum(largest, column_max(s))
                top = jnp.max(largest, axis=0, keepdims=True)
                total, out = 0.0, 0.0
                for key, s in zip(keys, parts):
                    p = jnp.exp(s - top)
                    total = total + column_sum(p)
                    out = out + dot(qkv[v_at, key], p.astype(BF), 1, 0)
                total = jnp.sum(total, axis=0, keepdims=True)
                att[block, at, :] = (out / total).astype(BF)
                lse[head, block] = jnp.broadcast_to(top + jnp.log(total), (8, SHORT))
            return unused

        lax.fori_loop(0, heads, one_head, 0)

    pl.when(is_long > 0)(lambda: run_path(True))
    pl.when(is_long == 0)(lambda: run_path(False))
    for place in range(n_out):
        outs[place][...] = att[mine ^ place]


def attend(flags, table, qkv, n_out, after):
    rows = qkv.shape[1]
    blocks = rows // SHORT
    local = qkv.shape[0] // 3
    return pl.pallas_call(
        partial(attend_kernel, len(after), n_out),
        out_shape=(jax.ShapeDtypeStruct((local // HD, blocks, 8, SHORT), F32),)
        + (jax.ShapeDtypeStruct((local, SHORT), BF),) * n_out,
        in_specs=[smem()] * 3 + [vmem()] + [anywhere()] * len(after),
        out_specs=[vmem()] * (1 + n_out),
        scratch_shapes=[pltpu.VMEM((blocks, local, SHORT), BF)],
        compiler_params=params(),
        cost_estimate=cost(15000000000, 45000000),
        name="attend",
    )(flags, *table, qkv, *after)


def attend_back_kernel(n_own, n_late, *refs):
    flags, seq_length, seq_group, q_all, k_all, v_all, lse, w_q, w_k, w_v = refs[:10]
    att, grads, rest = refs[10 : 10 + n_own], refs[10 + n_own : 10 + 2 * n_own], refs[10 + 2 * n_own :]
    late, (d_qkv, d_weight, attn_sum, *rest) = rest[:n_late], rest[n_late:]
    if n_late > 1:
        sent, kept, *rest = rest
    ag, delta, sems, *here = rest
    copies = [pltpu.make_async_copy(v, h, sems.at[n]) for n, (v, h) in enumerate(zip(late, here))]
    for copy in copies:
        copy.start()
    pre, *here = here
    rows, width = pre.shape
    blocks = rows // SHORT
    is_long, mine = holds_long(flags, seq_length, seq_group), flags[1]

    for place in range(n_own):
        grad = grads[place][...]
        ag[mine ^ place] = grad
        product = grad.astype(F32) * att[place][...].astype(F32)
        delta[mine ^ place] = jnp.broadcast_to(jnp.sum(product, axis=0, keepdims=True), (8, SHORT))

    half = SHORT // 2

    def pair(k_t, v_t, index, first, masked):
        q_t = q_all[:, index * SHORT + first : (index + 1) * SHORT]
        grad = ag[index][:, first:]
        p = jnp.exp(dot(k_t, q_t, 0, 0) - lse[0, index][0:1, first:])
        if masked:
            key_place = lax.broadcasted_iota(jnp.int32, p.shape, 0)
            p = jnp.where(key_place <= lax.broadcasted_iota(jnp.int32, p.shape, 1), p, 0.0)
        d_p = dot(v_t, grad, 0, 0)
        d_s = (p * (d_p - delta[index][0:1, first:])).astype(BF)
        p = p.astype(BF)
        return dot(k_t, d_s, 1, 0), dot(q_t, d_s, 1, 1), dot(grad, p, 1, 1)

    def run_path(long_path):
        d_q = [None] * blocks
        for block in range(blocks):
            k_cols = slice(block * SHORT, (block + 1) * SHORT)
            k_t = k_all[:, k_cols]
            v_t = v_all[:, k_cols]
            q_1, k_1, v_1 = pair(k_t[:, :half], v_t[:, :half], block, 0, True)
            q_2, k_2, v_2 = pair(k_t[:, half:], v_t[:, half:], block, half, True)
            add = jnp.concatenate([q_1[:, :half], q_1[:, half:] + q_2], axis=1)
            d_q[block] = add if d_q[block] is None else d_q[block] + add
            d_k = jnp.concatenate([k_1, k_2], axis=1)
            d_v = jnp.concatenate([v_1, v_2], axis=1)
            for index in range(block + 1, blocks if long_path else block + 1):
                add_q, add_k, add_v = pair(k_t, v_t, index, 0, False)
                d_q[index] = add_q if d_q[index] is None else d_q[index] + add_q
                d_k = d_k + add_k
                d_v = d_v + add_v
            d_qkv[HD : 2 * HD, k_cols] = d_k.astype(BF)
            d_qkv[2 * HD :, k_cols] = d_v.astype(BF)
        for block in range(blocks):
            d_qkv[0:HD, block * SHORT : (block + 1) * SHORT] = (d_q[block] * HD ** (-0.5)).astype(BF)

    pl.when(is_long > 0)(lambda: run_path(True))
    pl.when(is_long == 0)(lambda: run_path(False))
    for copy in copies:
        copy.wait()
    product = dot(d_qkv[...], pre[...], 1, 0)
    start = d_weight.shape[0] - 3 * HD
    d_weight[start:, :] = product.astype(BF)
    cross = jnp.zeros((8, width), F32)
    for place, weight in enumerate((w_q, w_k, w_v)):
        part = product[place * HD : (place + 1) * HD] * weight[...].astype(F32)
        cross = cross + jnp.sum(part.reshape(HD // 8, 8, width), axis=0)
    attn_sum[...] = cross
    if n_late > 1:
        w_t, d_before, *earlier = here
        d_weight[0:start, :] = d_before[...]
        for place in range(n_own):
            cols = pl.ds(pl.multiple_of((mine ^ place) * SHORT, SHORT), SHORT)
            joined = [d[i * HD : (i + 1) * HD, cols] for i in range(3) for d in (*earlier, d_qkv)]
            grad = dot(w_t[...], jnp.concatenate(joined, axis=0), 0, 0)
            target = sent if place % 2 else kept
            target[place // 2] = grad.astype(BF)


def attend_back(flags, table, qkv, head, lse, pre, w_t, att, grads, d_before=None, earlier=()):
    rows, width = pre.shape
    blocks = rows // SHORT
    heads = qkv.shape[0] // (3 * HD)
    n_own = len(att)

    def part(place, columns):
        return pl.BlockSpec((HD, columns), lambda i, at=place: (at, 0))

    def whole(struct):
        return pl.BlockSpec(struct.shape, lambda i, n=len(struct.shape): (0,) * n)

    late = [pre, *([w_t, d_before, *earlier] if earlier else [])]
    weight_rows = 3 * HD + (d_before.shape[0] if earlier else 0)
    outs = (
        jax.ShapeDtypeStruct((3 * HD, rows), BF),
        jax.ShapeDtypeStruct((weight_rows, width), BF),
        jax.ShapeDtypeStruct((8, width), F32),
    )
    if earlier:
        outs += (jax.ShapeDtypeStruct((n_own // 2, width, SHORT), BF),) * 2
    return pl.pallas_call(
        partial(attend_back_kernel, n_own, len(late)),
        grid=(1,),
        out_shape=outs,
        in_specs=[smem()] * 3
        + [part(place * heads + head, rows) for place in range(3)]
        + [pl.BlockSpec((1,) + lse.shape[1:], lambda i: (head, 0, 0, 0))]
        + [part(place * heads + head, width) for place in range(3)]
        + [part(head, SHORT)] * (2 * n_own)
        + [anywhere()] * len(late),
        out_specs=[whole(o) for o in outs],
        scratch_shapes=[
            pltpu.VMEM((blocks, HD, SHORT), BF),
            pltpu.VMEM((blocks, 8, SHORT), F32),
            pltpu.SemaphoreType.DMA((len(late),)),
        ]
        + [pltpu.VMEM(v.shape, BF) for v in late],
        compiler_params=params(),
        cost_estimate=cost(11_500_000_000, 34_500_000),
        name="attend_back",
    )(flags, *table, qkv, qkv, qkv, lse, w_t, w_t, w_t, *att, *grads, *late)


def gelu_parts(h):
    phi = jnp.exp(h * h * (-0.5)) * 0.3989422804014327
    big = 0.5 * lax.erf(h * 0.7071067811865476) + 0.5
    return h * big, big + h * phi


def inner_stats(att, width):
    total = sum(jnp.sum(piece[...].astype(F32), axis=0, keepdims=True) for piece in att)
    average = total / width
    square = 0.0
    for piece in att:
        centred = piece[...].astype(F32) - average
        square = square + jnp.sum(centred * centred, axis=0, keepdims=True)
    return average, lax.rsqrt(square / width + EPSILON)


def row_norm(x):
    centred = x - jnp.mean(x, axis=1, keepdims=True)
    factor = lax.rsqrt(jnp.mean(centred * centred, axis=1, keepdims=True) + EPSILON)
    return centred * factor, factor


def fetch(pieces, places, target, sems):
    copies = [
        pltpu.make_async_copy(
            pieces[number].at[pl.ds(start, rows), :], target.at[pl.ds(to, rows), :], sems.at[i]
        )
        for i, (number, start, to, rows) in enumerate(places)
    ]
    for copy in copies:
        copy.start()

    def wait():
        for copy in copies:
            copy.wait()

    return wait


def outer_kernel(left, left_came, right, right_came, over_2, over_4, own, first, second):
    size = own.shape[0]
    half = size // 2
    places = [
        ((own, 0), (own, half)),
        ((over_2, 0), (second, 0)),
        ((first, 0), (over_4, 0)),
        ((over_2, half), (over_4, half)),
    ]
    for number, pair in enumerate(places):
        at = slice(number * size, (number + 1) * size)
        product = dot(left[:, at], right[...], 0, 0) + dot(left_came[:, at], right_came[...], 0, 0)
        for part, (out, start) in enumerate(pair):
            out[start : start + half, :] = product[part * half : (part + 1) * half].astype(BF)


def outer(left, left_came, right, right_came):
    size, width = left.shape[1] // 4, right.shape[1]
    whole, half = (jax.ShapeDtypeStruct((rows, width), BF) for rows in (size, size // 2))
    return pl.pallas_call(
        outer_kernel,
        out_shape=(whole, whole, whole, half, half),
        in_specs=[vmem()] * 4,
        out_specs=[vmem()] * 5,
        compiler_params=params(),
        cost_estimate=cost(5_000_000_000, 15_000_000),
        name="outer",
    )(left, left_came, right, right_came)


def start_copies(pairs, sems):
    copies = [pltpu.make_async_copy(a, b, sems.at[i]) for i, (a, b) in enumerate(pairs)]
    for copy in copies:
        copy.start()

    def wait():
        for copy in copies:
            copy.wait()

    return wait


def expand_kernel(n_own, n_piece, places, flags, *refs):
    att, w_out = refs[:n_own], refs[n_own : 2 * n_own]
    tokens, gain_ffn = refs[2 * n_own : 2 * n_own + 2]
    pieces, rest = refs[2 * n_own + 2 : 2 * n_own + 2 + n_piece], refs[2 * n_own + 2 + n_piece :]
    *posts, factors, slope_out, middle_out, mid_out, inner_out = rest[:7]
    weight, act, own, slope, middle, mid_low, inner_t, sems, own_sem, *out_sems = rest[7:]
    rows, width = middle.shape
    start = pl.multiple_of(flags[1] * rows, rows)
    own_copy = pltpu.make_async_copy(tokens.at[pl.ds(start, rows), :], own, own_sem)
    own_copy.start()
    local = att[0].shape[0]
    hidden = weight.shape[0]
    chunk = width
    wait = fetch(pieces, places, weight, sems)

    average, inner_factor = inner_stats(att, width)
    for place, piece in enumerate(att):
        hat = (piece[...].astype(F32) - average) * inner_factor
        inner_t[place * local : (place + 1) * local, :] = hat.astype(BF)
    waits = [start_copies([(inner_t, inner_out)], out_sems[0])]
    branch = dot(inner_t[0:local, :], w_out[0][...], 0, 0)
    for place in range(1, n_own):
        branch += dot(inner_t[place * local : (place + 1) * local, :], w_out[place][...], 0, 0)
    own_copy.wait()
    total = own[...].astype(F32) + branch
    middle[...] = total
    mid_low[...] = (row_norm(total)[0] * gain_ffn[...].astype(F32).reshape(1, -1)).astype(BF)
    waits.append(start_copies([(middle, middle_out), (mid_low, mid_out)], out_sems[1]))
    wait()
    for start in range(0, hidden, chunk):
        to = slice(start, start + chunk)
        a, s = gelu_parts(dot(mid_low[...], weight[to, :], 1, 1))
        act[:, to] = a
        slope[:, to] = s.astype(BF)
    waits.append(start_copies([(slope, slope_out)], out_sems[2]))
    n, factor = row_norm(act[...])
    for number, post in enumerate(posts):
        post[...] = n[:, number * hidden // 2 : (number + 1) * hidden // 2].astype(BF)
    factors[...] = jnp.broadcast_to(factor, (rows, 128))
    for wait in waits:
        wait()


def expand_ffn(flags, att, w_out, tokens, gain_ffn, expand, places):
    rows, width = att[0].shape[1], tokens.shape[1]
    hidden = sum(e.shape[0] for e in expand)
    n_own = len(att)
    local = att[0].shape[0]
    return pl.pallas_call(
        partial(expand_kernel, n_own, len(expand), places),
        out_shape=(
            jax.ShapeDtypeStruct((rows, hidden // 2), BF),
            jax.ShapeDtypeStruct((rows, hidden // 2), BF),
            jax.ShapeDtypeStruct((rows, 128), F32),
            jax.ShapeDtypeStruct((rows, hidden), BF),
            jax.ShapeDtypeStruct((rows, width), F32),
            jax.ShapeDtypeStruct((rows, width), BF),
            jax.ShapeDtypeStruct((n_own * local, rows), BF),
        ),
        in_specs=[smem()]
        + [vmem()] * (2 * n_own)
        + [anywhere(), vmem()]
        + [anywhere()] * len(expand),
        out_specs=[vmem()] * 3 + [anywhere()] * 4,
        scratch_shapes=[
            pltpu.VMEM((hidden, width), BF),
            pltpu.VMEM((rows, hidden), F32),
            pltpu.VMEM((rows, width), BF),
            pltpu.VMEM((rows, hidden), BF),
            pltpu.VMEM((rows, width), F32),
            pltpu.VMEM((rows, width), BF),
            pltpu.VMEM((n_own * local, rows), BF),
            pltpu.SemaphoreType.DMA((len(places),)),
            pltpu.SemaphoreType.DMA,
            pltpu.SemaphoreType.DMA((1,)),
            pltpu.SemaphoreType.DMA((2,)),
            pltpu.SemaphoreType.DMA((1,)),
        ],
        compiler_params=params(),
        cost_estimate=cost(12000000000, 36000000),
        name="expand_ffn",
    )(flags, *att, *w_out, tokens, gain_ffn, *expand)


def reduce_kernel(n_piece, places, *refs):
    posts, (slope, factors, middle, cotangent), rest = refs[:2], refs[2:6], refs[6:]
    pieces, (output, *grads, weight, d_post, sems) = rest[:n_piece], rest[n_piece:]
    hidden, width = weight.shape
    half = hidden // 2
    fetch(pieces, places, weight, sems)()
    total = middle[...]
    for start in range(0, hidden, width):
        at = slice(start % half, start % half + width)
        rows = slice(start, start + width)
        d_post[:, rows] = dot(cotangent[...], weight[rows, :], 1, 1)
        total = total + dot(posts[start // half][:, at], weight[rows, :], 1, 0)
    output[...] = total.astype(BF)
    mean_e, mean_en = 0.0, 0.0
    for number, post in enumerate(posts):
        e = d_post[:, number * half : (number + 1) * half]
        mean_e = mean_e + jnp.sum(e, axis=1, keepdims=True) / hidden
        mean_en = mean_en + jnp.sum(e * post[...].astype(F32), axis=1, keepdims=True) / hidden
    for number, (post, grad) in enumerate(zip(posts, grads)):
        at = slice(number * half, (number + 1) * half)
        back = d_post[:, at] - mean_e - post[...].astype(F32) * mean_en
        grad[...] = (factors[:, 0:1] * back * slope[:, at].astype(F32)).astype(BF)


def reduce_ffn(posts, slope, factors, middle, cotangent, reduced, places):
    rows, width = middle.shape
    hidden = slope.shape[1]
    return pl.pallas_call(
        partial(reduce_kernel, len(reduced), places),
        out_shape=(
            jax.ShapeDtypeStruct((rows, width), BF),
            jax.ShapeDtypeStruct((rows, hidden // 2), BF),
            jax.ShapeDtypeStruct((rows, hidden // 2), BF),
        ),
        in_specs=[vmem()] * 6 + [anywhere()] * len(reduced),
        out_specs=[vmem()] * 3,
        scratch_shapes=[
            pltpu.VMEM((hidden, width), BF),
            pltpu.VMEM((rows, hidden), F32),
            pltpu.SemaphoreType.DMA((len(places),)),
        ],
        compiler_params=params(),
        cost_estimate=cost(15_000_000_000, 45_000_000),
        name="reduce_ffn",
    )(*posts, slope, factors, middle, cotangent, *reduced)


def middle_kernel(n_own, n_piece, places, *refs):
    att, w_far = refs[:n_own], refs[n_own : 2 * n_own]
    *hidden_grads, middle, cotangent, inner_far, gain_ffn = refs[2 * n_own : 2 * n_own + 6]
    rest = refs[2 * n_own + 6 :]
    pieces, rest = rest[:n_piece], rest[n_piece:]
    ffn_sum, sent, kept_first, kept_second, *grads = rest[: 4 + n_own]
    middle_out, weight, branch_grad, e_buf, w_out, inner_t, middle_grad = rest[4 + n_own : 11 + n_own]
    sems, far_sems, out_sem = rest[11 + n_own :]
    rows, width = middle.shape
    local = att[0].shape[0]
    half = weight.shape[0] // 2
    gain_row = gain_ffn[...].astype(F32).reshape(1, -1)
    wait = fetch(pieces, places, weight, sems)
    targets = [w_out.at[place] for place in range(n_own)] + [inner_t]
    wait_far = start_copies(zip((*w_far, inner_far), targets), far_sems)
    n, factor = row_norm(middle[...])
    average, inner_factor = inner_stats(att, width)
    wait()
    grad = dot(hidden_grads[0][...], weight[0:half, :], 1, 0)
    grad = grad + dot(hidden_grads[1][...], weight[half:, :], 1, 0)
    ffn_sum[...] = jnp.sum((grad * n).reshape(rows // 8, 8, width), axis=0)
    e = grad * gain_row
    back = factor * (
        e - jnp.mean(e, axis=1, keepdims=True) - n * jnp.mean(e * n, axis=1, keepdims=True)
    )
    full = cotangent[...].astype(F32) + back
    middle_grad[...] = full
    wait_out = start_copies([(middle_grad, middle_out)], out_sem)
    branch_grad[...] = full.astype(BF)

    wait_far()
    grad_sum = jnp.zeros((1, rows), F32)
    cross_sum = jnp.zeros((1, rows), F32)
    for place in range(n_own):
        e = dot(w_out[place], branch_grad[...], 1, 1)
        e_buf[place] = e
        grad_sum = grad_sum + jnp.sum(e, axis=0, keepdims=True)
        hat = (att[place][...].astype(F32) - average) * inner_factor
        cross_sum = cross_sum + jnp.sum(e * hat, axis=0, keepdims=True)
    for place in range(n_own):
        hat = (att[place][...].astype(F32) - average) * inner_factor
        grad = inner_factor * (e_buf[place] - grad_sum / width - hat * (cross_sum / width))
        grads[place][...] = grad.astype(BF)
        product = dot(inner_t[place * local : (place + 1) * local, :], branch_grad[...], 1, 0)
        if place % 2:
            sent[place // 2] = product.astype(BF)
        else:
            (kept_second if place else kept_first)[...] = product.astype(BF)
    wait_out()


def middle_back(att, w_out, hidden_grads, middle, cotangent, inner_t, gain_ffn, expand, places):
    rows, width = middle.shape
    hidden = 2 * hidden_grads[0].shape[1]
    n_own = len(att)
    local = att[0].shape[0]
    return pl.pallas_call(
        partial(middle_kernel, n_own, len(expand), places),
        out_shape=(
            jax.ShapeDtypeStruct((8, width), F32),
            jax.ShapeDtypeStruct((n_own // 2, local, width), BF),
            jax.ShapeDtypeStruct((local, width), BF),
            jax.ShapeDtypeStruct((local, width), BF),
        )
        + (jax.ShapeDtypeStruct((local, rows), BF),) * n_own
        + (jax.ShapeDtypeStruct((rows, width), F32),),
        in_specs=[vmem()] * n_own
        + [anywhere()] * n_own
        + [vmem()] * 4
        + [anywhere(), vmem()]
        + [anywhere()] * len(expand),
        out_specs=[vmem()] * (4 + n_own) + [anywhere()],
        scratch_shapes=[
            pltpu.VMEM((hidden, width), BF),
            pltpu.VMEM((rows, width), BF),
            pltpu.VMEM((n_own, local, rows), F32),
            pltpu.VMEM((n_own, local, width), BF),
            pltpu.VMEM((n_own * local, rows), BF),
            pltpu.VMEM((rows, width), F32),
            pltpu.SemaphoreType.DMA((len(places),)),
            pltpu.SemaphoreType.DMA((n_own + 1,)),
            pltpu.SemaphoreType.DMA((1,)),
        ],
        compiler_params=params(),
        cost_estimate=cost(12_500_000_000, 37_500_000),
        name="middle_back",
    )(*att, *w_out, *hidden_grads, middle, cotangent, inner_t, gain_ffn, *expand)


def input_gradient_kernel(
    flags, kept, came, first, second, tokens, gain, middle_grad, out, own, sem
):
    rows = out.shape[0]
    start = pl.multiple_of(flags[1] * rows, rows)
    copy = pltpu.make_async_copy(tokens.at[pl.ds(start, rows), :], own, sem)
    copy.start()
    last = jnp.concatenate([first[...], second[...]], axis=0)
    total = kept[0].astype(F32) + came[0].astype(F32) + last.astype(F32)
    e = total.T * gain[...].astype(F32).reshape(1, -1)
    copy.wait()
    n, factor = row_norm(own[...].astype(F32))
    back = factor * (
        e - jnp.mean(e, axis=1, keepdims=True) - n * jnp.mean(e * n, axis=1, keepdims=True)
    )
    out[...] = (middle_grad[...] + back).astype(BF)


def input_gradient(flags, terms, tokens, gain, middle_grad):
    kept, came, first, second = terms
    block = pl.BlockSpec((1,) + kept.shape[1:], lambda i: (0, 0, 0))

    def whole(v):
        return pl.BlockSpec(v.shape, lambda i: (0,) * v.ndim)

    return pl.pallas_call(
        input_gradient_kernel,
        grid=(1,),
        out_shape=jax.ShapeDtypeStruct(middle_grad.shape, BF),
        in_specs=[smem(), block, block, whole(first), whole(second), anywhere()]
        + [whole(gain), whole(middle_grad)],
        out_specs=whole(middle_grad),
        scratch_shapes=[pltpu.VMEM(middle_grad.shape, BF), pltpu.SemaphoreType.DMA],
        compiler_params=params(),
        cost_estimate=cost(4500000000, 13500000),
        name="input_gradient",
    )(flags, *terms, tokens, gain, middle_grad)


def body(
    tokens,
    w_query,
    w_key,
    w_value,
    w_output,
    gain_attn,
    gain_inner,
    gain_ffn,
    w_expand,
    w_reduce,
    gain_hidden,
    cotangent,
    seq_length,
    seq_group,
):
    n_batch, n_own = lax.axis_size("batch"), lax.axis_size("heads")
    n_all = n_batch * n_own
    mine = lax.axis_index("heads")
    quarter = cotangent.shape[0]
    width = tokens.shape[1]
    local = w_query.shape[1]
    n_heads = local // HD

    def swap(value, bit):
        return lax.ppermute(value, AXES, [(i, i ^ bit) for i in range(n_all)])

    flags = jnp.stack([lax.axis_index("batch"), mine]).astype(jnp.int32)
    table = (seq_length, seq_group)
    far = [1 << b for b in range(3, n_all.bit_length() - 1)]
    near = (2, 4, 6)

    def parts(value, offsets):
        return [value] + [swap(value, off) for off in offsets]

    def around(value, offsets):
        return jnp.concatenate(parts(value, offsets), axis=0)

    def far_steps(value):
        for bit in reversed(far):
            value = around(value, (bit,))
            yield value

    def add(values):
        return sum(v.astype(F32) for v in values)

    phase = lax.optimization_barrier

    def sum_begin(value):
        rows = value.shape[0]
        value = lax.all_to_all(value, "batch", 0, 0, tiled=True)
        return value.reshape(n_batch, rows // n_batch, width)

    def sum_middle(value):
        return jnp.sum(value.astype(F32), axis=0)

    def sum_end(share):
        share = jnp.broadcast_to(share.astype(BF)[None], (n_batch,) + share.shape)
        return lax.all_to_all(share, "batch", 0, 0, tiled=True)

    def last(steps):
        *_, value = steps
        return value

    w_t = jnp.concatenate([w_query.T, w_key.T, w_value.T], axis=0)
    w_reduce_scaled = (w_reduce.astype(F32) * gain_hidden.astype(F32)[:, None]).astype(BF)
    w_output_scaled = (w_output.astype(F32) * gain_inner.astype(F32)[:, None]).astype(BF)

    if len(far) == 2:
        expand_far = parts(w_expand, (far[1], far[0], far[0] | far[1]))
    else:
        expand_far = [last(far_steps(w_expand))]
    reduced = w_reduce_scaled
    for bit in far[:0:-1]:
        reduced = parts(jnp.concatenate(reduced) if isinstance(reduced, list) else reduced, (bit,))
    w_out_y = swap(w_output_scaled, 2)
    pre, qkv = project(tokens, w_t, gain_attn, [])
    expand_far, reduced, w_out_y, pre, qkv = phase((expand_far, reduced, w_out_y, pre, qkv))

    expand = parts(jnp.concatenate(expand_far), near)
    reduced = parts(jnp.concatenate(reduced), (far[0],))
    w_out_c = swap(jnp.stack([w_output_scaled, w_out_y]), 1)
    lse, *pieces = attend(flags, table, qkv, n_own, [])
    reduced, w_out_c, lse, pieces = phase((reduced, w_out_c, lse, pieces))

    att = [pieces[0]] + [swap(pieces[k], k) for k in range(1, n_own)]
    expand, att = phase((expand, att))
    expand = jnp.concatenate(expand)
    expand = [expand, swap(expand, 1)]
    reduced = jnp.concatenate(reduced)
    half = reduced.shape[0] // 2
    first = [swap(reduced[:half], 4), swap(reduced[half:], 2)]
    w_out = [w_output_scaled, w_out_c[0], w_out_y, w_out_c[1]]
    att, expand, reduced, first, w_out, cotangent = phase(
        (att, expand, reduced, first, w_out, cotangent)
    )
    cot_came = swap(cotangent, 1)

    def stacked(parts):
        starts = [sum(p.shape[0] for p in parts[:i]) for i in range(len(parts))]
        return [(i, 0, start, p.shape[0]) for i, (start, p) in enumerate(zip(starts, parts))]

    places = stacked(expand)
    second = [
        swap(jnp.concatenate([reduced[:half], first[0]]), 2),
        swap(jnp.concatenate([reduced[half:], first[1]]), 4),
    ]
    *posts, factors, slope, middle, mid_low, inner_t = expand_ffn(
        flags, att, w_out, tokens, gain_ffn, expand, places
    )
    reduced, posts, slope, factors, middle, mid_low, inner_t, cot_came = phase(
        ([reduced, *first, *second], posts, slope, factors, middle, mid_low, inner_t, cot_came)
    )

    starts = [(0, 0, 0), (0, half, 1), (1, 0, 4), (2, 0, 3)]
    starts += [(3, 0, 2), (3, half, 6), (4, 0, 5), (4, half, 7)]
    reduce_places = [
        (number + core * 5, start, core * 8 * half + at * half, half)
        for core in range(2)
        for number, start, at in starts
    ]
    post_came = swap(posts[1], 1)
    reduced = reduced + [swap(r, 1) for r in reduced]
    d_reduce = outer(posts[0], post_came, cotangent, cot_came)
    reduced, posts, mid_low, d_reduce = phase((reduced, posts, mid_low, d_reduce))

    def near_begin(products):
        return swap(products[0], 2), swap(products[1], 4)

    def near_middle(products, came):
        half = came[0].shape[0] // 2
        terms = [add((p, c[half:])).astype(BF) for p, c in zip(products[3:], came)]
        return came, (swap(terms[0], 4), swap(terms[1], 2))

    def near_end(products, begun, came):
        half = came[0].shape[0]
        return [
            add((products[2][i * half : (i + 1) * half], b[:half], c))
            for i, (b, c) in enumerate(zip(begun, came))
        ]

    begun_r = near_begin(d_reduce)
    mid_came = swap(mid_low, 1)
    output, *hidden_grads = reduce_ffn(
        posts, slope, factors, middle, cotangent, reduced, reduce_places
    )
    output, hidden_grads, begun_r, d_reduce, mid_came = phase(
        (output, hidden_grads, begun_r, d_reduce, mid_came)
    )

    begun_r, came_r = near_middle(d_reduce, begun_r)
    grad_came = swap(hidden_grads[1], 1)
    ffn_sum, d_sent, kept_first, kept_second, *att_grads, middle_grad = middle_back(
        att, w_out, hidden_grads, middle, cotangent, inner_t, gain_ffn, expand, places
    )
    d_kept = [kept_first, kept_second]
    came_r, grad_came, middle_grad, ffn_sum, d_sent, d_kept, att_grads = phase(
        (came_r, grad_came, middle_grad, ffn_sum, d_sent, d_kept, att_grads)
    )

    def far_sum(value, bit):
        return value[0], swap(value[1].astype(BF), bit)

    def halves(value):
        return value.reshape(2, -1, width)

    grads = [att_grads[0]] + [swap(att_grads[k], k) for k in range(1, n_own)]
    d_came = swap(d_sent, 1)
    d_came, mid_came, begun_r, came_r = phase((d_came, mid_came, begun_r, came_r))
    d_reduce = far_sum(near_end(d_reduce, begun_r, came_r), far[0])
    d_expand = outer(hidden_grads[0], grad_came, mid_low, mid_came)
    d_reduce, grads, d_expand, d_came = phase((d_reduce, grads, d_expand, d_came))

    back = partial(attend_back, flags, table, qkv)

    begun_e = near_begin(d_expand)
    for bit in far[1:]:
        d_reduce = far_sum(halves(add(d_reduce)), bit)
    d_last = swap(add((d_kept[1], d_came[1])).astype(BF), 2)
    back_0 = back(0, lse, pre, w_t, pieces, grads)
    back_0, d_reduce, begun_e, d_expand, d_last, grads = phase(
        (back_0, d_reduce, begun_e, d_expand, d_last, grads)
    )

    d_own = add((d_kept[0], d_came[0], d_last)).astype(BF)
    share_0 = sum_begin(jnp.concatenate([back_0[1], d_own]))
    begun_e, came_e = near_middle(d_expand, begun_e)
    back_1 = back(1, lse, pre, w_t, pieces, grads)
    back_1, came_e, share_0, grads = phase((back_1, came_e, share_0, grads))

    batch_bits = [1 << b for b in range(n_batch.bit_length() - 1)][::-1]

    def gather_step(value, bit):
        return value, swap(value, bit * n_own)

    def joined(pair, bit):
        axis = batch_bits.index(bit)
        mine_first = (lax.axis_index("batch") & bit) == 0
        return jnp.where(
            mine_first, jnp.concatenate(pair, axis), jnp.concatenate(pair[::-1], axis)
        )

    d_expand = near_end(d_expand, begun_e, came_e)
    if len(far) == 2:
        blocks = [v.astype(BF) for part in d_expand for v in halves(part)]
        offs = (far[1], far[0], far[0] | far[1])
        d_expand = [halves(d_expand[0])[0]] + [swap(b, o) for b, o in zip(blocks[1:], offs)]
    else:
        d_expand = far_sum(d_expand, far[0])
        for bit in far[1:]:
            d_expand = far_sum(halves(add(d_expand)), bit)
    share_0 = sum_middle(share_0).astype(BF)
    share_0 = gather_step(share_0.reshape((1,) * len(batch_bits) + share_0.shape), batch_bits[0])
    earlier = (back_0[0], back_1[0])
    back_2 = back(2, lse, pre, w_t, pieces, grads, d_before=back_1[1], earlier=earlier)
    back_2, d_expand, share_0 = phase((back_2, d_expand, share_0))

    share_1 = sum_begin(back_2[1])
    small = jnp.sum(jnp.stack([back_0[2] + back_1[2] + back_2[2], ffn_sum]), axis=1)
    small = small + swap(small, 1)
    small = small + swap(small, 2)
    sent, kept = back_2[3:]
    came = swap(sent, 1)
    came, kept, small = phase((came, kept, small))
    split = width // 2
    terms = [
        add((kept[1, at], came[1, at])).astype(BF)
        for at in (slice(0, split), slice(split, width))
    ]
    first = swap(terms[0], 2)
    for bit, later in zip(batch_bits[:-1], batch_bits[1:-1]):
        share_0 = gather_step(joined(share_0, bit), later)
    share_1, share_0, first, terms, d_expand = phase((share_1, share_0, first, terms, d_expand))

    second = [first, swap(terms[1], 2)]
    share_1 = sum_middle(share_1)
    count = share_1.shape[0]
    total_1 = sum_end(jnp.concatenate([share_1, small], axis=0))
    share_0 = gather_step(joined(share_0, batch_bits[-2]), batch_bits[-1])
    grad_tokens = input_gradient(
        flags, (kept, came, *second), tokens, gain_attn, middle_grad
    )
    grad_tokens, share_0, d_reduce, d_expand = phase((grad_tokens, share_0, d_reduce, d_expand))
    d_expand = add(d_expand)
    d_reduce = add(d_reduce)
    g_hidden = jnp.sum(d_reduce * w_reduce.astype(F32), axis=1)
    d_reduce = d_reduce * gain_hidden.astype(F32)[:, None]

    total_0 = joined(share_0, batch_bits[-1]).astype(F32).reshape(-1, width)
    total_1 = total_1.astype(F32)
    small = jnp.sum(total_1[:, count:], axis=0)
    total_1 = total_1[:, :count].reshape(-1, width)
    totals = [total_0, total_1[: 3 * HD], total_1[3 * HD :]]
    def weight_grad(place):
        at = slice(place * HD, (place + 1) * HD)
        return jnp.concatenate([t[at] for t in totals], axis=0).T

    g_out = totals[0][3 * HD :]
    return (
        output,
        grad_tokens,
        weight_grad(0),
        weight_grad(1),
        weight_grad(2),
        g_out * gain_inner.astype(F32)[:, None],
        small[0] / gain_attn.astype(F32),
        jnp.sum(g_out * w_output.astype(F32), axis=1),
        small[1],
        d_expand,
        d_reduce,
        g_hidden,
    )


def solution(mesh):
    both = P(AXES, None)
    return jax.shard_map(
        body,
        mesh=mesh,
        in_specs=(
            P("batch", None),
            P(None, "heads"),
            P(None, "heads"),
            P(None, "heads"),
            P("heads", None),
            P(),
            P("heads"),
            P(),
            both,
            both,
            P(AXES),
            both,
            P(),
            P(),
        ),
        out_specs=(
            both,
            both,
            P(None, "heads"),
            P(None, "heads"),
            P(None, "heads"),
            P("heads", None),
            P(),
            P("heads"),
            P(),
            both,
            both,
            P(AXES),
        ),
        check_vma=False,
    )
```
